128 devices in a mesh: pipe: 2 (over y_hi), dp: 16 (over z, y_lo, core), tensor: 4 (over x).
Axes of the slice: x: 4, y: 4 (y_hi: 2, y_lo: 2; y = y_hi * 2 + y_lo), z: 4, core: 2. Of those that a mesh axis runs over, the one named last changes fastest.
Arguments:
- boundary: float32 [2, 4, 4096, 768], P('pipe', None, 'dp'), may hold values from -6 to 6
- segment_ids: int32 [4, 4, 1024], replicated, may hold values from 0 to 4, as said below
- attn_gain: float32 [2, 768], P('pipe'), may hold values from 0.1 to 1.9
- attn_shift: float32 [2, 768], P('pipe'), may hold values from -1.5 to 1.5
- mlp_gain: float32 [2, 768], P('pipe'), may hold values from 0.1 to 1.9
- mlp_shift: float32 [2, 768], P('pipe'), may hold values from -1.5 to 1.5
- qkv_weight: bfloat16 [2, 768, 2304], P('pipe', None, 'tensor'), may hold values from -0.21875 to 0.21875
- qkv_bias: float32 [2, 2304], P('pipe', 'tensor'), may hold values from -2.5 to 2.5
- dense_weight: bfloat16 [2, 768, 768], P('pipe', 'tensor'), may hold values from -1.75 to 1.75
- dense_bias: float32 [2, 768], P('pipe'), may hold values from -2.5 to 2.5
- up_weight: bfloat16 [2, 768, 3072], P('pipe', None, 'tensor'), may hold values from -0.21875 to 0.21875
- up_bias: float32 [2, 3072], P('pipe', 'tensor'), may hold values from -2.5 to 2.5
- down_weight: bfloat16 [2, 3072, 768], P('pipe', 'tensor'), may hold values from -0.109375 to 0.109375
- down_bias: float32 [2, 768], P('pipe'), may hold values from -2.5 to 2.5
Outputs:
- boundary_out: float32 [2, 4, 4096, 768], P('pipe', None, 'dp')
- attn_gain_grad: float32 [2, 768], P('pipe')
- attn_shift_grad: float32 [2, 768], P('pipe')
- mlp_gain_grad: float32 [2, 768], P('pipe')
- mlp_shift_grad: float32 [2, 768], P('pipe')
- qkv_weight_grad: float32 [2, 768, 2304], P('pipe', None, 'tensor')
- qkv_bias_grad: float32 [2, 2304], P('pipe', 'tensor')
- dense_weight_grad: float32 [2, 768, 768], P('pipe', 'tensor')
- dense_bias_grad: float32 [2, 768], P('pipe')
- up_weight_grad: float32 [2, 768, 3072], P('pipe', None, 'tensor')
- up_bias_grad: float32 [2, 3072], P('pipe', 'tensor')
- down_weight_grad: float32 [2, 3072, 768], P('pipe', 'tensor')
- down_bias_grad: float32 [2, 768], P('pipe')
The draws below stay inside these ranges and needn't reach their ends.
Inputs may be any that keep to these rules, and one draw needn't show every extreme that they name: `segment_ids`: within each sequence the numbers start at 0, never fall and rise by at most one from token to token; each document but the last of a sequence has at least 204 tokens; in every draw one whole sequence is a single document.
All inputs are finite; a program needn't handle non-finite values.
Results may differ from the reference program's by a relative error of at most 0.028.
Values may be sent and summed in bfloat16 or wider, within the bound.
A program may use at most 192 MiB of HBM per device.

```python
import jax
import jax.numpy as jnp
from jax import lax

D = 768
HEADS = 12
HEAD_DIM = 64
FF = 3072
ROT = 16
SEQ_LEN = 1024
SEQS = 4
MICRO = 4
LAYERS = 2


def draw_segment_ids(key, part):
    number = MICRO * SEQS
    spans = jax.random.randint(jax.random.fold_in(key, 11), (number, 8), SEQ_LEN // 5, 2 * SEQ_LEN)
    ends = jnp.cumsum(spans, axis=1)
    spots = jnp.arange(SEQ_LEN, dtype=jnp.int32)
    labels = jnp.sum((spots[None, :, None] >= ends[:, None, :]).astype(jnp.int32), axis=2)
    labels = jnp.minimum(labels, 4)
    single = jax.random.randint(jax.random.fold_in(key, 12), (), 0, number)
    offset = jax.random.randint(jax.random.fold_in(key, 13), (), 0, number - 1)
    crowded = (single + 1 + offset) % number
    even = jnp.minimum(spots // (SEQ_LEN // 5), 4)
    rows = jnp.arange(number)
    labels = jnp.where((rows == crowded)[:, None], even[None, :], labels)
    labels = jnp.where((rows == single)[:, None], 0, labels)
    return labels.astype(jnp.int32).reshape(MICRO, SEQS, SEQ_LEN)


def shard_levels(stream_key, extent, pieces, smallest, top_value):
    factor_of, own = 1.0, jax.random.fold_in(stream_key, 6)
    for axis_at, blocks in pieces:
        draws = jnp.exp(jax.random.uniform(jax.random.fold_in(own, axis_at), (blocks,), jnp.float32, smallest / len(pieces), top_value / len(pieces)))
        factor_of = factor_of * jnp.repeat(draws, extent[axis_at] // blocks).reshape([-1 if axis == axis_at else 1 for axis in range(len(extent))])
    return factor_of


def scatter_about(rng, extent, deviation, most, cuts=(), kind=jnp.bfloat16):
    array = jax.random.normal(rng, extent, jnp.float32) * deviation
    if len(cuts) > 0:
        array = shard_levels(rng, extent, cuts, -0.22, 0.18) * array
    return jnp.clip(array, min=-most, max=most).astype(kind)


def setup_inputs(seed: int = 0) -> dict:
    seeds = jax.random.split(jax.random.key(seed), 15)
    return {
        "boundary": scatter_about(seeds[0], (2, MICRO, SEQS * SEQ_LEN, D), 1.0, 6.0, ((0, 2), (2, 16)), jnp.float32),
        "segment_ids": draw_segment_ids(jax.random.fold_in(seeds[14], 71), 0),
        "attn_gain": jnp.clip(1.0 + 0.18 * jax.random.normal(seeds[2], (LAYERS, D), jnp.float32), 0.1, 1.9),
        "attn_shift": scatter_about(seeds[3], (LAYERS, D), 0.3, 1.5, ((0, 2),), jnp.float32),
        "mlp_gain": jnp.clip(1.0 + 0.18 * jax.random.normal(seeds[4], (LAYERS, D), jnp.float32), 0.1, 1.9),
        "mlp_shift": scatter_about(seeds[5], (LAYERS, D), 0.3, 1.5, ((0, 2),), jnp.float32),
        "qkv_weight": scatter_about(seeds[6], (LAYERS, D, 3 * D), D ** -0.5, 0.21875, ((0, 2), (2, 4))),
        "qkv_bias": scatter_about(seeds[7], (LAYERS, 3 * D), 0.5, 2.5, ((0, 2), (1, 4)), jnp.float32),
        "dense_weight": scatter_about(seeds[8], (LAYERS, D, D), (D * 16 // SEQ_LEN) ** -0.5, 1.75, ((0, 2), (1, 4))),
        "dense_bias": scatter_about(seeds[9], (LAYERS, D), 0.5, 2.5, ((0, 2),), jnp.float32),
        "up_weight": scatter_about(seeds[10], (LAYERS, D, FF), D ** -0.5, 0.21875, ((0, 2), (2, 4))),
        "up_bias": scatter_about(seeds[11], (LAYERS, FF), 0.5, 2.5, ((0, 2), (1, 4)), jnp.float32),
        "down_weight": scatter_about(seeds[12], (LAYERS, FF, D), FF ** -0.5, 0.109375, ((0, 2), (1, 4))),
        "down_bias": scatter_about(seeds[13], (LAYERS, D), 0.5, 2.5, ((0, 2),), jnp.float32),
    }


EPS = 1e-05
MASKED = -1e+30
HIGH = lax.Precision.HIGHEST

@jax.custom_vjp
def low(v):
    return lax.optimization_barrier(v.astype(jnp.bfloat16)).astype(jnp.float32)

@jax.custom_vjp
def low_back(v):
    return v

def low_keep(v):
    return (low(v), None)

def low_pass(kept, grad):
    return (grad,)

def back_keep(v):
    return (v, None)

def back_low(kept, grad):
    return (low(grad),)
low.defvjp(low_keep, low_pass)
low_back.defvjp(back_keep, back_low)

def layer_norm(flat, gain, shift):
    middle = lax.optimization_barrier(jnp.mean(flat, axis=-1, keepdims=True))
    centred = flat - middle
    spread = lax.optimization_barrier(jnp.mean(centred * centred, axis=-1, keepdims=True))
    return centred * lax.rsqrt(spread + EPS) * gain + shift

def rotary_tables(places, rot_dims):
    half = rot_dims // 2
    freqs = 10000.0 ** (-(2.0 * jnp.arange(half, dtype=jnp.float32)) / rot_dims)
    angles = places.astype(jnp.float32)[..., None] * freqs
    angles = jnp.concatenate([angles, angles], axis=-1)
    return (jnp.cos(angles), jnp.sin(angles))

def rotate(vector, cosine, sine, rot_dims):
    portion = vector[..., :rot_dims]
    half = rot_dims // 2
    turned = jnp.concatenate([-portion[..., half:], portion[..., :half]], axis=-1)
    return jnp.concatenate([portion * cosine + turned * sine, vector[..., rot_dims:]], axis=-1)

def attend(pair):
    packed, labels = pair
    spots = jnp.arange(SEQ_LEN, dtype=jnp.int32)
    before = lax.optimization_barrier(jnp.sum((labels[None, :] < labels[:, None]).astype(jnp.int32), axis=1))
    cosine, sine = rotary_tables(spots - before, ROT)
    cosine = cosine[:, None, :]
    sine = sine[:, None, :]
    query = low(rotate(packed[:, :, 0], cosine, sine, ROT))
    keys = low(rotate(packed[:, :, 1], cosine, sine, ROT))
    values = low(packed[:, :, 2])
    score = jnp.einsum('qhd,khd->hqk', query, keys, precision=HIGH) * HEAD_DIM ** (-0.5)
    score = low_back(score)
    allowed = (labels[None, :] == labels[:, None]) & (spots[None, :] <= spots[:, None])
    score = jnp.where(allowed[None], score, MASKED)
    top = lax.optimization_barrier(jnp.max(score, axis=-1, keepdims=True))
    expo = jnp.exp(score - top)
    prob = low(expo / lax.optimization_barrier(jnp.sum(expo, axis=-1, keepdims=True)))
    mixed = jnp.einsum('hqk,khd->qhd', prob, values, precision=HIGH)
    return mixed.reshape(SEQ_LEN, HEADS * HEAD_DIM)

def block(stream, labels, weights):
    attn_gain, attn_shift, mlp_gain, mlp_shift, qkv_weight, qkv_bias, dense_weight, dense_bias, up_weight, up_bias, down_weight, down_bias = weights
    flat = stream.reshape(-1, D)
    first = low(layer_norm(flat, attn_gain, attn_shift))
    second = low(layer_norm(flat, mlp_gain, mlp_shift))
    packed = low_back(jnp.dot(first, qkv_weight, precision=HIGH) + qkv_bias)
    packed = packed.reshape(-1, SEQ_LEN, HEADS, 3, HEAD_DIM)
    mixed = lax.map(jax.checkpoint(attend), (packed, labels))
    mixed = low(low_back(mixed.reshape(-1, D)))
    hidden = low_back(jnp.dot(second, up_weight, precision=HIGH) + up_bias)
    active = low(jax.nn.gelu(hidden, approximate=False))
    branch = jnp.dot(mixed, dense_weight, precision=HIGH) + jnp.dot(active, down_weight, precision=HIGH)
    branch = branch + dense_bias + down_bias
    return (flat + low_back(branch)).reshape(stream.shape)

def reference(boundary, segment_ids, attn_gain, attn_shift, mlp_gain, mlp_shift, qkv_weight, qkv_bias, dense_weight, dense_bias, up_weight, up_bias, down_weight, down_bias):
    number = MICRO * SEQS
    start_in = boundary[0].reshape(number, SEQ_LEN, D)
    cotangent = boundary[1].reshape(number, SEQ_LEN, D)
    labels = segment_ids.reshape(number, SEQ_LEN)
    params = tuple((weight.astype(jnp.float32) for weight in (attn_gain, attn_shift, mlp_gain, mlp_shift, qkv_weight, qkv_bias, dense_weight, dense_bias, up_weight, up_bias, down_weight, down_bias)))

    def forward(stream, params):
        for layer_id in range(LAYERS):
            stream = block(stream, labels, tuple((weight[layer_id] for weight in params)))
        return stream
    result, pullback = jax.vjp(forward, start_in, params)
    grad_in, grads = pullback(cotangent)
    edges = jnp.stack([grad_in, result]).reshape(2, MICRO, SEQS * SEQ_LEN, D)
    return (edges, grads[0], grads[1], grads[2], grads[3], grads[4], grads[5], grads[6], grads[7], grads[8], grads[9], grads[10], grads[11])
```

```python
import functools

import jax
import jax.numpy as jnp
from jax import lax
from jax.experimental import pallas as pl
from jax.experimental.pallas import tpu as pltpu
from jax.sharding import PartitionSpec as P

MESH = pl.DeviceIdType.MESH
HEAD_DIM = 64
ROT = 16
EPS = 1e-05
MASKED = -1e30
WIDTH = 768
SEQ = 1024
BLOCK = 256
HEADS = 3
INNER = HEADS * HEAD_DIM
GRAD_ROWS = 2304
bf16 = jnp.bfloat16
f32 = jnp.float32
VMEM_LIMIT = 56 * 1024 * 1024


class Place:
    def __init__(self):
        self.p = lax.axis_index("pipe")
        self.d = lax.axis_index("dp")
        self.x = lax.axis_index("tensor")
        self.z = self.d // 4
        self.low = (self.d // 2) % 2
        self.c = self.d % 2
        self.y = 2 * self.p + self.low

    def at_x(self, steps):
        return (self.p, self.d, (self.x + steps) % 4)

    def at_y(self, steps):
        y = (self.y + steps) % 4
        return (y // 2, self.z * 4 + (y % 2) * 2 + self.c, self.x)

    def at_z(self, steps):
        return (self.p, ((self.z + steps) % 4) * 4 + self.d % 4, self.x)

    def sibling(self):
        return (self.p, self.d + 1 - 2 * self.c, self.x)

    def partner(self):
        return (1 - self.p, self.z * 4 + (1 - self.low) * 2 + self.c, self.x)

    def beside(self):
        return (self.p, self.z * 4 + (1 - self.low) * 2 + self.c, self.x)


def greet(devices):
    barrier = pltpu.get_barrier_semaphore()
    for device in devices:
        pl.semaphore_signal(barrier, inc=1, device_id=device, device_id_type=MESH)
    pl.semaphore_wait(barrier, len(devices))


class Copies:
    def __init__(self, send_sems, recv_sems, somebody):
        self.send_sems, self.recv_sems = send_sems, recv_sems
        self.somebody = somebody
        self.count = 0
        self.started = []

    def send(self, src, dst, device):
        k = self.count
        self.count += 1
        copy = pltpu.make_async_remote_copy(
            src_ref=src,
            dst_ref=dst,
            send_sem=self.send_sems.at[k],
            recv_sem=self.recv_sems.at[k],
            device_id=device,
            device_id_type=MESH,
        )
        copy.start()
        self.started.append(copy)
        return k

    def landed(self, k, dst):
        pltpu.make_async_remote_copy(
            src_ref=dst,
            dst_ref=dst,
            send_sem=self.send_sems.at[k],
            recv_sem=self.recv_sems.at[k],
            device_id=self.somebody,
            device_id_type=MESH,
        ).wait_recv()

    def drain(self):
        for copy in self.started:
            copy.wait_send()


class RingSum:
    def __init__(self, copies, me, right, left, chunk, relay, direct, final):
        self.copies, self.me, self.right, self.left = copies, me, right, left
        self.chunk, self.relay_in, self.direct, self.final = chunk, relay, direct, final

    def start(self):
        me, send = self.me, self.copies.send
        far, after, before = (me + 2) % 4, (me + 1) % 4, (me + 3) % 4
        self.k = [
            send(self.chunk(far, 0), self.relay_in[0], self.right),
            send(self.chunk(far, 1), self.relay_in[1], self.left),
            send(self.chunk(after, 1), self.direct[1], self.right),
            send(self.chunk(before, 0), self.direct[0], self.left),
        ]

    def relay(self):
        me, copies = self.me, self.copies
        after, before = (me + 1) % 4, (me + 3) % 4
        copies.landed(self.k[0], self.relay_in[0])
        add_into(self.relay_in[0], self.chunk(after, 0))
        k0 = copies.send(self.relay_in[0], self.final[0], self.right)
        copies.landed(self.k[1], self.relay_in[1])
        add_into(self.relay_in[1], self.chunk(before, 1))
        k1 = copies.send(self.relay_in[1], self.final[1], self.left)
        self.k += [k0, k1]

    def finish(self, out):
        copies = self.copies
        copies.landed(self.k[3], self.direct[0])
        copies.landed(self.k[4], self.final[0])
        store_sum(out(0), self.chunk(self.me, 0), self.direct[0], self.final[0])
        copies.landed(self.k[2], self.direct[1])
        copies.landed(self.k[5], self.final[1])
        store_sum(out(1), self.chunk(self.me, 1), self.direct[1], self.final[1])


class RingGather:
    def __init__(self, copies, me, right, left, piece, halves):
        self.copies, self.me, self.right, self.left = copies, me, right, left
        self.piece, self.halves = piece, halves

    def start(self):
        mine = self.piece(self.me)
        self.k = [
            self.copies.send(mine, mine, self.right),
            self.copies.send(mine, mine, self.left),
        ]

    def relay(self):
        before, after = (self.me + 3) % 4, (self.me + 1) % 4
        self.copies.landed(self.k[0], self.piece(before))
        view = self.halves(before, 0)
        k0 = self.copies.send(view, view, self.right)
        self.copies.landed(self.k[1], self.piece(after))
        view = self.halves(after, 1)
        k1 = self.copies.send(view, view, self.left)
        self.k += [k0, k1]

    def finish(self):
        far = (self.me + 2) % 4
        self.copies.landed(self.k[2], self.halves(far, 0))
        self.copies.landed(self.k[3], self.halves(far, 1))


def add_into(ref, other):
    ref[...] = (ref[...].astype(f32) + other[...].astype(f32)).astype(ref.dtype)


def store_sum(out, *parts):
    total = parts[0][...].astype(f32)
    for part in parts[1:]:
        total = total + part[...].astype(f32)
    out[...] = total.astype(out.dtype)


def rows(start, size, step=16):
    return pl.ds(pl.multiple_of(start, step), size)


def spread_kernel(block, wq, wd, wu, wn, small, xg, oq, od, ou, on, osm, send_sems, recv_sems, local_sems):
    at = Place()
    p, x, y, z, c = at.p, at.x, at.y, at.z, at.c
    greet(
        [at.at_x(1), at.at_x(3), at.at_y(1), at.at_y(2), at.at_y(3), at.at_z(1), at.at_z(3), at.sibling()]
    )
    copies = Copies(send_sems, recv_sems, at.at_x(1))
    weights = [(wq, oq), (wd, od), (wu, ou), (wn, on)]

    def piece(ref, zz, cc):
        if ref.shape[-2] == INNER:
            return ref.at[rows(48 * zz, 48), pl.ds(pl.multiple_of(384 * cc, 128), 384)]
        return ref.at[rows(192 * zz + 96 * cc, 96)]

    def half(ref, zz, cc, h):
        if ref.shape[-2] == INNER:
            return ref.at[rows(48 * zz + 32 * h, 32 - 16 * h), pl.ds(pl.multiple_of(384 * cc, 128), 384)]
        return ref.at[rows(192 * zz + 96 * cc + 48 * h, 48)]

    quarter = rows(64 * x, 64)
    first = [
        copies.send(block.at[(y + k) % 4, quarter], xg.at[p, at.low, quarter], at.at_y(k)) for k in (1, 3, 2)
    ]
    sent = [
        copies.send(piece(src, z, c), piece(dst.at[p], z, c), at.partner()) for src, dst in weights
    ]
    sent_small = copies.send(small, osm.at[p], at.partner())
    local = [
        pltpu.make_async_copy(src, dst, local_sems.at[n])
        for n, (src, dst) in enumerate(
            [(block.at[y], xg.at[p, at.low]), (small, osm.at[p])] + [(s, d.at[p]) for s, d in weights]
        )
    ]
    for copy in local:
        copy.start()
    gathers = []
    for k, index in zip((1, 3, 2), first):
        source = (y + 4 - k) % 4
        slot = xg.at[source // 2, source % 2]
        copies.landed(index, slot.at[quarter])
        gather = RingGather(
            copies,
            x,
            at.at_x(1),
            at.at_x(3),
            lambda j, slot=slot: slot.at[rows(64 * j, 64)],
            lambda j, h, slot=slot: slot.at[rows(64 * j + 32 * h, 32)],
        )
        gather.start()
        gathers.append(gather)
    others = [dst.at[1 - p] for _, dst in weights]
    rings, shared = [], []
    for other, index in zip(others, sent):
        copies.landed(index, piece(other, z, c))
        ring = RingGather(
            copies,
            z,
            at.at_z(1),
            at.at_z(3),
            lambda j, other=other: piece(other, j, c),
            lambda j, h, other=other: half(other, j, c, h),
        )
        ring.start()
        rings.append(ring)
        mine = piece(other, z, c)
        shared.append((copies.send(mine, mine, at.sibling()), piece(other, z, 1 - c)))
    for gather in gathers:
        gather.relay()
    for other, ring in zip(others, rings):
        ring.relay()
        for j in ((z + 3) % 4, (z + 1) % 4):
            mine = piece(other, j, c)
            shared.append((copies.send(mine, mine, at.sibling()), piece(other, j, 1 - c)))
    for gather in gathers:
        gather.finish()
    for other, ring in zip(others, rings):
        ring.finish()
        j = (z + 2) % 4
        mine = piece(other, j, c)
        shared.append((copies.send(mine, mine, at.sibling()), piece(other, j, 1 - c)))
    copies.landed(sent_small, osm.at[1 - p])
    for index, view in shared:
        copies.landed(index, view)
    for copy in local:
        copy.wait()
    copies.drain()


SPREAD_COPIES = 3 + 4 + 1 + 12 + 16 + 16


def spread(block, wq, wd, wu, wn, small):
    any_space = pl.BlockSpec(memory_space=pl.ANY)
    shapes = [(2, 2, BLOCK, WIDTH)] + [(2,) + w.shape for w in (wq, wd, wu, wn)]
    return pl.pallas_call(
        spread_kernel,
        out_shape=[jax.ShapeDtypeStruct(s, bf16) for s in shapes]
        + [jax.ShapeDtypeStruct((2,) + small.shape, f32)],
        in_specs=[any_space] * 6,
        out_specs=[any_space] * 6,
        scratch_shapes=[
            pltpu.SemaphoreType.DMA((SPREAD_COPIES,)),
            pltpu.SemaphoreType.DMA((SPREAD_COPIES,)),
            pltpu.SemaphoreType.DMA((6,)),
        ],
        compiler_params=pltpu.CompilerParams(collective_id=0, has_side_effects=True),
        name="spread",
    )(block, wq, wd, wu, wn, small)


def x_sums(at, copies, parts, bufs):
    sums = []
    for n, part in enumerate(parts):
        sums.append(
            RingSum(
                copies,
                at.x,
                at.at_x(1),
                at.at_x(3),
                lambda j, h, part=part: part.at[h, rows(64 * j, 64)],
                [bufs.at[n, 0], bufs.at[n, 1]],
                [bufs.at[n, 2], bufs.at[n, 3]],
                [bufs.at[n, 4], bufs.at[n, 5]],
            )
        )
    return sums


SPLITS = 2


def total_kernel(part, out, bufs, send_sems, recv_sems):
    at = Place()
    greet([at.at_x(1), at.at_x(3)])
    copies = Copies(send_sems, recv_sems, at.at_x(1))
    wide = WIDTH // SPLITS
    cols = [pl.ds(n * wide, wide) for n in range(SPLITS)]
    sums = x_sums(at, copies, [part.at[:, :, col] for col in cols], bufs)
    for ring in sums:
        ring.start()
    for ring in sums:
        ring.relay()
    gathers = []
    for ring, col in zip(sums, cols):
        ring.finish(lambda h, col=col: out.at[h, rows(64 * at.x, 64), col])
        gather = RingGather(
            copies,
            at.x,
            at.at_x(1),
            at.at_x(3),
            lambda j, col=col: out.at[:, rows(64 * j, 64), col],
            lambda j, h, col=col: out.at[h, rows(64 * j, 64), col],
        )
        gather.start()
        gathers.append(gather)
    for gather in gathers:
        gather.relay()
    for gather in gathers:
        gather.finish()
    copies.drain()


def total_over_tensor(part):
    vmem = pl.BlockSpec(memory_space=pltpu.VMEM)
    count = SPLITS * 10
    return pl.pallas_call(
        total_kernel,
        out_shape=jax.ShapeDtypeStruct((2, BLOCK, WIDTH), bf16),
        in_specs=[vmem],
        out_specs=vmem,
        scratch_shapes=[
            pltpu.VMEM((SPLITS, 6, 64, WIDTH // SPLITS), bf16),
            pltpu.SemaphoreType.DMA((count,)),
            pltpu.SemaphoreType.DMA((count,)),
        ],
        compiler_params=pltpu.CompilerParams(
            collective_id=1, has_side_effects=True, vmem_limit_bytes=VMEM_LIMIT
        ),
        name="total",
    )(part)


def pieces_kernel(one, two, out, bufs, send_sems, recv_sems):
    at = Place()
    greet([at.at_x(1), at.at_x(3)])
    copies = Copies(send_sems, recv_sems, at.at_x(1))
    sums = x_sums(at, copies, [one, two], bufs)
    for ring in sums:
        ring.start()
    for ring in sums:
        ring.relay()
    for n, ring in enumerate(sums):
        ring.finish(lambda h, n=n: out.at[n, h])
    copies.drain()


def pieces_over_tensor(one, two):
    vmem = pl.BlockSpec(memory_space=pltpu.VMEM)
    return pl.pallas_call(
        pieces_kernel,
        out_shape=jax.ShapeDtypeStruct((2, 2, 64, WIDTH), bf16),
        in_specs=[vmem, vmem],
        out_specs=vmem,
        scratch_shapes=[
            pltpu.VMEM((2, 6, 64, WIDTH), bf16),
            pltpu.SemaphoreType.DMA((12,)),
            pltpu.SemaphoreType.DMA((12,)),
        ],
        compiler_params=pltpu.CompilerParams(
            collective_id=2, has_side_effects=True, vmem_limit_bytes=VMEM_LIMIT
        ),
        name="pieces",
    )(one, two)


def final_kernel(
    grads, small, slices, out, small_out, back,
    chip, a_one, b_one, a_bufs, b_bufs, a_tail, a_tail2, b_tail, b_tail2, got, send_sems, recv_sems, local_sem,
):
    at = Place()
    x, y, z, c, low = at.x, at.y, at.z, at.c, at.low
    greet(
        [at.at_x(k) for k in (1, 2, 3)]
        + [at.at_y(k) for k in (1, 2, 3)]
        + [at.at_z(k) for k in (1, 2, 3)]
        + [at.sibling()]
    )
    copies = Copies(send_sems, recv_sems, at.at_x(1))
    send, landed = copies.send, copies.landed
    left_cols, right_cols = pl.ds(0, 384), pl.ds(384, 384)
    quarter = rows(64 * x, 64)
    mine, theirs = rows(1152 * c, 1152), rows(1152 * (1 - c), 1152)

    core = []
    for cols in (left_cols, right_cols):
        for layer in range(2):
            core.append(send(grads.at[layer, theirs, cols], chip.at[layer, :, cols], at.sibling()))
    home = []
    for k in (1, 3, 2):
        j = (y + k) % 4
        home.append((k, send(slices.at[j // 2, j % 2], back.at[y, quarter], at.at_y(k))))
    own = pltpu.make_async_copy(slices.at[y // 2, y % 2], back.at[y, quarter], local_sem)
    own.start()
    small_x = [(k, send(small, got.at[k - 1], at.at_x(k))) for k in (1, 3, 2)]

    def add_core(n, layer, cols):
        landed(core[n], chip.at[layer, :, cols])

        def body(i, carry):
            here = rows(i * 128, 128)
            there = rows(1152 * c + i * 128, 128)
            chip[layer, here, cols] = (
                chip[layer, here, cols].astype(f32) + grads[layer, there, cols].astype(f32)
            ).astype(bf16)
            return carry

        lax.fori_loop(0, 9, body, 0)

    add_core(0, 0, left_cols)
    add_core(1, 1, left_cols)
    a_y = RingSum(
        copies, y, at.at_y(1), at.at_y(3),
        lambda j, h: chip.at[j // 2, rows(576 * (j % 2) + 288 * h, 288), left_cols],
        [a_bufs.at[0], a_bufs.at[1]], [a_bufs.at[2], a_bufs.at[3]], [a_bufs.at[4], a_bufs.at[5]],
    )
    a_y.start()
    add_core(2, 0, right_cols)
    add_core(3, 1, right_cols)
    b_z = RingSum(
        copies, z, at.at_z(1), at.at_z(3),
        lambda j, h: chip.at[h, rows(288 * j, 288), right_cols],
        [b_bufs.at[0], b_bufs.at[1]], [b_bufs.at[2], b_bufs.at[3]], [b_bufs.at[4], b_bufs.at[5]],
    )
    b_z.start()

    own.wait()
    for k, index in home:
        landed(index, back.at[(y + 4 - k) % 4, quarter])
    outer = RingGather(
        copies, x, at.at_x(1), at.at_x(3),
        lambda j: back.at[:, rows(64 * j, 64)],
        lambda j, h: back.at[pl.ds(2 * h, 2), rows(64 * j, 64)],
    )
    outer.start()
    for k, index in small_x:
        landed(index, got.at[k - 1])
    normed = lax.broadcasted_iota(jnp.int32, small.shape, 1) < 4
    others = got[0] + got[1] + got[2]
    small_out[...] = small[...] + jnp.where(normed, others, 0.0)
    small_z = [(k, send(small_out, got.at[2 + k], at.at_z(k))) for k in (1, 3, 2)]

    a_y.relay()
    b_z.relay()
    outer.relay()
    a_y.finish(lambda h: a_one.at[pl.ds(288 * h, 288)])

    def uneven(ref, start, h):
        return ref.at[rows(start + 80 * h, 80 - 16 * h)]

    a_rows = 1152 * c + 576 * low
    a_z = RingSum(
        copies, z, at.at_z(1), at.at_z(3),
        lambda j, h: uneven(a_one, 144 * j, h),
        [a_tail.at[0], a_tail2.at[0]], [a_tail.at[1], a_tail2.at[1]], [a_tail.at[2], a_tail2.at[2]],
    )
    a_z.start()
    b_z.finish(lambda h: b_one.at[h])
    b_rows = 1152 * c + 288 * z
    b_y = RingSum(
        copies, y, at.at_y(1), at.at_y(3),
        lambda j, h: b_one.at[j // 2, rows(144 * (j % 2) + 80 * h, 80 - 16 * h)],
        [b_tail.at[0], b_tail2.at[0]], [b_tail.at[1], b_tail2.at[1]], [b_tail.at[2], b_tail2.at[2]],
    )
    b_y.start()

    for k, index in small_z:
        landed(index, got.at[2 + k])
    for k, index in small_z:
        copies.started[index].wait_send()
    small_out[...] = small_out[...] + (got[3] + got[4] + got[5])
    small_y = [(k, send(small_out, got.at[5 + k], at.at_y(k))) for k in (1, 3, 2)]

    a_z.relay()
    b_y.relay()
    a_out, b_out = out.at[:, left_cols], out.at[:, right_cols]
    a_z.finish(lambda h: uneven(a_out, a_rows + 144 * z, h))
    a_gather = RingGather(
        copies, z, at.at_z(1), at.at_z(3),
        lambda j: a_out.at[rows(a_rows + 144 * j, 144)],
        lambda j, h: uneven(a_out, a_rows + 144 * j, h),
    )
    a_gather.start()
    b_y.finish(lambda h: uneven(b_out, b_rows + 144 * low, h))
    view = b_out.at[rows(b_rows + 144 * low, 144)]
    b_beside = send(view, view, at.beside())

    for k, index in small_y:
        landed(index, got.at[5 + k])
    for k, index in small_y:
        copies.started[index].wait_send()
    small_out[...] = small_out[...] + (got[6] + got[7] + got[8])
    small_c = send(small_out, got.at[9], at.sibling())

    landed(b_beside, b_out.at[rows(b_rows + 144 * (1 - low), 144)])
    b_gather = RingGather(
        copies, z, at.at_z(1), at.at_z(3),
        lambda j: b_out.at[rows(1152 * c + 288 * j, 288)],
        lambda j, h: b_out.at[rows(1152 * c + 288 * j + 144 * h, 144)],
    )
    b_gather.start()
    a_gather.relay()
    a_gather.finish()
    view = a_out.at[rows(a_rows, 576)]
    a_beside = send(view, view, at.beside())
    a_half = send(view, view, at.sibling())
    b_gather.relay()
    landed(small_c, got.at[9])
    copies.started[small_c].wait_send()
    small_out[...] = small_out[...] + got[9]
    outer.finish()
    landed(a_beside, a_out.at[rows(1152 * c + 576 * (1 - low), 576)])
    view = a_out.at[rows(1152 * c + 576 * (1 - low), 576)]
    a_other = send(view, view, at.sibling())
    b_gather.finish()
    view = b_out.at[mine]
    b_all = send(view, view, at.sibling())
    landed(a_half, a_out.at[rows(1152 * (1 - c) + 576 * low, 576)])
    landed(a_other, a_out.at[rows(1152 * (1 - c) + 576 * (1 - low), 576)])
    landed(b_all, b_out.at[theirs])
    waited = {index for _, index in small_z} | {index for _, index in small_y} | {small_c}
    for index, copy in enumerate(copies.started):
        if index not in waited:
            copy.wait_send()


FINAL_COPIES = 64


def final(grads, small, slices):
    vmem = pl.BlockSpec(memory_space=pltpu.VMEM)
    return pl.pallas_call(
        final_kernel,
        out_shape=[
            jax.ShapeDtypeStruct((GRAD_ROWS, WIDTH), bf16),
            jax.ShapeDtypeStruct((2, 8, WIDTH), f32),
            jax.ShapeDtypeStruct((4, BLOCK, WIDTH), bf16),
        ],
        in_specs=[vmem] * 3,
        out_specs=[vmem] * 3,
        scratch_shapes=[
            pltpu.VMEM((2, 1152, WIDTH), bf16),
            pltpu.VMEM((576, 384), bf16),
            pltpu.VMEM((2, 288, 384), bf16),
            pltpu.VMEM((6, 288, 384), bf16),
            pltpu.VMEM((6, 288, 384), bf16),
            pltpu.VMEM((3, 80, 384), bf16),
            pltpu.VMEM((3, 64, 384), bf16),
            pltpu.VMEM((3, 80, 384), bf16),
            pltpu.VMEM((3, 64, 384), bf16),
            pltpu.VMEM((10, 2, 8, WIDTH), f32),
            pltpu.SemaphoreType.DMA((FINAL_COPIES,)),
            pltpu.SemaphoreType.DMA((FINAL_COPIES,)),
            pltpu.SemaphoreType.DMA,
        ],
        compiler_params=pltpu.CompilerParams(
            collective_id=3, has_side_effects=True, vmem_limit_bytes=VMEM_LIMIT
        ),
        name="final",
    )(grads, small, slices)


def normed_of(flat):
    middle = jnp.mean(flat, axis=-1, keepdims=True)
    centred = flat - middle
    inverse = lax.rsqrt(jnp.mean(centred * centred, axis=-1, keepdims=True) + EPS)
    return centred * inverse, inverse


def norm_back(scaled, normed, inverse):
    inner = scaled - jnp.mean(scaled, axis=-1, keepdims=True)
    inner = inner - normed * jnp.mean(scaled * normed, axis=-1, keepdims=True)
    return inner * inverse


def rotate(vector, cosine, sine):
    portion = vector[..., :ROT]
    half = ROT // 2
    turned = jnp.concatenate([-portion[..., half:], portion[..., :half]], axis=-1)
    return jnp.concatenate([portion * cosine + turned * sine, vector[..., ROT:]], axis=-1)


def unrotate(grad, cosine, sine):
    portion = grad[..., :ROT]
    half = ROT // 2
    moved = portion * sine
    back = jnp.concatenate([moved[..., half:], -moved[..., :half]], axis=-1)
    return jnp.concatenate([portion * cosine + back, grad[..., ROT:]], axis=-1)


def swapped(value):
    return lax.ppermute(value, "dp", [(n, n ^ 1) for n in range(16)])


def interleaved(own, other):
    return jnp.concatenate([own[:BLOCK], other[:BLOCK], own[BLOCK:], other[BLOCK:]], axis=0)


def gelu_parts(hidden):
    return jax.nn.gelu(hidden, approximate=False)


SPANS = ((0, BLOCK, 2 * BLOCK), (BLOCK, 2 * BLOCK, 4 * BLOCK))


def forward_layer(flat, w, geometry):
    allowed, cosine, sine = geometry
    scale = HEAD_DIM ** (-0.5)
    normed, inverse = normed_of(flat)
    first = (normed * w["g1"] + w["s1"]).astype(bf16)
    second = (normed * w["g2"] + w["s2"]).astype(bf16)
    packed = jnp.dot(first, w["qkv"], preferred_element_type=f32) + w["qkv_bias"]
    packed = packed.reshape(2 * BLOCK, HEADS, 3, HEAD_DIM)
    query = rotate(packed[:, :, 0], cosine, sine).astype(bf16)
    key = rotate(packed[:, :, 1], cosine, sine).astype(bf16)
    value = packed[:, :, 2].astype(bf16)
    both = jnp.concatenate([key.reshape(-1, INNER), value.reshape(-1, INNER)], axis=1)
    other = swapped(both)
    hidden = jnp.dot(second, w["up"], preferred_element_type=f32) + w["up_bias"]
    active = gelu_parts(hidden).astype(bf16)
    both_all = interleaved(both, other)
    keys = both_all[:, :INNER].reshape(-1, HEADS, HEAD_DIM)
    values = both_all[:, INNER:].reshape(-1, HEADS, HEAD_DIM)
    mixed, logs = [], []
    for (lo, hi, span), allow in zip(SPANS, allowed):
        score = (
            jnp.einsum("qhd,khd->hqk", query[lo:hi], keys[:span], preferred_element_type=f32) * scale
        )
        score = jnp.where(allow[None], score, MASKED)
        top = jnp.max(score, axis=-1, keepdims=True)
        expo = jnp.exp(score - top)
        total = jnp.sum(expo, axis=-1, keepdims=True)
        weights = (expo / total).astype(bf16)
        mixed.append(
            jnp.einsum("hqk,khd->qhd", weights, values[:span], preferred_element_type=f32)
        )
        logs.append(top + jnp.log(total))
    mixed = jnp.concatenate(mixed, axis=0).reshape(2 * BLOCK, INNER).astype(bf16)
    partial = jnp.dot(mixed, w["dense"], preferred_element_type=f32)
    partial = partial + jnp.dot(active, w["down"], preferred_element_type=f32)
    partial = partial.astype(bf16).reshape(2, BLOCK, WIDTH)
    kept = (normed, inverse, first, second, query, keys, values, logs, mixed, hidden, active)
    return partial, kept


def backward_layer(grad_low, w, geometry, kept):
    allowed, cosine, sine = geometry
    scale = HEAD_DIM ** (-0.5)
    normed, inverse, first, second, query, keys, values, logs, mixed, hidden, active = kept
    d_mixed = jnp.einsum("rn,kn->rk", grad_low, w["dense"], preferred_element_type=f32)
    d_mixed = d_mixed.astype(bf16).reshape(2 * BLOCK, HEADS, HEAD_DIM)
    d_query, d_keys, d_values = [], [], []
    for (lo, hi, span), allow, log_total in zip(SPANS, allowed, logs):
        q, dm = query[lo:hi], d_mixed[lo:hi]
        score = jnp.einsum("qhd,khd->hqk", q, keys[:span], preferred_element_type=f32) * scale
        prob = jnp.exp(jnp.where(allow[None], score, MASKED) - log_total)
        prob_low = prob.astype(bf16)
        d_prob = jnp.einsum("qhd,khd->hqk", dm, values[:span], preferred_element_type=f32)
        d_score = prob * (d_prob - jnp.sum(prob * d_prob, axis=-1, keepdims=True))
        d_score = d_score.astype(bf16)
        d_query.append(
            jnp.einsum("hqk,khd->qhd", d_score, keys[:span], preferred_element_type=f32) * scale
        )
        d_keys.append(jnp.einsum("hqk,qhd->khd", d_score, q, preferred_element_type=f32) * scale)
        d_values.append(jnp.einsum("hqk,qhd->khd", prob_low, dm, preferred_element_type=f32))
    d_query = jnp.concatenate(d_query, axis=0)
    halves = []
    for short, long in (d_keys, d_values):
        halves.append(jnp.concatenate([long[: 2 * BLOCK] + short, long[2 * BLOCK :]], axis=0))
    d_both = jnp.concatenate([half.reshape(-1, INNER) for half in halves], axis=1)
    d_both = d_both.reshape(2, 2, BLOCK, 2 * INNER)
    got = swapped(d_both[:, 1].astype(bf16))
    d_active = jnp.einsum("rn,kn->rk", grad_low, w["down"], preferred_element_type=f32)
    d_hidden = jax.vjp(gelu_parts, hidden)[1](d_active)[0]
    d_hidden = d_hidden.astype(bf16)
    d_second = jnp.einsum("rn,kn->rk", d_hidden, w["up"], preferred_element_type=f32)
    d_up = jnp.einsum("rk,rn->kn", second, d_hidden, preferred_element_type=bf16)
    d_dense = jnp.einsum("rk,rn->kn", mixed, grad_low, preferred_element_type=bf16)
    d_down = jnp.einsum("rk,rn->kn", active, grad_low, preferred_element_type=bf16)
    d_both = (d_both[:, 0] + got.astype(f32)).reshape(2 * BLOCK, 2, HEADS, HEAD_DIM)
    d_query = unrotate(d_query, cosine, sine)
    d_key = unrotate(d_both[:, 0], cosine, sine)
    d_packed = jnp.stack([d_query, d_key, d_both[:, 1]], axis=2)
    d_packed = d_packed.reshape(2 * BLOCK, 3 * INNER).astype(bf16)
    d_first = jnp.einsum("rn,kn->rk", d_packed, w["qkv"], preferred_element_type=f32)
    d_qkv = jnp.einsum("rn,rk->nk", d_packed, first, preferred_element_type=bf16)
    scaled = d_first * w["g1"] + d_second * w["g2"]
    scaled = scaled.astype(bf16).reshape(2, BLOCK, WIDTH)
    small = jnp.stack(
        [
            jnp.sum(d_first * normed, axis=0),
            jnp.sum(d_first, axis=0),
            jnp.sum(d_second * normed, axis=0),
            jnp.sum(d_second, axis=0),
            jnp.sum(grad_low.astype(f32), axis=0),
            jnp.sum(d_hidden.astype(f32), axis=0),
            jnp.pad(jnp.sum(d_packed.astype(f32), axis=0), (0, WIDTH - 3 * INNER)),
            jnp.zeros((WIDTH,), f32),
        ]
    )
    grads = jnp.concatenate([d_qkv, d_dense, d_up, d_down], axis=0)
    return scaled, grads, small


def geometry_of(segment_ids):
    at = Place()
    seq = lax.dynamic_slice(segment_ids, (at.y, at.z, 0), (1, 1, SEQ))[0, 0]
    spots = jnp.arange(SEQ, dtype=jnp.int32)
    own = [at.c * BLOCK, (2 + at.c) * BLOCK]
    other = [(1 - at.c) * BLOCK, (3 - at.c) * BLOCK]
    order = [own[0], other[0], own[1], other[1]]
    labels = jnp.concatenate([lax.dynamic_slice(seq, (s,), (BLOCK,)) for s in order])
    places = jnp.concatenate([s + jnp.arange(BLOCK, dtype=jnp.int32) for s in order])
    mine = jnp.concatenate([labels[:BLOCK], labels[2 * BLOCK : 3 * BLOCK]])
    my_places = jnp.concatenate([places[:BLOCK], places[2 * BLOCK : 3 * BLOCK]])
    before = jnp.sum((seq[None, :] < mine[:, None]).astype(jnp.int32), axis=1)
    allowed = []
    for lo, hi, span in SPANS:
        allowed.append(
            (labels[None, :span] == mine[lo:hi, None]) & (places[None, :span] <= my_places[lo:hi, None])
        )
    half = ROT // 2
    freqs = 10000.0 ** (-(2.0 * jnp.arange(half, dtype=f32)) / ROT)
    angles = (my_places - before).astype(f32)[:, None] * freqs
    angles = jnp.concatenate([angles, angles], axis=-1)[:, None, :]
    return allowed, jnp.cos(angles), jnp.sin(angles)


def local(
    boundary,
    segment_ids,
    attn_gain,
    attn_shift,
    mlp_gain,
    mlp_shift,
    qkv_weight,
    qkv_bias,
    dense_weight,
    dense_bias,
    up_weight,
    up_bias,
    down_weight,
    down_bias,
):
    at = Place()
    small = jnp.concatenate(
        [
            attn_gain,
            attn_shift,
            mlp_gain,
            mlp_shift,
            jnp.pad(qkv_bias, ((0, 0), (0, WIDTH - 3 * INNER))),
            up_bias,
            dense_bias + down_bias,
            jnp.zeros((1, WIDTH), f32),
        ]
    )
    xg, wq, wd, wu, wn, smalls = spread(
        boundary[0].astype(bf16), qkv_weight[0], dense_weight[0], up_weight[0], down_weight[0], small
    )
    layers = []
    for n in range(2):
        s = smalls[n]
        layers.append(
            dict(
                g1=s[0], s1=s[1], g2=s[2], s2=s[3], qkv_bias=s[4, : 3 * INNER], up_bias=s[5], extra=s[6],
                qkv=wq[n], dense=wd[n], up=wu[n], down=wn[n],
            )
        )
    geometry = geometry_of(segment_ids)
    flat = xg[0].reshape(2 * BLOCK, WIDTH).astype(f32)
    partial, kept_zero = forward_layer(flat, layers[0], geometry)
    branch = total_over_tensor(partial).reshape(2 * BLOCK, WIDTH).astype(f32)
    middle = flat + (branch + layers[0]["extra"])
    partial_one, kept_one = forward_layer(middle, layers[1], geometry)

    grad = xg[1].reshape(2 * BLOCK, WIDTH)
    scaled, grads_one, small_one = backward_layer(grad, layers[1], geometry, kept_one)
    scaled = total_over_tensor(scaled).reshape(2 * BLOCK, WIDTH).astype(f32)
    grad_zero = grad.astype(f32) + norm_back(scaled, kept_one[0], kept_one[1])
    scaled, grads_zero, small_zero = backward_layer(
        grad_zero.astype(bf16), layers[0], geometry, kept_zero
    )
    sums = pieces_over_tensor(scaled, partial_one).astype(f32)

    def quarter(value):
        value = value.reshape(2, BLOCK, value.shape[-1])
        return lax.dynamic_slice_in_dim(value, 64 * at.x, 64, 1)

    grad_in = quarter(grad_zero) + norm_back(sums[0], quarter(kept_zero[0]), quarter(kept_zero[1]))
    result = quarter(middle) + (sums[1] + layers[1]["extra"])
    slices = jnp.stack([grad_in, result]).astype(bf16)
    total, small_total, back = final(
        jnp.stack([grads_zero, grads_one]), jnp.stack([small_zero, small_one]), slices
    )
    mine = lax.dynamic_index_in_dim(small_total, at.p, 0, keepdims=False)
    total = total.astype(f32)
    d_qkv = total[: 3 * INNER].T
    d_dense = total[3 * INNER : 4 * INNER]
    d_up = total[4 * INNER : 4 * INNER + WIDTH]
    d_down = total[4 * INNER + WIDTH :]
    return (
        back.astype(f32)[None],
        mine[0:1],
        mine[1:2],
        mine[2:3],
        mine[3:4],
        d_qkv[None],
        mine[6:7, : 3 * INNER],
        d_dense[None],
        mine[4:5],
        d_up[None],
        mine[5:6],
        d_down[None],
        mine[4:5],
    )


def solution(mesh):
    in_specs = (
        P("pipe", None, "dp", None),
        P(),
        P("pipe", None),
        P("pipe", None),
        P("pipe", None),
        P("pipe", None),
        P("pipe", None, "tensor"),
        P("pipe", "tensor"),
        P("pipe", "tensor", None),
        P("pipe", None),
        P("pipe", None, "tensor"),
        P("pipe", "tensor"),
        P("pipe", "tensor", None),
        P("pipe", None),
    )
    out_specs = (
        P("pipe", None, "dp", None),
        P("pipe", None),
        P("pipe", None),
        P("pipe", None),
        P("pipe", None),
        P("pipe", None, "tensor"),
        P("pipe", "tensor"),
        P("pipe", "tensor", None),
        P("pipe", None),
        P("pipe", None, "tensor"),
        P("pipe", "tensor"),
        P("pipe", "tensor", None),
        P("pipe", None),
    )
    return jax.shard_map(local, mesh=mesh, in_specs=in_specs, out_specs=out_specs, check_vma=False)
```

```python
import functools

import jax
import jax.numpy as jnp
from jax import lax
from jax.experimental import pallas as pl
from jax.experimental.pallas import tpu as pltpu
from jax.sharding import PartitionSpec as P

MESH = pl.DeviceIdType.MESH
HEAD_DIM = 64
ROT = 16
EPS = 1e-05
MASKED = -1e30
WIDTH = 768
SEQ = 1024
BLOCK = 256
HEADS = 3
INNER = HEADS * HEAD_DIM
GRAD_ROWS = 2304
bf16 = jnp.bfloat16
f32 = jnp.float32
VMEM_LIMIT = 56 * 1024 * 1024


class Place:
    def __init__(self):
        self.p = lax.axis_index("pipe")
        self.d = lax.axis_index("dp")
        self.x = lax.axis_index("tensor")
        self.z = self.d // 4
        self.low = (self.d // 2) % 2
        self.c = self.d % 2
        self.y = 2 * self.p + self.low

    def at_x(self, steps):
        return (self.p, self.d, (self.x + steps) % 4)

    def at_y(self, steps):
        y = (self.y + steps) % 4
        return (y // 2, self.z * 4 + (y % 2) * 2 + self.c, self.x)

    def at_z(self, steps):
        return (self.p, ((self.z + steps) % 4) * 4 + self.d % 4, self.x)

    def sibling(self):
        return (self.p, self.d + 1 - 2 * self.c, self.x)

    def partner(self):
        return (1 - self.p, self.z * 4 + (1 - self.low) * 2 + self.c, self.x)

    def beside(self):
        return (self.p, self.z * 4 + (1 - self.low) * 2 + self.c, self.x)


def greet(devices):
    barrier = pltpu.get_barrier_semaphore()
    for device in devices:
        pl.semaphore_signal(barrier, inc=1, device_id=device, device_id_type=MESH)
    pl.semaphore_wait(barrier, len(devices))


class Copies:
    def __init__(self, send_sems, recv_sems, somebody):
        self.send_sems, self.recv_sems = send_sems, recv_sems
        self.somebody = somebody
        self.count = 0
        self.started = []

    def send(self, src, dst, device):
        k = self.count
        self.count += 1
        copy = pltpu.make_async_remote_copy(
            src_ref=src,
            dst_ref=dst,
            send_sem=self.send_sems.at[k],
            recv_sem=self.recv_sems.at[k],
            device_id=device,
            device_id_type=MESH,
        )
        copy.start()
        self.started.append(copy)
        return k

    def landed(self, k, dst):
        pltpu.make_async_remote_copy(
            src_ref=dst,
            dst_ref=dst,
            send_sem=self.send_sems.at[k],
            recv_sem=self.recv_sems.at[k],
            device_id=self.somebody,
            device_id_type=MESH,
        ).wait_recv()

    def drain(self):
        for copy in self.started:
            copy.wait_send()


class RingSum:
    def __init__(self, copies, me, right, left, chunk, relay, direct, final):
        self.copies, self.me, self.right, self.left = copies, me, right, left
        self.chunk, self.relay_in, self.direct, self.final = chunk, relay, direct, final

    def start(self):
        me, send = self.me, self.copies.send
        far, after, before = (me + 2) % 4, (me + 1) % 4, (me + 3) % 4
        self.k = [
            send(self.chunk(far, 0), self.relay_in[0], self.right),
            send(self.chunk(far, 1), self.relay_in[1], self.left),
            send(self.chunk(after, 1), self.direct[1], self.right),
            send(self.chunk(before, 0), self.direct[0], self.left),
        ]

    def relay(self):
        me, copies = self.me, self.copies
        after, before = (me + 1) % 4, (me + 3) % 4
        copies.landed(self.k[0], self.relay_in[0])
        add_into(self.relay_in[0], self.chunk(after, 0))
        k0 = copies.send(self.relay_in[0], self.final[0], self.right)
        copies.landed(self.k[1], self.relay_in[1])
        add_into(self.relay_in[1], self.chunk(before, 1))
        k1 = copies.send(self.relay_in[1], self.final[1], self.left)
        self.k += [k0, k1]

    def finish(self, out):
        copies = self.copies
        copies.landed(self.k[3], self.direct[0])
        copies.landed(self.k[4], self.final[0])
        store_sum(out(0), self.chunk(self.me, 0), self.direct[0], self.final[0])
        copies.landed(self.k[2], self.direct[1])
        copies.landed(self.k[5], self.final[1])
        store_sum(out(1), self.chunk(self.me, 1), self.direct[1], self.final[1])


class RingGather:
    def __init__(self, copies, me, right, left, piece, halves):
        self.copies, self.me, self.right, self.left = copies, me, right, left
        self.piece, self.halves = piece, halves

    def start(self):
        mine = self.piece(self.me)
        self.k = [
            self.copies.send(mine, mine, self.right),
            self.copies.send(mine, mine, self.left),
        ]

    def relay(self):
        before, after = (self.me + 3) % 4, (self.me + 1) % 4
        self.copies.landed(self.k[0], self.piece(before))
        view = self.halves(before, 0)
        k0 = self.copies.send(view, view, self.right)
        self.copies.landed(self.k[1], self.piece(after))
        view = self.halves(after, 1)
        k1 = self.copies.send(view, view, self.left)
        self.k += [k0, k1]

    def finish(self):
        far = (self.me + 2) % 4
        self.copies.landed(self.k[2], self.halves(far, 0))
        self.copies.landed(self.k[3], self.halves(far, 1))


def add_into(ref, other):
    ref[...] = (ref[...].astype(f32) + other[...].astype(f32)).astype(ref.dtype)


def store_sum(out, *parts):
    total = parts[0][...].astype(f32)
    for part in parts[1:]:
        total = total + part[...].astype(f32)
    out[...] = total.astype(out.dtype)


def rows(start, size, step=16):
    return pl.ds(pl.multiple_of(start, step), size)


def spread_kernel(
    block, wq, wd, wu, wn, small, xg, oq, od, ou, on, osm,
    hold_x, hold_s, hold_q, hold_d, hold_u, hold_n, send_sems, recv_sems, local_sems,
):
    at = Place()
    p, x, y, z, c = at.p, at.x, at.y, at.z, at.c
    greet(
        [at.at_x(1), at.at_x(3), at.at_y(1), at.at_y(2), at.at_y(3), at.at_z(1), at.at_z(3), at.sibling()]
    )
    copies = Copies(send_sems, recv_sems, at.at_x(1))
    weights = [(wq, oq), (wd, od), (wu, ou), (wn, on)]

    def piece(ref, zz, cc):
        if ref.shape[-2] == WIDTH:
            return ref.at[rows(192 * zz + 96 * cc, 96)]
        each = ref.shape[-2] // 4
        return ref.at[rows(each * zz, each), pl.ds(pl.multiple_of(384 * cc, 128), 384)]

    def half(ref, zz, cc, h):
        if ref.shape[-2] == WIDTH:
            return ref.at[rows(192 * zz + 96 * cc + 48 * h, 48)]
        each = ref.shape[-2] // 4
        more = (each // 2 + 15) // 16 * 16
        size = each - more if h else more
        return ref.at[rows(each * zz + more * h, size), pl.ds(pl.multiple_of(384 * cc, 128), 384)]

    quarter = rows(64 * x, 64)
    first = [
        copies.send(block.at[(y + k) % 4, quarter], xg.at[p, at.low, quarter], at.at_y(k)) for k in (1, 3, 2)
    ]
    sent = [
        copies.send(piece(src, z, c), piece(dst.at[p], z, c), at.partner()) for src, dst in weights
    ]
    sent_small = copies.send(small, osm.at[p], at.partner())
    held = [hold_x, hold_s, hold_q, hold_d, hold_u, hold_n]
    kept = [(block.at[y], xg.at[p, at.low]), (small, osm.at[p])] + [(s, d.at[p]) for s, d in weights]
    inward = [
        pltpu.make_async_copy(src, hold, local_sems.at[n]) for n, ((src, _), hold) in enumerate(zip(kept, held))
    ]
    for copy in inward:
        copy.start()
    outward = []
    for n, ((_, dst), hold) in enumerate(zip(kept, held)):
        inward[n].wait()
        copy = pltpu.make_async_copy(hold, dst, local_sems.at[n + 6])
        copy.start()
        outward.append(copy)
    gathers = []
    for k, index in zip((1, 3, 2), first):
        source = (y + 4 - k) % 4
        slot = xg.at[source // 2, source % 2]
        copies.landed(index, slot.at[quarter])
        gather = RingGather(
            copies,
            x,
            at.at_x(1),
            at.at_x(3),
            lambda j, slot=slot: slot.at[rows(64 * j, 64)],
            lambda j, h, slot=slot: slot.at[rows(64 * j + 32 * h, 32)],
        )
        gather.start()
        gathers.append(gather)
    others = [dst.at[1 - p] for _, dst in weights]
    rings, shared = [], []
    for other, index in zip(others, sent):
        copies.landed(index, piece(other, z, c))
        ring = RingGather(
            copies,
            z,
            at.at_z(1),
            at.at_z(3),
            lambda j, other=other: piece(other, j, c),
            lambda j, h, other=other: half(other, j, c, h),
        )
        ring.start()
        rings.append(ring)
        mine = piece(other, z, c)
        shared.append((copies.send(mine, mine, at.sibling()), piece(other, z, 1 - c)))
    for gather in gathers:
        gather.relay()
    for other, ring in zip(others, rings):
        ring.relay()
        for j in ((z + 3) % 4, (z + 1) % 4):
            mine = piece(other, j, c)
            shared.append((copies.send(mine, mine, at.sibling()), piece(other, j, 1 - c)))
    for gather in gathers:
        gather.finish()
    for other, ring in zip(others, rings):
        ring.finish()
        j = (z + 2) % 4
        mine = piece(other, j, c)
        shared.append((copies.send(mine, mine, at.sibling()), piece(other, j, 1 - c)))
    copies.landed(sent_small, osm.at[1 - p])
    for index, view in shared:
        copies.landed(index, view)
    for copy in outward:
        copy.wait()
    copies.drain()


SPREAD_COPIES = 3 + 4 + 1 + 12 + 16 + 16


def spread(block, wq, wd, wu, wn, small):
    any_space = pl.BlockSpec(memory_space=pl.ANY)
    shapes = [(2, 2, BLOCK, WIDTH)] + [(2,) + w.shape for w in (wq, wd, wu, wn)]
    return pl.pallas_call(
        spread_kernel,
        out_shape=[jax.ShapeDtypeStruct(s, bf16) for s in shapes]
        + [jax.ShapeDtypeStruct((2,) + small.shape, f32)],
        in_specs=[any_space] * 6,
        out_specs=[any_space] * 6,
        scratch_shapes=[
            pltpu.VMEM((BLOCK, WIDTH), bf16),
            pltpu.VMEM(small.shape, f32),
        ]
        + [pltpu.VMEM(w.shape, bf16) for w in (wq, wd, wu, wn)]
        + [
            pltpu.SemaphoreType.DMA((SPREAD_COPIES,)),
            pltpu.SemaphoreType.DMA((SPREAD_COPIES,)),
            pltpu.SemaphoreType.DMA((12,)),
        ],
        compiler_params=pltpu.CompilerParams(
            collective_id=0, has_side_effects=True, vmem_limit_bytes=VMEM_LIMIT
        ),
        name="spread",
    )(block, wq, wd, wu, wn, small)


def x_sums(at, copies, parts, bufs):
    sums = []
    for n, part in enumerate(parts):
        sums.append(
            RingSum(
                copies,
                at.x,
                at.at_x(1),
                at.at_x(3),
                lambda j, h, part=part: part.at[h, rows(64 * j, 64)],
                [bufs.at[n, 0], bufs.at[n, 1]],
                [bufs.at[n, 2], bufs.at[n, 3]],
                [bufs.at[n, 4], bufs.at[n, 5]],
            )
        )
    return sums


SPLITS = 2


def total_kernel(part, out, bufs, send_sems, recv_sems):
    at = Place()
    greet([at.at_x(1), at.at_x(3)])
    copies = Copies(send_sems, recv_sems, at.at_x(1))
    wide = WIDTH // SPLITS
    cols = [pl.ds(n * wide, wide) for n in range(SPLITS)]
    sums = x_sums(at, copies, [part.at[:, :, col] for col in cols], bufs)
    for ring in sums:
        ring.start()
    for ring in sums:
        ring.relay()
    gathers = []
    for ring, col in zip(sums, cols):
        ring.finish(lambda h, col=col: out.at[h, rows(64 * at.x, 64), col])
        gather = RingGather(
            copies,
            at.x,
            at.at_x(1),
            at.at_x(3),
            lambda j, col=col: out.at[:, rows(64 * j, 64), col],
            lambda j, h, col=col: out.at[h, rows(64 * j, 64), col],
        )
        gather.start()
        gathers.append(gather)
    for gather in gathers:
        gather.relay()
    for gather in gathers:
        gather.finish()
    copies.drain()


def total_over_tensor(part):
    vmem = pl.BlockSpec(memory_space=pltpu.VMEM)
    count = SPLITS * 10
    return pl.pallas_call(
        total_kernel,
        out_shape=jax.ShapeDtypeStruct((2, BLOCK, WIDTH), bf16),
        in_specs=[vmem],
        out_specs=vmem,
        scratch_shapes=[
            pltpu.VMEM((SPLITS, 6, 64, WIDTH // SPLITS), bf16),
            pltpu.SemaphoreType.DMA((count,)),
            pltpu.SemaphoreType.DMA((count,)),
        ],
        compiler_params=pltpu.CompilerParams(
            collective_id=1, has_side_effects=True, vmem_limit_bytes=VMEM_LIMIT
        ),
        name="total",
    )(part)


def final_kernel(
    f_zero, e_zero, f_one, e_one, sf_zero, se_zero, sf_one, se_one,
    scaled, branch, grad, normed, inverse, middle, params, out, small_out, back,
    chip, own_half, a_one, b_one, a_bufs, b_bufs, a_tail, a_tail2, b_tail, b_tail2, got, first_small, x_bufs, x_sum,
    slices, send_sems, recv_sems, local_sem, half_sems,
):
    at = Place()
    x, y, z, c, low = at.x, at.y, at.z, at.c, at.low
    greet(
        [at.at_x(k) for k in (1, 2, 3)]
        + [at.at_y(k) for k in (1, 2, 3)]
        + [at.at_z(k) for k in (1, 2, 3)]
        + [at.sibling()]
    )
    copies = Copies(send_sems, recv_sems, at.at_x(1))
    send, landed = copies.send, copies.landed
    left_cols, right_cols = pl.ds(0, 384), pl.ds(384, 384)
    quarter = rows(64 * x, 64)
    mine, theirs = rows(1152 * c, 1152), rows(1152 * (1 - c), 1152)

    layers = ((f_zero, e_zero), (f_one, e_one))
    parts = [(0, 288, 0), (1, 864, 288)]
    core, halves = {}, []
    for cols in (left_cols, right_cols):
        for layer in range(2):
            for which, size, place in parts:
                src = layers[layer][which].at[rows(size * (1 - c), size), cols]
                index = send(src, chip.at[layer, pl.ds(place, size), cols], at.sibling())
                core[cols is right_cols, layer, which] = index
    for layer in range(2):
        for which, size, place in parts:
            copy = pltpu.make_async_copy(
                layers[layer][which].at[rows(size * c, size)],
                own_half.at[layer, pl.ds(place, size)],
                half_sems.at[2 * layer + which],
            )
            copy.start()
            halves.append(copy)
    last = x_sums(at, copies, [scaled, branch], x_bufs)
    for ring in last:
        ring.start()
    for layer, refs in enumerate(((sf_zero, se_zero), (sf_one, se_one))):
        for which, ref in enumerate(refs):
            first_small[layer, pl.ds(8 * which, 8)] = ref[...]
    small_x = [(k, send(first_small, got.at[k - 1], at.at_x(k))) for k in (1, 3, 2)]
    for copy in halves:
        copy.wait()

    def add_core(cols):
        for layer in range(2):
            for which, size, place in parts:
                landed(core[cols is right_cols, layer, which], chip.at[layer, pl.ds(place, size), cols])

        def body(i, carry):
            here = rows(i * 128, 128)
            for layer in range(2):
                chip[layer, here, cols] = (
                    chip[layer, here, cols].astype(f32) + own_half[layer, here, cols].astype(f32)
                ).astype(bf16)
            return carry

        lax.fori_loop(0, 9, body, 0)

    add_core(left_cols)
    a_y = RingSum(
        copies, y, at.at_y(1), at.at_y(3),
        lambda j, h: chip.at[j // 2, rows(576 * (j % 2) + 288 * h, 288), left_cols],
        [a_bufs.at[0], a_bufs.at[1]], [a_bufs.at[2], a_bufs.at[3]], [a_bufs.at[4], a_bufs.at[5]],
    )
    a_y.start()
    add_core(right_cols)
    b_z = RingSum(
        copies, z, at.at_z(1), at.at_z(3),
        lambda j, h: chip.at[h, rows(288 * j, 288), right_cols],
        [b_bufs.at[0], b_bufs.at[1]], [b_bufs.at[2], b_bufs.at[3]], [b_bufs.at[4], b_bufs.at[5]],
    )
    b_z.start()

    for ring in last:
        ring.relay()
    for n, ring in enumerate(last):
        ring.finish(lambda h, n=n: x_sum.at[n, h])
    for h in range(2):
        here = rows(256 * h + 64 * x, 64)
        value = grad[here] + norm_back(x_sum[0, h], normed[here], inverse[here, 0:1])
        slices[0, h] = value.astype(bf16)
        slices[1, h] = (middle[here] + (x_sum[1, h] + params[1, 8:9])).astype(bf16)
    home = []
    for k in (1, 3, 2):
        j = (y + k) % 4
        home.append((k, send(slices.at[j // 2, j % 2], back.at[y, quarter], at.at_y(k))))
    own = pltpu.make_async_copy(slices.at[y // 2, y % 2], back.at[y, quarter], local_sem)
    own.start()
    for k, index in small_x:
        landed(index, got.at[k - 1])
    of_norms = lax.broadcasted_iota(jnp.int32, first_small.shape, 1) % 8 < 2
    others = got[0] + got[1] + got[2]
    small_out[...] = first_small[...] + jnp.where(of_norms, others, 0.0)
    small_z = [(k, send(small_out, got.at[2 + k], at.at_z(k))) for k in (1, 3, 2)]

    a_y.relay()
    b_z.relay()
    own.wait()
    for k, index in home:
        landed(index, back.at[(y + 4 - k) % 4, quarter])
    outer = RingGather(
        copies, x, at.at_x(1), at.at_x(3),
        lambda j: back.at[:, rows(64 * j, 64)],
        lambda j, h: back.at[pl.ds(2 * h, 2), rows(64 * j, 64)],
    )
    outer.start()
    a_y.finish(lambda h: a_one.at[pl.ds(288 * h, 288)])

    def uneven(ref, start, h):
        return ref.at[rows(start + 80 * h, 80 - 16 * h)]

    a_rows = 1152 * c + 576 * low
    a_z = RingSum(
        copies, z, at.at_z(1), at.at_z(3),
        lambda j, h: uneven(a_one, 144 * j, h),
        [a_tail.at[0], a_tail2.at[0]], [a_tail.at[1], a_tail2.at[1]], [a_tail.at[2], a_tail2.at[2]],
    )
    a_z.start()
    b_z.finish(lambda h: b_one.at[h])
    b_rows = 1152 * c + 288 * z
    b_y = RingSum(
        copies, y, at.at_y(1), at.at_y(3),
        lambda j, h: b_one.at[j // 2, rows(144 * (j % 2) + 80 * h, 80 - 16 * h)],
        [b_tail.at[0], b_tail2.at[0]], [b_tail.at[1], b_tail2.at[1]], [b_tail.at[2], b_tail2.at[2]],
    )
    b_y.start()

    for k, index in small_z:
        landed(index, got.at[2 + k])
    for k, index in small_z:
        copies.started[index].wait_send()
    small_out[...] = small_out[...] + (got[3] + got[4] + got[5])
    small_y = [(k, send(small_out, got.at[5 + k], at.at_y(k))) for k in (1, 3, 2)]

    a_z.relay()
    b_y.relay()
    outer.relay()
    a_out, b_out = out.at[:, left_cols], out.at[:, right_cols]
    a_z.finish(lambda h: uneven(a_out, a_rows + 144 * z, h))
    a_gather = RingGather(
        copies, z, at.at_z(1), at.at_z(3),
        lambda j: a_out.at[rows(a_rows + 144 * j, 144)],
        lambda j, h: uneven(a_out, a_rows + 144 * j, h),
    )
    a_gather.start()
    b_y.finish(lambda h: uneven(b_out, b_rows + 144 * low, h))
    view = b_out.at[rows(b_rows + 144 * low, 144)]
    b_beside = send(view, view, at.beside())

    for k, index in small_y:
        landed(index, got.at[5 + k])
    for k, index in small_y:
        copies.started[index].wait_send()
    small_out[...] = small_out[...] + (got[6] + got[7] + got[8])
    small_c = send(small_out, got.at[9], at.sibling())

    landed(b_beside, b_out.at[rows(b_rows + 144 * (1 - low), 144)])
    b_gather = RingGather(
        copies, z, at.at_z(1), at.at_z(3),
        lambda j: b_out.at[rows(1152 * c + 288 * j, 288)],
        lambda j, h: b_out.at[rows(1152 * c + 288 * j + 144 * h, 144)],
    )
    b_gather.start()
    a_gather.relay()
    a_gather.finish()
    view = a_out.at[rows(a_rows, 576)]
    a_beside = send(view, view, at.beside())
    a_half = send(view, view, at.sibling())
    b_gather.relay()
    landed(small_c, got.at[9])
    copies.started[small_c].wait_send()
    small_out[...] = small_out[...] + got[9]
    outer.finish()
    landed(a_beside, a_out.at[rows(1152 * c + 576 * (1 - low), 576)])
    view = a_out.at[rows(1152 * c + 576 * (1 - low), 576)]
    a_other = send(view, view, at.sibling())
    b_gather.finish()
    view = b_out.at[mine]
    b_all = send(view, view, at.sibling())
    landed(a_half, a_out.at[rows(1152 * (1 - c) + 576 * low, 576)])
    landed(a_other, a_out.at[rows(1152 * (1 - c) + 576 * (1 - low), 576)])
    landed(b_all, b_out.at[theirs])
    waited = {index for _, index in small_z} | {index for _, index in small_y} | {small_c}
    for index, copy in enumerate(copies.started):
        if index not in waited:
            copy.wait_send()


FINAL_COPIES = 80


def final(grads, small, last):
    vmem = pl.BlockSpec(memory_space=pltpu.VMEM)
    return pl.pallas_call(
        final_kernel,
        out_shape=[
            jax.ShapeDtypeStruct((GRAD_ROWS, WIDTH), bf16),
            jax.ShapeDtypeStruct((2, 16, WIDTH), f32),
            jax.ShapeDtypeStruct((4, BLOCK, WIDTH), bf16),
        ],
        in_specs=[pl.BlockSpec(memory_space=pl.ANY)] * 4 + [vmem] * 11,
        out_specs=[vmem] * 3,
        scratch_shapes=[
            pltpu.VMEM((2, 1152, WIDTH), bf16),
            pltpu.VMEM((2, 1152, WIDTH), bf16),
            pltpu.VMEM((576, 384), bf16),
            pltpu.VMEM((2, 288, 384), bf16),
            pltpu.VMEM((6, 288, 384), bf16),
            pltpu.VMEM((6, 288, 384), bf16),
            pltpu.VMEM((3, 80, 384), bf16),
            pltpu.VMEM((3, 64, 384), bf16),
            pltpu.VMEM((3, 80, 384), bf16),
            pltpu.VMEM((3, 64, 384), bf16),
            pltpu.VMEM((10, 2, 16, WIDTH), f32),
            pltpu.VMEM((2, 16, WIDTH), f32),
            pltpu.VMEM((2, 6, 64, WIDTH), bf16),
            pltpu.VMEM((2, 2, 64, WIDTH), f32),
            pltpu.VMEM((2, 2, 64, WIDTH), bf16),
            pltpu.SemaphoreType.DMA((FINAL_COPIES,)),
            pltpu.SemaphoreType.DMA((FINAL_COPIES,)),
            pltpu.SemaphoreType.DMA,
            pltpu.SemaphoreType.DMA((4,)),
        ],
        compiler_params=pltpu.CompilerParams(
            collective_id=3, has_side_effects=True, vmem_limit_bytes=VMEM_LIMIT
        ),
        name="final",
    )(*grads, *small, *last)


def nn(a, b):
    return lax.dot_general(a, b, (((1,), (0,)), ((), ())), preferred_element_type=f32)


def nt(a, b):
    return lax.dot_general(a, b, (((1,), (1,)), ((), ())), preferred_element_type=f32)


def tn(a, b):
    return lax.dot_general(a, b, (((0,), (0,)), ((), ())), preferred_element_type=f32)


def turner():
    c = lax.broadcasted_iota(jnp.int32, (INNER, INNER), 0)
    r = lax.broadcasted_iota(jnp.int32, (INNER, INNER), 1)
    lane = c % HEAD_DIM
    half = ROT // 2
    minus = (lane < half) & (r == c + half)
    plus = (lane >= half) & (lane < ROT) & (r == c - half)
    return jnp.where(plus, 1.0, jnp.where(minus, -1.0, 0.0)).astype(bf16)


def head_lanes(shape, h):
    lane = lax.broadcasted_iota(jnp.int32, shape, len(shape) - 1)
    return (lane >= h * HEAD_DIM) & (lane < (h + 1) * HEAD_DIM)


def pick(value, h):
    return jnp.where(head_lanes(value.shape, h), value, jnp.zeros_like(value))


def chunk_rows(i):
    return pl.ds(pl.multiple_of(i * BLOCK, BLOCK), BLOCK)


def front_kernel(later, *refs):
    if later:
        x_ref, add_ref, wq, small, cos, sin, x_out, n_out, inv_out, first_out, second_out, q_out, kv_out, wt = refs
    else:
        x_ref, wq, small, cos, sin, n_out, inv_out, first_out, second_out, q_out, kv_out, wt = refs
    turn = turner()
    for i in range(2):
        wt[INNER * i : INNER * (i + 1)] = nn(turn, wq[0, INNER * i : INNER * (i + 1)]).astype(bf16)

    def row(i, wide=WIDTH):
        return small[0, i : i + 1, :wide]

    def body(i, carry):
        here = chunk_rows(i)
        if later:
            x = x_ref[here] + (add_ref[here].astype(f32) + row(8))
            x_out[here] = x
        else:
            x = x_ref[0, i].astype(f32)
        centred = x - jnp.mean(x, axis=-1, keepdims=True)
        inverse = lax.rsqrt(jnp.mean(centred * centred, axis=-1, keepdims=True) + EPS)
        normed = centred * inverse
        n_out[here] = normed
        inv_out[here] = jnp.broadcast_to(inverse, (BLOCK, 128))
        first = (normed * row(0) + row(1)).astype(bf16)
        first_out[here] = first
        second_out[here] = (normed * row(2) + row(3)).astype(bf16)
        cosine, sine = cos[here], sin[here]
        query = (nt(first, wq[0, :INNER]) + row(4, INNER)) * cosine
        query = query + (nt(first, wt[:INNER]) + row(9, INNER)) * sine
        q_out[here] = (query * HEAD_DIM ** (-0.5)).astype(bf16)
        key = (nt(first, wq[0, INNER : 2 * INNER]) + row(5, INNER)) * cosine
        key = key + (nt(first, wt[INNER:]) + row(10, INNER)) * sine
        kv_out[0, here] = key.astype(bf16)
        kv_out[1, here] = (nt(first, wq[0, 2 * INNER :]) + row(6, INNER)).astype(bf16)
        return carry

    lax.fori_loop(0, 2, body, 0)


def feed_kernel(second, up, small, active_out, slope_out):
    def body(i, carry):
        here = pl.ds(pl.multiple_of(i * 128, 128), 128)
        hidden = nn(second[here], up[0]) + small[0, 7:8]
        below = 0.5 + 0.5 * lax.erf(hidden * (0.5**0.5))
        active_out[here] = (hidden * below).astype(bf16)
        density = jnp.exp(-0.5 * hidden * hidden) * 0.3989422804014327
        slope_out[here] = (below + hidden * density).astype(bf16)
        return carry

    lax.fori_loop(0, 4, body, 0)


def gather_keys(own, other, keys, values):
    for n, ref in enumerate((keys, values)):
        ref[0:BLOCK] = own[n, 0:BLOCK]
        ref[BLOCK : 2 * BLOCK] = other[n, 0:BLOCK]
        ref[2 * BLOCK : 3 * BLOCK] = own[n, BLOCK : 2 * BLOCK]
        ref[3 * BLOCK : 4 * BLOCK] = other[n, BLOCK : 2 * BLOCK]


def key_places(c, shape, dim, blocks):
    i = lax.broadcasted_iota(jnp.int32, shape, dim)
    place = jnp.where(i < BLOCK, i + BLOCK * c, i - BLOCK * c)
    if blocks == 4:
        late = jnp.where(i < 3 * BLOCK, i + BLOCK * c, i - BLOCK * c)
        place = jnp.where(i < 2 * BLOCK, place, late)
    return place


SPANS = ((0, 2), (1, 4))


def mix_kernel(q, own, other, active, dense, down, starts, part_out, mixed_out, log_out, keys, values, logs, bias):
    c = lax.axis_index("dp") % 2
    gather_keys(own, other, keys, values)
    logs[...] = jnp.zeros_like(logs)
    for block, span in SPANS:
        here, n = pl.ds(block * BLOCK, BLOCK), span * BLOCK
        place = key_places(c, (BLOCK, n), 1, span)
        mine = lax.broadcasted_iota(jnp.int32, (BLOCK, n), 0) + (2 * block + c) * BLOCK
        allowed = (place <= mine) & (place >= starts[here])
        bias[:, :n] = jnp.where(allowed, 0.0, MASKED)
        query = q[here]
        mixed = jnp.zeros((BLOCK, INNER), f32)
        for h in range(HEADS):
            score = nt(pick(query, h), keys[:n]) + bias[:, :n]
            top = jnp.max(score, axis=-1, keepdims=True)
            expo = jnp.exp(score - top)
            total = jnp.sum(expo, axis=-1, keepdims=True)
            logs[here, h : h + 1] = top + jnp.log(total)
            mixed = mixed + pick(nn(expo.astype(bf16), values[:n]) * (1.0 / total), h)
        mixed = mixed.astype(bf16)
        mixed_out[here] = mixed
        part = nn(mixed, dense[0]) + nn(active[here], down[0])
        part_out[block] = part.astype(bf16)
    log_out[...] = logs[...].T


def back_mix_kernel(later, *refs):
    if later:
        (g_ref, q, own, other, mixed, log, dense, starts, dq_out, own_out, other_out,
         keys, values, inner, bias, dkeys, dvalues) = refs
        grad_ref = g_ref
    else:
        (g_ref, add_ref, n_ref, inv_ref, q, own, other, mixed, log, dense, starts, dq_out, own_out, other_out,
         grad_out, grad_ref, keys, values, inner, bias, dkeys, dvalues) = refs

        def body(i, carry):
            here = chunk_rows(i)
            grad = g_ref[0, i].astype(f32) + norm_back(add_ref[here].astype(f32), n_ref[here], inv_ref[here, 0:1])
            grad_out[here] = grad
            grad_ref[here] = grad.astype(bf16)
            return carry

        lax.fori_loop(0, 2, body, 0)
    c = lax.axis_index("dp") % 2
    gather_keys(own, other, keys, values)
    inner[...] = jnp.zeros_like(inner)
    for block, span in reversed(SPANS):
        here, n = pl.ds(block * BLOCK, BLOCK), span * BLOCK
        place = key_places(c, (n, BLOCK), 0, span)
        mine = lax.broadcasted_iota(jnp.int32, (n, BLOCK), 1) + (2 * block + c) * BLOCK
        allowed = (place <= mine) & (place >= starts[0:1, here])
        bias[:n] = jnp.where(allowed, 0.0, MASKED)
        grad = grad_ref[0, block] if later else grad_ref[here]
        d_mixed = nt(grad, dense[0]).astype(bf16)
        product = d_mixed.astype(f32) * mixed[here].astype(f32)
        for h in range(HEADS):
            inner[:, h : h + 1] = jnp.sum(pick(product, h), axis=-1, keepdims=True)
        inner_rows = inner[...].T
        query = q[here]
        d_query = jnp.zeros((BLOCK, INNER), f32)
        for h in range(HEADS):
            mine_q, mine_d = pick(query, h), pick(d_mixed, h)
            prob = jnp.exp(nt(keys[:n], mine_q) + bias[:n] - log[h : h + 1, here])
            d_prob = nt(values[:n], mine_d)
            d_score = (prob * (d_prob - inner_rows[h : h + 1])).astype(bf16)
            d_value = nn(prob.astype(bf16), mine_d)
            d_key = nn(d_score, mine_q)
            if span == 4 and h == 0:
                dvalues[...] = d_value
                dkeys[...] = d_key
            else:
                dvalues[:n] += d_value
                dkeys[:n] += d_key
            d_query = d_query + pick(tn(d_score, keys[:n]), h)
        dq_out[here] = d_query * HEAD_DIM ** (-0.5)
    for n, ref in enumerate((dkeys, dvalues)):
        own_out[n, 0:BLOCK] = ref[0:BLOCK]
        other_out[n, 0:BLOCK] = ref[BLOCK : 2 * BLOCK].astype(bf16)
        own_out[n, BLOCK : 2 * BLOCK] = ref[2 * BLOCK : 3 * BLOCK]
        other_out[n, BLOCK : 2 * BLOCK] = ref[3 * BLOCK : 4 * BLOCK].astype(bf16)


def back_feed_kernel(later, grad, down, up, small, slope, second, active, mixed, normed, e_out, grads_out, sums_out, hid):
    sums_out[...] = jnp.zeros_like(sums_out)

    def body(i, carry):
        here = chunk_rows(i)
        g = grad[0, i] if later else grad[here]
        d_hidden = (nt(g, down[0]) * slope[here].astype(f32)).astype(bf16)
        hid[here] = d_hidden
        d_second = nt(d_hidden, up[0])
        e_out[here] = d_second * small[0, 2:3]
        sums_out[0:1] += jnp.sum(d_second * normed[here], axis=0, keepdims=True)
        sums_out[1:2] += jnp.sum(d_second, axis=0, keepdims=True)
        sums_out[2:3] += jnp.sum(g.astype(f32), axis=0, keepdims=True)
        sums_out[3:4] += jnp.sum(d_hidden.astype(f32), axis=0, keepdims=True)
        return carry

    lax.fori_loop(0, 2, body, 0)
    g = grad[0].reshape(2 * BLOCK, WIDTH) if later else grad[...]
    grads_out[:INNER] = tn(mixed[...], g).astype(bf16)
    grads_out[INNER : INNER + WIDTH] = tn(second[...], hid[...]).astype(bf16)
    grads_out[INNER + WIDTH :] = tn(active[...], g).astype(bf16)


def back_front_kernel(d_query, own, got, cos, sin, wq, small, first, normed, e_in, e_out, grads_out, sums_out, packed):
    sums_out[...] = jnp.zeros_like(sums_out)
    turn = turner()

    def unrotate(value, cosine, sine):
        moved = value * sine
        high = moved.astype(bf16)
        low = (moved - high.astype(f32)).astype(bf16)
        return value * cosine + (nn(high, turn) + nn(low, turn))

    def body(i, carry):
        here = chunk_rows(i)
        cosine, sine = cos[here], sin[here]
        parts = [
            unrotate(d_query[here], cosine, sine),
            unrotate(own[0, here] + got[0, here].astype(f32), cosine, sine),
            own[1, here] + got[1, here].astype(f32),
        ]
        d_first = jnp.zeros((BLOCK, WIDTH), f32)
        for n, part in enumerate(parts):
            part = part.astype(bf16)
            packed[n, here] = part
            d_first = d_first + nn(part, wq[0, INNER * n : INNER * (n + 1)])
            sums_out[2 + n : 3 + n, :INNER] += jnp.sum(part.astype(f32), axis=0, keepdims=True)
        e_out[i] = (d_first * small[0, 0:1] + e_in[here]).astype(bf16)
        sums_out[0:1] += jnp.sum(d_first * normed[here], axis=0, keepdims=True)
        sums_out[1:2] += jnp.sum(d_first, axis=0, keepdims=True)
        return carry

    lax.fori_loop(0, 2, body, 0)
    for n in range(3):
        grads_out[INNER * n : INNER * (n + 1)] = tn(packed[n], first[...]).astype(bf16)


ROWS = 2 * BLOCK


def shape_of(*dims, dtype=f32):
    return jax.ShapeDtypeStruct(dims, dtype)


def at_layer(layer, *dims):
    return pl.BlockSpec((1,) + dims, lambda i: (layer,) + (0,) * len(dims))


def on_device(kernel, name, args, specs, outs, scratch):
    whole = pl.BlockSpec(memory_space=pltpu.VMEM)
    return pl.pallas_call(
        kernel,
        grid=(1,),
        out_shape=outs,
        in_specs=[whole if spec is None else spec for spec in specs],
        out_specs=[whole] * len(outs),
        scratch_shapes=scratch,
        compiler_params=pltpu.CompilerParams(vmem_limit_bytes=VMEM_LIMIT),
        name=name,
    )(*args)


def norm_back(scaled, normed, inverse):
    inner = scaled - jnp.mean(scaled, axis=-1, keepdims=True)
    inner = inner - normed * jnp.mean(scaled * normed, axis=-1, keepdims=True)
    return inner * inverse


def swapped(value):
    return lax.ppermute(value, "dp", [(n, n ^ 1) for n in range(16)])


def forward_layer(layer, x, add, stacks, tables):
    wq, wd, wu, wn, small = stacks
    cosine, sine, start_col, start_row = tables
    later = add is not None
    small_spec = at_layer(layer, 16, WIDTH)
    args, specs = ([x, add], [None, None]) if later else ([x], [at_layer(0, 2, BLOCK, WIDTH)])
    outs = [
        shape_of(ROWS, WIDTH), shape_of(ROWS, 128), shape_of(ROWS, WIDTH, dtype=bf16),
        shape_of(ROWS, WIDTH, dtype=bf16), shape_of(ROWS, INNER, dtype=bf16), shape_of(2, ROWS, INNER, dtype=bf16),
    ]
    if later:
        outs = [shape_of(ROWS, WIDTH)] + outs
    got = on_device(
        functools.partial(front_kernel, later), "front",
        args + [wq, small, cosine, sine], specs + [at_layer(layer, 3 * INNER, WIDTH), small_spec, None, None],
        outs, [pltpu.VMEM((2 * INNER, WIDTH), bf16)],
    )
    flat = got[0] if later else None
    normed, inverse, first, second, query, own = got[-6:]
    other = swapped(own)
    active, slope = on_device(
        feed_kernel, "feed", [second, wu, small], [None, at_layer(layer, WIDTH, WIDTH), small_spec],
        [shape_of(ROWS, WIDTH, dtype=bf16)] * 2, [],
    )
    part, mixed, log = on_device(
        mix_kernel, "mix", [query, own, other, active, wd, wn, start_col],
        [None] * 4 + [at_layer(layer, INNER, WIDTH), at_layer(layer, WIDTH, WIDTH), None],
        [shape_of(2, BLOCK, WIDTH, dtype=bf16), shape_of(ROWS, INNER, dtype=bf16), shape_of(128, ROWS)],
        [pltpu.VMEM((SEQ, INNER), bf16)] * 2 + [pltpu.VMEM((ROWS, 128), f32), pltpu.VMEM((BLOCK, SEQ), f32)],
    )
    return flat, part, (normed, inverse, first, second, query, own, other, active, slope, mixed, log)


def backward_layer(layer, xg, extra, stacks, tables, kept):
    wq, wd, wu, wn, small = stacks
    cosine, sine, start_col, start_row = tables
    normed, inverse, first, second, query, own, other, active, slope, mixed, log = kept
    later = extra is None
    small_spec = at_layer(layer, 16, WIDTH)
    grad_spec = at_layer(1, 2, BLOCK, WIDTH)
    args, specs = [xg], [grad_spec]
    outs = [shape_of(ROWS, INNER), shape_of(2, ROWS, INNER), shape_of(2, ROWS, INNER, dtype=bf16)]
    if not later:
        args, specs = args + list(extra), specs + [None] * 3
        outs = outs + [shape_of(ROWS, WIDTH), shape_of(ROWS, WIDTH, dtype=bf16)]
    got = on_device(
        functools.partial(back_mix_kernel, later), "back_mix",
        args + [query, own, other, mixed, log, wd, start_row],
        specs + [None] * 5 + [at_layer(layer, INNER, WIDTH), None],
        outs,
        [pltpu.VMEM((SEQ, INNER), bf16)] * 2
        + [pltpu.VMEM((BLOCK, 128), f32), pltpu.VMEM((SEQ, BLOCK), f32)]
        + [pltpu.VMEM((SEQ, INNER), f32)] * 2,
    )
    d_query, d_own, d_other = got[:3]
    grad, low, low_spec = (None, xg, grad_spec) if later else (got[3], got[4], None)
    arrived = swapped(d_other)
    e_two, grads_two, sums_two = on_device(
        functools.partial(back_feed_kernel, later), "back_feed",
        [low, wn, wu, small, slope, second, active, mixed, normed],
        [low_spec, at_layer(layer, WIDTH, WIDTH), at_layer(layer, WIDTH, WIDTH), small_spec] + [None] * 5,
        [shape_of(ROWS, WIDTH), shape_of(INNER + 2 * WIDTH, WIDTH, dtype=bf16), shape_of(8, WIDTH)],
        [pltpu.VMEM((ROWS, WIDTH), bf16)],
    )
    e, grads_one, sums_one = on_device(
        back_front_kernel, "back_front",
        [d_query, d_own, arrived, cosine, sine, wq, small, first, normed, e_two],
        [None] * 5 + [at_layer(layer, 3 * INNER, WIDTH), small_spec] + [None] * 3,
        [shape_of(2, BLOCK, WIDTH, dtype=bf16), shape_of(3 * INNER, WIDTH, dtype=bf16), shape_of(8, WIDTH)],
        [pltpu.VMEM((3, ROWS, INNER), bf16)],
    )
    return grad, e, grads_one, grads_two, sums_one, sums_two


def tables_of(segment_ids):
    at = Place()
    seq = lax.dynamic_slice(segment_ids, (at.y, at.z, 0), (1, 1, SEQ))[0, 0]
    blocks = seq.reshape(2, 2, BLOCK)
    mine = lax.dynamic_index_in_dim(blocks, at.c, 1, keepdims=False).reshape(ROWS)
    start = jnp.sum((seq[None, :] < mine[:, None]).astype(jnp.int32), axis=1)
    i = jnp.arange(ROWS, dtype=jnp.int32)
    place = i + BLOCK * (i // BLOCK + at.c) - start
    half = ROT // 2
    freqs = 10000.0 ** (-(2.0 * jnp.arange(half, dtype=f32)) / ROT)
    angles = place.astype(f32)[:, None] * freqs
    cosine, sine = jnp.cos(angles), jnp.sin(angles)
    rest = HEAD_DIM - ROT
    cosine = jnp.concatenate([cosine, cosine, jnp.ones((ROWS, rest), f32)], axis=1)
    sine = jnp.concatenate([sine, sine, jnp.zeros((ROWS, rest), f32)], axis=1)
    return jnp.tile(cosine, (1, HEADS)), jnp.tile(sine, (1, HEADS)), start[:, None], start[None, :]


def by_kind(value):
    return value.reshape(value.shape[0], HEADS, 3, HEAD_DIM).transpose(2, 1, 3, 0).reshape(3 * INNER, -1)


def local(
    boundary,
    segment_ids,
    attn_gain,
    attn_shift,
    mlp_gain,
    mlp_shift,
    qkv_weight,
    qkv_bias,
    dense_weight,
    dense_bias,
    up_weight,
    up_bias,
    down_weight,
    down_bias,
):
    bias = qkv_bias.reshape(HEADS, 3, HEAD_DIM).transpose(1, 0, 2)
    half = ROT // 2
    turned = jnp.concatenate(
        [-bias[:2, :, half:ROT], bias[:2, :, :half], jnp.zeros((2, HEADS, HEAD_DIM - ROT), f32)], axis=2
    )
    bias = jnp.concatenate([bias, turned]).reshape(5, INNER)
    bias = jnp.pad(bias, ((0, 0), (0, WIDTH - INNER)))
    small = jnp.concatenate(
        [
            attn_gain, attn_shift, mlp_gain, mlp_shift, bias[:3], up_bias, dense_bias + down_bias, bias[3:],
            jnp.zeros((5, WIDTH), f32),
        ]
    )
    xg, *stacks = spread(
        boundary[0].astype(bf16), by_kind(qkv_weight[0]), dense_weight[0], up_weight[0], down_weight[0], small
    )
    tables = tables_of(segment_ids)
    _, part_zero, kept_zero = forward_layer(0, xg, None, stacks, tables)
    branch = total_over_tensor(part_zero).reshape(ROWS, WIDTH)
    flat = xg[0].reshape(ROWS, WIDTH).astype(f32)
    small_one = stacks[4]
    small_one = small_one.at[1, 8].set(stacks[4][0, 8])
    middle, part_one, kept_one = forward_layer(1, flat, branch, stacks[:4] + [small_one], tables)

    _, e_one, grads_one, grads_two, sums_one, sums_two = backward_layer(1, xg, None, stacks, tables, kept_one)
    e_one = total_over_tensor(e_one).reshape(ROWS, WIDTH)
    grad, e_zero, grads_three, grads_four, sums_three, sums_four = backward_layer(
        0, xg, (e_one, kept_one[0], kept_one[1]), stacks, tables, kept_zero
    )
    total, small_total, back = final(
        [grads_three, grads_four, grads_one, grads_two],
        [sums_three, sums_four, sums_one, sums_two],
        [e_zero, part_one, grad, kept_zero[0], kept_zero[1], middle, stacks[4]],
    )
    mine = lax.dynamic_index_in_dim(small_total, lax.axis_index("pipe"), 0, keepdims=False)
    total = total.astype(f32).reshape(2, GRAD_ROWS // 2, WIDTH)
    d_qkv = jnp.concatenate([total[0, :288], total[1, :288]])
    d_qkv = d_qkv.reshape(3, HEADS, HEAD_DIM, WIDTH).transpose(3, 1, 0, 2).reshape(1, WIDTH, 3 * INNER)
    d_bias = mine[2:5, :INNER].reshape(3, HEADS, HEAD_DIM).transpose(1, 0, 2).reshape(1, 3 * INNER)
    d_up = jnp.concatenate([total[0, 480:], total[1, 288:384]])
    return (
        back.astype(f32)[None],
        mine[0:1],
        mine[1:2],
        mine[8:9],
        mine[9:10],
        d_qkv,
        d_bias,
        total[0, 288:480][None],
        mine[10:11],
        d_up[None],
        mine[11:12],
        total[1, 384:][None],
        mine[10:11],
    )


def solution(mesh):
    in_specs = (
        P("pipe", None, "dp", None),
        P(),
        P("pipe", None),
        P("pipe", None),
        P("pipe", None),
        P("pipe", None),
        P("pipe", None, "tensor"),
        P("pipe", "tensor"),
        P("pipe", "tensor", None),
        P("pipe", None),
        P("pipe", None, "tensor"),
        P("pipe", "tensor"),
        P("pipe", "tensor", None),
        P("pipe", None),
    )
    out_specs = (
        P("pipe", None, "dp", None),
        P("pipe", None),
        P("pipe", None),
        P("pipe", None),
        P("pipe", None),
        P("pipe", None, "tensor"),
        P("pipe", "tensor"),
        P("pipe", "tensor", None),
        P("pipe", None),
        P("pipe", None, "tensor"),
        P("pipe", "tensor"),
        P("pipe", "tensor", None),
        P("pipe", None),
    )
    return jax.shard_map(local, mesh=mesh, in_specs=in_specs, out_specs=out_specs, check_vma=False)
```

```python
import functools
import types

import jax
import jax.numpy as jnp
from jax import lax
from jax.experimental import pallas as pl
from jax.experimental.pallas import tpu as pltpu
from jax.sharding import PartitionSpec as P

MESH = pl.DeviceIdType.MESH
HEAD_DIM = 64
ROT = 16
EPS = 1e-05
MASKED = -1e30
WIDTH = 768
SEQ = 1024
BLOCK = 256
HEADS = 3
INNER = HEADS * HEAD_DIM
GRAD_ROWS = 2304
bf16 = jnp.bfloat16
f32 = jnp.float32
VMEM_LIMIT = 56 * 1024 * 1024


class Place:
    def __init__(self):
        self.p = lax.axis_index("pipe")
        self.d = lax.axis_index("dp")
        self.x = lax.axis_index("tensor")
        self.z = self.d // 4
        self.low = (self.d // 2) % 2
        self.c = self.d % 2
        self.y = 2 * self.p + self.low

    def at_x(self, steps):
        return (self.p, self.d, (self.x + steps) % 4)

    def at_y(self, steps):
        y = (self.y + steps) % 4
        return (y // 2, self.z * 4 + (y % 2) * 2 + self.c, self.x)

    def at_z(self, steps):
        return (self.p, ((self.z + steps) % 4) * 4 + self.d % 4, self.x)

    def sibling(self):
        return (self.p, self.d + 1 - 2 * self.c, self.x)

    def partner(self):
        return (1 - self.p, self.z * 4 + (1 - self.low) * 2 + self.c, self.x)

    def beside(self):
        return (self.p, self.z * 4 + (1 - self.low) * 2 + self.c, self.x)


def greet(devices):
    barrier = pltpu.get_barrier_semaphore()
    for device in devices:
        pl.semaphore_signal(barrier, inc=1, device_id=device, device_id_type=MESH)
    pl.semaphore_wait(barrier, len(devices))


class Copies:
    def __init__(self, send_sems, recv_sems, somebody):
        self.send_sems, self.recv_sems = send_sems, recv_sems
        self.somebody = somebody
        self.count = 0
        self.started = []

    def send(self, src, dst, device):
        k = self.count
        self.count += 1
        copy = pltpu.make_async_remote_copy(
            src_ref=src,
            dst_ref=dst,
            send_sem=self.send_sems.at[k],
            recv_sem=self.recv_sems.at[k],
            device_id=device,
            device_id_type=MESH,
        )
        copy.start()
        self.started.append(copy)
        return k

    def landed(self, k, dst):
        pltpu.make_async_remote_copy(
            src_ref=dst,
            dst_ref=dst,
            send_sem=self.send_sems.at[k],
            recv_sem=self.recv_sems.at[k],
            device_id=self.somebody,
            device_id_type=MESH,
        ).wait_recv()

    def drain(self):
        for copy in self.started:
            copy.wait_send()


class RingSum:
    def __init__(self, copies, me, right, left, chunk, relay, direct, final):
        self.copies, self.me, self.right, self.left = copies, me, right, left
        self.chunk, self.relay_in, self.direct, self.final = chunk, relay, direct, final

    def start(self):
        me, send = self.me, self.copies.send
        far, after, before = (me + 2) % 4, (me + 1) % 4, (me + 3) % 4
        self.k = [
            send(self.chunk(far, 0), self.relay_in[0], self.right),
            send(self.chunk(far, 1), self.relay_in[1], self.left),
            send(self.chunk(after, 1), self.direct[1], self.right),
            send(self.chunk(before, 0), self.direct[0], self.left),
        ]

    def relay(self):
        me, copies = self.me, self.copies
        after, before = (me + 1) % 4, (me + 3) % 4
        copies.landed(self.k[0], self.relay_in[0])
        add_into(self.relay_in[0], self.chunk(after, 0))
        k0 = copies.send(self.relay_in[0], self.final[0], self.right)
        copies.landed(self.k[1], self.relay_in[1])
        add_into(self.relay_in[1], self.chunk(before, 1))
        k1 = copies.send(self.relay_in[1], self.final[1], self.left)
        self.k += [k0, k1]

    def finish(self, out):
        copies = self.copies
        copies.landed(self.k[3], self.direct[0])
        copies.landed(self.k[4], self.final[0])
        store_sum(out(0), self.chunk(self.me, 0), self.direct[0], self.final[0])
        copies.landed(self.k[2], self.direct[1])
        copies.landed(self.k[5], self.final[1])
        store_sum(out(1), self.chunk(self.me, 1), self.direct[1], self.final[1])


class RingGather:
    def __init__(self, copies, me, right, left, piece, halves):
        self.copies, self.me, self.right, self.left = copies, me, right, left
        self.piece, self.halves = piece, halves

    def start(self):
        mine = self.piece(self.me)
        self.k = [
            self.copies.send(mine, mine, self.right),
            self.copies.send(mine, mine, self.left),
        ]

    def relay(self):
        before, after = (self.me + 3) % 4, (self.me + 1) % 4
        self.copies.landed(self.k[0], self.piece(before))
        view = self.halves(before, 0)
        k0 = self.copies.send(view, view, self.right)
        self.copies.landed(self.k[1], self.piece(after))
        view = self.halves(after, 1)
        k1 = self.copies.send(view, view, self.left)
        self.k += [k0, k1]

    def finish(self):
        far = (self.me + 2) % 4
        self.copies.landed(self.k[2], self.halves(far, 0))
        self.copies.landed(self.k[3], self.halves(far, 1))


class DirectSum:
    def __init__(self, copies, me, to, chunk, bufs):
        self.copies, self.me, self.to, self.chunk, self.bufs = copies, me, to, chunk, bufs

    def start(self):
        self.k = [
            self.copies.send(self.chunk((self.me + k) % 4), self.bufs[k - 1], self.to(k)) for k in (1, 3, 2)
        ]

    def finish(self, out):
        for index, k in zip(self.k, (1, 3, 2)):
            self.copies.landed(index, self.bufs[k - 1])
        store_sum(out, self.chunk(self.me), *self.bufs)


class DirectGather:
    def __init__(self, copies, me, to, piece):
        self.copies, self.me, self.to, self.piece = copies, me, to, piece

    def start(self):
        mine = self.piece(self.me)
        self.k = [self.copies.send(mine, mine, self.to(k)) for k in (1, 3, 2)]

    def finish(self):
        for index, k in zip(self.k, (1, 3, 2)):
            self.copies.landed(index, self.piece((self.me + 4 - k) % 4))


def add_into(ref, other):
    ref[...] = (ref[...].astype(f32) + other[...].astype(f32)).astype(ref.dtype)


def store_sum(out, *parts):
    total = parts[0][...].astype(f32)
    for part in parts[1:]:
        total = total + part[...].astype(f32)
    out[...] = total.astype(out.dtype)


def rows(start, size, step=16):
    return pl.ds(pl.multiple_of(start, step), size)


def spread_kernel(
    block, wq, wd, wu, wn, small, xg, oq, od, ou, on, osm,
    hold_x, hold_s, hold_q, hold_d, hold_u, hold_n, send_sems, recv_sems, local_sems,
):
    at = Place()
    p, x, y, z, c = at.p, at.x, at.y, at.z, at.c
    greet(
        [at.at_x(1), at.at_x(3), at.at_y(1), at.at_y(2), at.at_y(3), at.at_z(1), at.at_z(3), at.sibling()]
    )
    copies = Copies(send_sems, recv_sems, at.at_x(1))
    weights = [(wq, oq), (wd, od), (wu, ou), (wn, on)]

    def piece(ref, zz, cc):
        if ref.shape[-2] == WIDTH:
            return ref.at[rows(192 * zz + 96 * cc, 96)]
        each = ref.shape[-2] // 4
        return ref.at[rows(each * zz, each), pl.ds(pl.multiple_of(384 * cc, 128), 384)]

    def half(ref, zz, cc, h):
        if ref.shape[-2] == WIDTH:
            return ref.at[rows(192 * zz + 96 * cc + 48 * h, 48)]
        each = ref.shape[-2] // 4
        more = (each // 2 + 15) // 16 * 16
        size = each - more if h else more
        return ref.at[rows(each * zz + more * h, size), pl.ds(pl.multiple_of(384 * cc, 128), 384)]

    quarter = rows(64 * x, 64)
    first = [
        copies.send(block.at[(y + k) % 4, quarter], xg.at[p, at.low, quarter], at.at_y(k)) for k in (1, 3, 2)
    ]
    sent = [
        copies.send(piece(src, z, c), piece(dst.at[p], z, c), at.partner()) for src, dst in weights
    ]
    sent_small = copies.send(small, osm.at[p], at.partner())
    held = [hold_x, hold_s, hold_q, hold_d, hold_u, hold_n]
    kept = [(block.at[y], xg.at[p, at.low]), (small, osm.at[p])] + [(s, d.at[p]) for s, d in weights]
    inward = [
        pltpu.make_async_copy(src, hold, local_sems.at[n]) for n, ((src, _), hold) in enumerate(zip(kept, held))
    ]
    for copy in inward:
        copy.start()
    outward = []
    for n, ((_, dst), hold) in enumerate(zip(kept, held)):
        inward[n].wait()
        copy = pltpu.make_async_copy(hold, dst, local_sems.at[n + 6])
        copy.start()
        outward.append(copy)
    gathers = []
    for k, index in zip((1, 3, 2), first):
        source = (y + 4 - k) % 4
        slot = xg.at[source // 2, source % 2]
        copies.landed(index, slot.at[quarter])
        gather = RingGather(
            copies,
            x,
            at.at_x(1),
            at.at_x(3),
            lambda j, slot=slot: slot.at[rows(64 * j, 64)],
            lambda j, h, slot=slot: slot.at[rows(64 * j + 32 * h, 32)],
        )
        gather.start()
        gathers.append(gather)
    others = [dst.at[1 - p] for _, dst in weights]
    rings, shared = [], []
    for other, index in zip(others, sent):
        copies.landed(index, piece(other, z, c))
        ring = RingGather(
            copies,
            z,
            at.at_z(1),
            at.at_z(3),
            lambda j, other=other: piece(other, j, c),
            lambda j, h, other=other: half(other, j, c, h),
        )
        ring.start()
        rings.append(ring)
        mine = piece(other, z, c)
        shared.append((copies.send(mine, mine, at.sibling()), piece(other, z, 1 - c)))
    for gather in gathers:
        gather.relay()
    for other, ring in zip(others, rings):
        ring.relay()
        for j in ((z + 3) % 4, (z + 1) % 4):
            mine = piece(other, j, c)
            shared.append((copies.send(mine, mine, at.sibling()), piece(other, j, 1 - c)))
    for gather in gathers:
        gather.finish()
    for other, ring in zip(others, rings):
        ring.finish()
        j = (z + 2) % 4
        mine = piece(other, j, c)
        shared.append((copies.send(mine, mine, at.sibling()), piece(other, j, 1 - c)))
    copies.landed(sent_small, osm.at[1 - p])
    for index, view in shared:
        copies.landed(index, view)
    for copy in outward:
        copy.wait()
    copies.drain()


SPREAD_COPIES = 3 + 4 + 1 + 12 + 16 + 16


def spread(block, wq, wd, wu, wn, small):
    any_space = pl.BlockSpec(memory_space=pl.ANY)
    shapes = [(2, 2, BLOCK, WIDTH)] + [(2,) + w.shape for w in (wq, wd, wu, wn)]
    return pl.pallas_call(
        spread_kernel,
        out_shape=[jax.ShapeDtypeStruct(s, bf16) for s in shapes]
        + [jax.ShapeDtypeStruct((2,) + small.shape, f32)],
        in_specs=[any_space] * 6,
        out_specs=[any_space] * 6,
        scratch_shapes=[
            pltpu.VMEM((BLOCK, WIDTH), bf16),
            pltpu.VMEM(small.shape, f32),
        ]
        + [pltpu.VMEM(w.shape, bf16) for w in (wq, wd, wu, wn)]
        + [
            pltpu.SemaphoreType.DMA((SPREAD_COPIES,)),
            pltpu.SemaphoreType.DMA((SPREAD_COPIES,)),
            pltpu.SemaphoreType.DMA((12,)),
        ],
        compiler_params=pltpu.CompilerParams(
            collective_id=0, has_side_effects=True, vmem_limit_bytes=VMEM_LIMIT
        ),
        name="spread",
    )(block, wq, wd, wu, wn, small)


PAIRS = 3
LANES = 128


class Flow:
    def __init__(self, at, copies, chip, own_half, out, cols):
        self.at, self.copies, self.cols = at, copies, cols
        self.chip, self.own_half, self.out = chip.at[:, :, cols], own_half.at[:, :, cols], out.at[:, cols]
        self.base, self.other_base = 1152 * at.c, 1152 * (1 - at.c)

    def send_core(self, layers):
        self.core = []
        for layer in range(2):
            for which, size, place in PARTS:
                src = layers[layer][which].at[rows(size * (1 - self.at.c), size), self.cols]
                dst = self.chip.at[layer, pl.ds(place, size)]
                self.core.append((self.copies.send(src, dst, self.at.sibling()), dst))

    def add_core(self):
        for index, dst in self.core:
            self.copies.landed(index, dst)
        chip, own_half = self.chip, self.own_half

        def body(i, carry):
            here = rows(i * 192, 192)
            for layer in range(2):
                chip[layer, here] = (chip[layer, here].astype(f32) + own_half[layer, here].astype(f32)).astype(bf16)
            return carry

        lax.fori_loop(0, 6, body, 0)

    def to_sibling(self, start, size):
        view = self.out.at[rows(self.base + start, size)]
        index = self.copies.send(view, view, self.at.sibling())
        return index, start, size

    def from_sibling(self, sent):
        index, start, size = sent
        self.copies.landed(index, self.out.at[rows(self.other_base + start, size)])


class FlowYZ(Flow):
    def begin(self, bufs, one, tail):
        at, chip = self.at, self.chip
        self.add_core()
        self.one, self.tail = one, tail
        self.ring = RingSum(
            self.copies, at.y, at.at_y(1), at.at_y(3),
            lambda j, h: chip.at[j // 2, rows(576 * (j % 2) + 288 * h, 288)],
            [bufs.at[0], bufs.at[1]], [bufs.at[2], bufs.at[3]], [bufs.at[4], bufs.at[5]],
        )
        self.ring.start()

    def relay(self):
        self.ring.relay()

    def second(self):
        at, one, tail = self.at, self.one, self.tail
        self.ring.finish(lambda h: one.at[pl.ds(288 * h, 288)])
        self.sum = DirectSum(
            self.copies, at.z, at.at_z, lambda j: one.at[rows(144 * j, 144)], [tail.at[n] for n in range(3)]
        )
        self.sum.start()

    def back(self):
        at, out = self.at, self.out
        start = self.base + 576 * at.low
        self.sum.finish(out.at[rows(start + 144 * at.z, 144)])
        self.gather = DirectGather(self.copies, at.z, at.at_z, lambda j: out.at[rows(start + 144 * j, 144)])
        self.gather.start()

    def beside(self):
        at, out = self.at, self.out
        self.gather.finish()
        view = out.at[rows(self.base + 576 * at.low, 576)]
        self.next = self.copies.send(view, view, at.beside())
        self.half = self.to_sibling(576 * at.low, 576)

    def share(self):
        at, out = self.at, self.out
        self.copies.landed(self.next, out.at[rows(self.base + 576 * (1 - at.low), 576)])
        self.rest = self.to_sibling(576 * (1 - at.low), 576)

    def share_rest(self):
        pass

    def end(self):
        self.from_sibling(self.half)
        self.from_sibling(self.rest)


class FlowZY(Flow):
    def begin(self, bufs, one, tail):
        at, chip = self.at, self.chip
        self.add_core()
        self.one, self.tail = one, tail
        self.ring = RingSum(
            self.copies, at.z, at.at_z(1), at.at_z(3),
            lambda j, h: chip.at[h, rows(288 * j, 288)],
            [bufs.at[0], bufs.at[1]], [bufs.at[2], bufs.at[3]], [bufs.at[4], bufs.at[5]],
        )
        self.ring.start()

    def relay(self):
        self.ring.relay()

    def second(self):
        at, one, tail = self.at, self.one, self.tail
        self.ring.finish(lambda h: one.at[pl.ds(288 * h, 288)])
        self.sum = DirectSum(
            self.copies, at.y, at.at_y, lambda j: one.at[rows(144 * j, 144)], [tail.at[n] for n in range(3)]
        )
        self.sum.start()

    def back(self):
        at, out = self.at, self.out
        view = out.at[rows(self.base + 288 * at.z + 144 * at.low, 144)]
        self.sum.finish(view)
        self.next = self.copies.send(view, view, at.beside())

    def beside(self):
        at, out = self.at, self.out
        self.copies.landed(self.next, out.at[rows(self.base + 288 * at.z + 144 * (1 - at.low), 144)])
        self.gather = RingGather(
            self.copies, at.z, at.at_z(1), at.at_z(3),
            lambda j: out.at[rows(self.base + 288 * j, 288)],
            lambda j, h: out.at[rows(self.base + 288 * j + 144 * h, 144)],
        )
        self.gather.start()

    def share(self):
        self.gather.relay()

    def share_rest(self):
        self.gather.finish()
        self.all = self.to_sibling(0, 1152)

    def end(self):
        self.from_sibling(self.all)


PARTS = ((0, 288, 0), (1, 864, 288))


def final_kernel(
    f_zero, e_zero, f_one, e_one, sf_zero, se_zero, sf_one, se_one,
    scaled, branch, grad, normed, inverse, middle, params, out, small_out, back,
    chip, own_half, ones, bufs, tails, got, first_small, grad_rows, normed_rows, inverse_rows, middle_rows,
    slices, send_sems, recv_sems, local_sem, half_sems, tail_sems,
):
    at = Place()
    x, y, c = at.x, at.y, at.c
    tail_loads = []
    for source, target in ((grad, grad_rows), (normed, normed_rows), (inverse, inverse_rows), (middle, middle_rows)):
        for h in range(2):
            copy = pltpu.make_async_copy(
                source.at[rows(256 * h + 64 * x, 64)], target.at[pl.ds(64 * h, 64)], tail_sems.at[len(tail_loads)]
            )
            copy.start()
            tail_loads.append(copy)
    greet(
        [at.at_x(k) for k in (1, 2, 3)]
        + [at.at_y(k) for k in (1, 2, 3)]
        + [at.at_z(k) for k in (1, 2, 3)]
        + [at.sibling()]
    )
    copies = Copies(send_sems, recv_sems, at.at_x(1))
    send, landed = copies.send, copies.landed
    quarter = rows(64 * x, 64)
    layers = ((f_zero, e_zero), (f_one, e_one))
    flows = []
    for n in range(PAIRS):
        for kind, start in ((FlowYZ, 0), (FlowZY, PAIRS * LANES)):
            flows.append(kind(at, copies, chip, own_half, out, pl.ds(start + n * LANES, LANES)))
    flows[0].send_core(layers)
    flows[1].send_core(layers)
    halves = []
    for layer in range(2):
        for which, size, place in PARTS:
            copy = pltpu.make_async_copy(
                layers[layer][which].at[rows(size * c, size)],
                own_half.at[layer, pl.ds(place, size)],
                half_sems.at[2 * layer + which],
            )
            copy.start()
            halves.append(copy)
    for copy in tail_loads:
        copy.wait()
    for h in range(2):
        here = pl.ds(64 * h, 64)
        value = grad_rows[here] + norm_back(scaled[h], normed_rows[here], inverse_rows[here, 0:1])
        slices[0, h] = value.astype(bf16)
        slices[1, h] = (middle_rows[here] + (branch[h] + params[1, 8:9])).astype(bf16)
    home = []
    for k in (1, 3, 2):
        j = (y + k) % 4
        home.append((k, send(slices.at[j // 2, j % 2], back.at[y, quarter], at.at_y(k))))
    own = pltpu.make_async_copy(slices.at[y // 2, y % 2], back.at[y, quarter], local_sem)
    own.start()
    for flow in flows[2:]:
        flow.send_core(layers)
    for layer, refs in enumerate(((sf_zero, se_zero), (sf_one, se_one))):
        for which, ref in enumerate(refs):
            first_small[layer, pl.ds(8 * which, 8)] = ref[...]
    small_x = [(k, send(first_small, got.at[k - 1], at.at_x(k))) for k in (1, 3, 2)]
    for copy in halves:
        copy.wait()

    def slot(t):
        for n in range(PAIRS):
            for m in (2 * n, 2 * n + 1):
                flow, stage = flows[m], t - n
                if stage == 0:
                    flow.begin(bufs.at[m], ones.at[m], tails.at[m])
                elif 0 < stage < 7:
                    (flow.relay, flow.second, flow.back, flow.beside, flow.share, flow.share_rest)[stage - 1]()

    slot(0)
    own.wait()
    for k, index in home:
        landed(index, back.at[(y + 4 - k) % 4, quarter])
    outer = RingGather(
        copies, x, at.at_x(1), at.at_x(3),
        lambda j: back.at[:, rows(64 * j, 64)],
        lambda j, h: back.at[pl.ds(2 * h, 2), rows(64 * j, 64)],
    )
    outer.start()
    slot(1)
    slot(2)
    outer.relay()
    for k, index in small_x:
        landed(index, got.at[k - 1])
    of_norms = lax.broadcasted_iota(jnp.int32, first_small.shape, 1) % 8 < 2
    others = got[0] + got[1] + got[2]
    small_out[...] = first_small[...] + jnp.where(of_norms, others, 0.0)
    small_z = [(k, send(small_out, got.at[2 + k], at.at_z(k))) for k in (1, 3, 2)]
    slot(3)
    for k, index in small_z:
        landed(index, got.at[2 + k])
    for k, index in small_z:
        copies.started[index].wait_send()
    small_out[...] = small_out[...] + (got[3] + got[4] + got[5])
    small_y = [(k, send(small_out, got.at[5 + k], at.at_y(k))) for k in (1, 3, 2)]
    slot(4)
    slot(5)
    for k, index in small_y:
        landed(index, got.at[5 + k])
    for k, index in small_y:
        copies.started[index].wait_send()
    small_out[...] = small_out[...] + (got[6] + got[7] + got[8])
    small_c = send(small_out, got.at[9], at.sibling())
    slot(6)
    landed(small_c, got.at[9])
    copies.started[small_c].wait_send()
    small_out[...] = small_out[...] + got[9]
    slot(7)
    slot(8)
    outer.finish()
    for flow in flows:
        flow.end()
    waited = {index for _, index in small_z} | {index for _, index in small_y} | {small_c}
    for index, copy in enumerate(copies.started):
        if index not in waited:
            copy.wait_send()


FINAL_COPIES = 160


def final(grads, small, last):
    vmem = pl.BlockSpec(memory_space=pltpu.VMEM)
    return pl.pallas_call(
        final_kernel,
        out_shape=[
            jax.ShapeDtypeStruct((GRAD_ROWS, WIDTH), bf16),
            jax.ShapeDtypeStruct((2, 16, WIDTH), f32),
            jax.ShapeDtypeStruct((4, BLOCK, WIDTH), bf16),
        ],
        in_specs=[pl.BlockSpec(memory_space=pl.ANY)] * 4 + [vmem] * 6 + [pl.BlockSpec(memory_space=pl.ANY)] * 4 + [vmem],
        out_specs=[vmem] * 3,
        scratch_shapes=[
            pltpu.VMEM((2, 1152, WIDTH), bf16),
            pltpu.VMEM((2, 1152, WIDTH), bf16),
            pltpu.VMEM((2 * PAIRS, 576, LANES), bf16),
            pltpu.VMEM((2 * PAIRS, 6, 288, LANES), bf16),
            pltpu.VMEM((2 * PAIRS, 3, 144, LANES), bf16),
            pltpu.VMEM((10, 2, 16, WIDTH), f32),
            pltpu.VMEM((2, 16, WIDTH), f32),
            pltpu.VMEM((128, WIDTH), f32),
            pltpu.VMEM((128, WIDTH), f32),
            pltpu.VMEM((128, 128), f32),
            pltpu.VMEM((128, WIDTH), f32),
            pltpu.VMEM((2, 2, 64, WIDTH), bf16),
            pltpu.SemaphoreType.DMA((FINAL_COPIES,)),
            pltpu.SemaphoreType.DMA((FINAL_COPIES,)),
            pltpu.SemaphoreType.DMA,
            pltpu.SemaphoreType.DMA((4,)),
            pltpu.SemaphoreType.DMA((8,)),
        ],
        compiler_params=pltpu.CompilerParams(
            collective_id=3, has_side_effects=True, vmem_limit_bytes=VMEM_LIMIT
        ),
        name="final",
    )(*grads, *small, *last)


def nn(a, b):
    return lax.dot_general(a, b, (((1,), (0,)), ((), ())), preferred_element_type=f32)


def nt(a, b):
    return lax.dot_general(a, b, (((1,), (1,)), ((), ())), preferred_element_type=f32)


def tn(a, b):
    return lax.dot_general(a, b, (((0,), (0,)), ((), ())), preferred_element_type=f32)


def turner():
    c = lax.broadcasted_iota(jnp.int32, (INNER, INNER), 0)
    r = lax.broadcasted_iota(jnp.int32, (INNER, INNER), 1)
    lane = c % HEAD_DIM
    half = ROT // 2
    minus = (lane < half) & (r == c + half)
    plus = (lane >= half) & (lane < ROT) & (r == c - half)
    return jnp.where(plus, 1.0, jnp.where(minus, -1.0, 0.0)).astype(bf16)


def head_lanes(shape, h):
    lane = lax.broadcasted_iota(jnp.int32, shape, len(shape) - 1)
    return (lane >= h * HEAD_DIM) & (lane < (h + 1) * HEAD_DIM)


def pick(value, h):
    return jnp.where(head_lanes(value.shape, h), value, jnp.zeros_like(value))


def chunk_rows(i):
    return pl.ds(pl.multiple_of(i * BLOCK, BLOCK), BLOCK)


def gather_keys(own, other, keys, values):
    for n, ref in enumerate((keys, values)):
        ref[0:BLOCK] = own[n, 0:BLOCK]
        ref[BLOCK : 2 * BLOCK] = other[n, 0:BLOCK]
        ref[2 * BLOCK : 3 * BLOCK] = own[n, BLOCK : 2 * BLOCK]
        ref[3 * BLOCK : 4 * BLOCK] = other[n, BLOCK : 2 * BLOCK]


def key_places(c, shape, dim, blocks):
    i = lax.broadcasted_iota(jnp.int32, shape, dim)
    place = jnp.where(i < BLOCK, i + BLOCK * c, i - BLOCK * c)
    if blocks == 4:
        late = jnp.where(i < 3 * BLOCK, i + BLOCK * c, i - BLOCK * c)
        place = jnp.where(i < 2 * BLOCK, place, late)
    return place


SPANS = ((0, 2), (1, 4))


ROWS = 2 * BLOCK


def shape_of(*dims, dtype=f32):
    return jax.ShapeDtypeStruct(dims, dtype)


def at_layer(layer, *dims):
    return pl.BlockSpec((1,) + dims, lambda i: (layer,) + (0,) * len(dims))


def on_device(kernel, name, args, specs, outs, scratch):
    whole = pl.BlockSpec(memory_space=pltpu.VMEM)
    return pl.pallas_call(
        kernel,
        grid=(1,),
        out_shape=outs,
        in_specs=[whole if spec is None else spec for spec in specs],
        out_specs=[whole] * len(outs),
        scratch_shapes=scratch,
        compiler_params=pltpu.CompilerParams(vmem_limit_bytes=VMEM_LIMIT),
        name=name,
    )(*args)


def norm_back(scaled, normed, inverse):
    inner = scaled - jnp.mean(scaled, axis=-1, keepdims=True)
    inner = inner - normed * jnp.mean(scaled * normed, axis=-1, keepdims=True)
    return inner * inverse


class Env:
    def __init__(self, refs, ins, outs, scratch):
        refs = list(refs)
        sources = {name: refs.pop(0) for name in ins}
        self.targets = {name: refs.pop(0) for name in outs}
        self.v = types.SimpleNamespace(**{name: refs.pop(0) for name in list(ins) + list(outs) + list(scratch)})
        self.send_sems, self.recv_sems, load_sems, self.store_sems = refs
        self.held = [getattr(self.v, name) for name in ins]
        self.kept = [getattr(self.v, name) for name in outs]
        self.targets = list(self.targets.values())
        self.loads, self.stores = [], []
        for n, name in enumerate(ins):
            source, index = sources[name], ins[name][1]
            source = source if index is None else source.at[index]
            copy = pltpu.make_async_copy(source, self.held[n], load_sems.at[n])
            copy.start()
            self.loads.append(copy)

    def need(self, *refs):
        for ref in refs:
            n = [held is ref for held in self.held].index(True)
            if self.loads[n] is not None:
                self.loads[n].wait()
                self.loads[n] = None

    def done(self, *refs):
        for ref in refs:
            n = [kept is ref for kept in self.kept].index(True)
            copy = pltpu.make_async_copy(ref, self.targets[n], self.store_sems.at[n])
            copy.start()
            self.stores.append(copy)

    def close(self):
        assert not any(self.loads) and len(self.stores) == len(self.kept)
        for copy in self.stores:
            copy.wait()


def fused(body, name, ins, outs, scratch, copies, collective_id):
    def kernel(*refs):
        env = Env(refs, ins, outs, scratch)
        body(env)
        env.close()

    any_space = pl.BlockSpec(memory_space=pl.ANY)
    arrays = [array for array, _ in ins.values()]
    held = [pltpu.VMEM(array.shape if index is None else array.shape[1:], array.dtype) for array, index in ins.values()]
    kept = [pltpu.VMEM(s.shape, s.dtype) for s in list(outs.values()) + list(scratch.values())]
    got = pl.pallas_call(
        kernel,
        out_shape=list(outs.values()),
        in_specs=[any_space] * len(ins),
        out_specs=[any_space] * len(outs),
        scratch_shapes=held
        + kept
        + [
            pltpu.SemaphoreType.DMA((copies,)),
            pltpu.SemaphoreType.DMA((copies,)),
            pltpu.SemaphoreType.DMA((len(ins),)),
            pltpu.SemaphoreType.DMA((len(outs),)),
        ],
        compiler_params=pltpu.CompilerParams(
            collective_id=collective_id, has_side_effects=True, vmem_limit_bytes=VMEM_LIMIT
        ),
        name=name,
    )(*arrays)
    return types.SimpleNamespace(**dict(zip(outs, got)))


def block_sum(at, copies, part, bufs, block):
    return RingSum(
        copies, at.x, at.at_x(1), at.at_x(3),
        lambda j, h: part.at[block, rows(64 * j, 64), pl.ds(384 * h, 384)],
        [bufs.at[block, 0], bufs.at[block, 1]], [bufs.at[block, 2], bufs.at[block, 3]],
        [bufs.at[block, 4], bufs.at[block, 5]],
    )


def block_gather(at, copies, out, block):
    return RingGather(
        copies, at.x, at.at_x(1), at.at_x(3),
        lambda j: out.at[block, rows(64 * j, 64)],
        lambda j, h: out.at[block, rows(64 * j, 64), pl.ds(384 * h, 384)],
    )


def sum_out(at, out, block):
    return lambda h: out.at[block, rows(64 * at.x, 64), pl.ds(384 * h, 384)]


def piece_out(out, block):
    return lambda h: out.at[block, :, pl.ds(384 * h, 384)]


def forward_body(later, env):
    at, v = Place(), env.v
    greet([at.sibling()] if later else [at.sibling(), at.at_x(1), at.at_x(3)])
    copies = Copies(env.send_sems, env.recv_sems, at.sibling())
    wq, wt, small = v.wq, v.wt, v.small
    env.need(v.wq, v.small)
    turn = turner()
    for i in range(2):
        wt[INNER * i : INNER * (i + 1)] = nn(turn, wq[INNER * i : INNER * (i + 1)]).astype(bf16)

    def row(i, wide=WIDTH):
        return small[i : i + 1, :wide]

    env.need(v.x, v.cos, v.sin)
    if later:
        env.need(v.add, v.before)

    def front(i, carry):
        here = chunk_rows(i)
        x = v.x[i].astype(f32)
        if later:
            x = x + (v.add[i].astype(f32) + v.before[8:9])
            v.middle[here] = x
        centred = x - jnp.mean(x, axis=-1, keepdims=True)
        inverse = lax.rsqrt(jnp.mean(centred * centred, axis=-1, keepdims=True) + EPS)
        normed = centred * inverse
        v.normed[here] = normed
        v.inverse[here] = jnp.broadcast_to(inverse, (BLOCK, 128))
        first = (normed * row(0) + row(1)).astype(bf16)
        v.first[here] = first
        v.second[here] = (normed * row(2) + row(3)).astype(bf16)
        cosine, sine = v.cos[here], v.sin[here]
        query = (nt(first, wq[:INNER]) + row(4, INNER)) * cosine
        query = query + (nt(first, wt[:INNER]) + row(9, INNER)) * sine
        v.query[here] = (query * HEAD_DIM ** (-0.5)).astype(bf16)
        key = (nt(first, wq[INNER : 2 * INNER]) + row(5, INNER)) * cosine
        key = key + (nt(first, wt[INNER:]) + row(10, INNER)) * sine
        v.own[0, here] = key.astype(bf16)
        v.own[1, here] = (nt(first, wq[2 * INNER :]) + row(6, INNER)).astype(bf16)
        return carry

    lax.fori_loop(0, 2, front, 0)
    swap = copies.send(v.own, v.other, at.sibling())
    env.done(v.normed, v.inverse, v.first, v.second, v.query, v.own)
    if later:
        env.done(v.middle)
    env.need(v.up)

    def feed(i, carry):
        here = pl.ds(pl.multiple_of(i * 128, 128), 128)
        hidden = nn(v.second[here], v.up[...]) + row(7)
        below = 0.5 + 0.5 * lax.erf(hidden * (0.5**0.5))
        v.active[here] = (hidden * below).astype(bf16)
        density = jnp.exp(-0.5 * hidden * hidden) * 0.3989422804014327
        v.slope[here] = (below + hidden * density).astype(bf16)
        return carry

    lax.fori_loop(0, 4, feed, 0)
    env.done(v.active, v.slope)
    copies.landed(swap, v.other)
    env.done(v.other)
    keys, values, bias, logs = v.keys, v.values, v.bias, v.logs
    gather_keys(v.own, v.other, keys, values)
    logs[...] = jnp.zeros_like(logs)
    env.need(v.dense, v.down, v.starts)
    sums = {}
    for block, span in reversed(SPANS):
        here, n = pl.ds(block * BLOCK, BLOCK), span * BLOCK
        place = key_places(at.c, (BLOCK, n), 1, span)
        mine = lax.broadcasted_iota(jnp.int32, (BLOCK, n), 0) + (2 * block + at.c) * BLOCK
        allowed = (place <= mine) & (place >= v.starts[here])
        bias[:, :n] = jnp.where(allowed, 0.0, MASKED)
        query = v.query[here]
        mixed = jnp.zeros((BLOCK, INNER), f32)
        for h in range(HEADS):
            score = nt(pick(query, h), keys[:n]) + bias[:, :n]
            top = jnp.max(score, axis=-1, keepdims=True)
            expo = jnp.exp(score - top)
            total = jnp.sum(expo, axis=-1, keepdims=True)
            logs[here, h : h + 1] = top + jnp.log(total)
            mixed = mixed + pick(nn(expo.astype(bf16), values[:n]) * (1.0 / total), h)
        mixed = mixed.astype(bf16)
        v.mixed[here] = mixed
        v.part[block] = (nn(mixed, v.dense[...]) + nn(v.active[here], v.down[...])).astype(bf16)
        if not later:
            sums[block] = block_sum(at, copies, v.part, v.bufs, block)
            sums[block].start()
    v.log[...] = logs[...].T
    env.done(v.mixed, v.log)
    if later:
        env.done(v.part)
    else:
        reduce_and_gather(at, copies, sums, v.total, ())
        env.done(v.total)
    copies.drain()


def reduce_and_gather(at, copies, sums, out, between):
    between = list(between)

    def work():
        if between:
            between.pop(0)()

    work()
    sums[1].relay()
    work()
    sums[0].relay()
    work()
    gathers = {}
    for block in (1, 0):
        sums[block].finish(sum_out(at, out, block))
        gathers[block] = block_gather(at, copies, out, block)
        gathers[block].start()
        work()
    for block in (1, 0):
        gathers[block].relay()
        work()
    for block in (1, 0):
        gathers[block].finish()


def backward_body(later, env):
    at, v = Place(), env.v
    greet([at.sibling(), at.at_x(1), at.at_x(3)])
    copies = Copies(env.send_sems, env.recv_sems, at.sibling())
    extra = []
    if later:
        env.need(v.part)
        extra = [block_sum(at, copies, v.part, v.part_bufs, block) for block in (1, 0)]
        for ring in extra:
            ring.start()
        env.need(v.g)
        low = v.g
    else:
        env.need(v.g, v.add, v.n_one, v.inv_one)
        low = v.low

        def incoming(i, carry):
            here = chunk_rows(i)
            grad = v.g[i].astype(f32) + norm_back(
                v.add[i].astype(f32), v.n_one[here], v.inv_one[here, 0:1]
            )
            v.grad[here] = grad
            low[i] = grad.astype(bf16)
            return carry

        lax.fori_loop(0, 2, incoming, 0)
        env.done(v.grad)
    keys, values, bias, inner = v.keys, v.values, v.bias, v.inner
    env.need(v.own, v.other, v.query, v.mixed, v.log, v.dense, v.starts)
    gather_keys(v.own, v.other, keys, values)
    inner[...] = jnp.zeros_like(inner)
    dkeys, dvalues, log = v.dkeys, v.dvalues, v.log
    for block, span in reversed(SPANS):
        here, n = pl.ds(block * BLOCK, BLOCK), span * BLOCK
        place = key_places(at.c, (n, BLOCK), 0, span)
        mine = lax.broadcasted_iota(jnp.int32, (n, BLOCK), 1) + (2 * block + at.c) * BLOCK
        allowed = (place <= mine) & (place >= v.starts[0:1, here])
        bias[:n] = jnp.where(allowed, 0.0, MASKED)
        d_mixed = nt(low[block], v.dense[...]).astype(bf16)
        product = d_mixed.astype(f32) * v.mixed[here].astype(f32)
        for h in range(HEADS):
            inner[:, h : h + 1] = jnp.sum(pick(product, h), axis=-1, keepdims=True)
        inner_rows = inner[...].T
        query = v.query[here]
        d_query = jnp.zeros((BLOCK, INNER), f32)
        for h in range(HEADS):
            mine_q, mine_d = pick(query, h), pick(d_mixed, h)
            prob = jnp.exp(nt(keys[:n], mine_q) + bias[:n] - log[h : h + 1, here])
            d_prob = nt(values[:n], mine_d)
            d_score = (prob * (d_prob - inner_rows[h : h + 1])).astype(bf16)
            d_value = nn(prob.astype(bf16), mine_d)
            d_key = nn(d_score, mine_q)
            if span == 4 and h == 0:
                dvalues[...] = d_value
                dkeys[...] = d_key
            else:
                dvalues[:n] += d_value
                dkeys[:n] += d_key
            d_query = d_query + pick(tn(d_score, keys[:n]), h)
        v.d_query[here] = d_query * HEAD_DIM ** (-0.5)
    for n, ref in enumerate((dkeys, dvalues)):
        v.d_other[n, 0:BLOCK] = ref[BLOCK : 2 * BLOCK].astype(bf16)
        v.d_other[n, BLOCK : 2 * BLOCK] = ref[3 * BLOCK : 4 * BLOCK].astype(bf16)
    swap = copies.send(v.d_other, v.got, at.sibling())
    for ring in extra:
        ring.relay()

    small, hid, normed = v.small, v.hid, v.normed
    sums_one, sums_two = v.sums_one, v.sums_two
    sums_one[...] = jnp.zeros_like(sums_one)
    sums_two[...] = jnp.zeros_like(sums_two)
    env.need(v.down, v.up, v.small, v.slope, v.normed)

    def feed(i, carry):
        here = chunk_rows(i)
        g = low[i]
        d_hidden = (nt(g, v.down[...]) * v.slope[here].astype(f32)).astype(bf16)
        hid[here] = d_hidden
        d_second = nt(d_hidden, v.up[...])
        v.e_two[here] = d_second * small[2:3]
        sums_two[0:1] += jnp.sum(d_second * normed[here], axis=0, keepdims=True)
        sums_two[1:2] += jnp.sum(d_second, axis=0, keepdims=True)
        sums_two[2:3] += jnp.sum(g.astype(f32), axis=0, keepdims=True)
        sums_two[3:4] += jnp.sum(d_hidden.astype(f32), axis=0, keepdims=True)
        return carry

    lax.fori_loop(0, 2, feed, 0)
    env.done(v.sums_two)
    for ring, block in zip(extra, (1, 0)):
        ring.finish(piece_out(v.part_sum, block))
    if later:
        env.done(v.part_sum)

    env.need(v.cos, v.sin, v.wq, v.first, v.second, v.active)
    turn = turner()
    wq, packed, got = v.wq, v.packed, v.got

    def unrotate(value, cosine, sine):
        moved = value * sine
        high = moved.astype(bf16)
        lower = (moved - high.astype(f32)).astype(bf16)
        return value * cosine + (nn(high, turn) + nn(lower, turn))

    copies.landed(swap, got)
    sums = {}
    for i in (1, 0):
        here = pl.ds(i * BLOCK, BLOCK)
        there = pl.ds(2 * i * BLOCK, BLOCK)
        cosine, sine = v.cos[here], v.sin[here]
        parts = [
            unrotate(v.d_query[here], cosine, sine),
            unrotate(dkeys[there] + got[0, here].astype(f32), cosine, sine),
            dvalues[there] + got[1, here].astype(f32),
        ]
        d_first = jnp.zeros((BLOCK, WIDTH), f32)
        for n, part in enumerate(parts):
            part = part.astype(bf16)
            packed[n, here] = part
            d_first = d_first + nn(part, wq[INNER * n : INNER * (n + 1)])
            sums_one[2 + n : 3 + n, :INNER] += jnp.sum(part.astype(f32), axis=0, keepdims=True)
        v.e[i] = (d_first * small[0:1] + v.e_two[here]).astype(bf16)
        sums[i] = block_sum(at, copies, v.e, v.bufs, i)
        sums[i].start()
        sums_one[0:1] += jnp.sum(d_first * normed[here], axis=0, keepdims=True)
        sums_one[1:2] += jnp.sum(d_first, axis=0, keepdims=True)
    env.done(v.sums_one)

    grads_one, grads_two = v.grads_one, v.grads_two

    def grad_dense():
        grads_two[:INNER] = tn(v.mixed[...], low[...].reshape(ROWS, WIDTH)).astype(bf16)

    def grad_up():
        grads_two[INNER : INNER + WIDTH] = tn(v.second[...], hid[...]).astype(bf16)

    def grad_down():
        grads_two[INNER + WIDTH :] = tn(v.active[...], low[...].reshape(ROWS, WIDTH)).astype(bf16)

    def grad_packed():
        for n in range(3):
            grads_one[INNER * n : INNER * (n + 1)] = tn(packed[n], v.first[...]).astype(bf16)

    if later:
        reduce_and_gather(at, copies, sums, v.total, (grad_dense, grad_packed, grad_up, grad_down))
        env.done(v.total)
    else:
        grad_dense()
        sums[1].relay()
        grad_packed()
        sums[0].relay()
        grad_up()
        grad_down()
        for block in (1, 0):
            sums[block].finish(piece_out(v.total, block))
        env.done(v.total)
    env.done(v.grads_one, v.grads_two)
    copies.drain()


def low_shape(*dims):
    return shape_of(*dims, dtype=bf16)


def forward_layer(layer, xg, add, stacks, tables):
    wq, wd, wu, wn, small = stacks
    cosine, sine, start_col, _ = tables
    later = add is not None
    ins = dict(wq=(wq, layer), small=(small, layer), x=(xg, 0))
    if later:
        ins.update(add=(add, None), before=(small, 0))
    ins.update(
        cos=(cosine, None), sin=(sine, None), up=(wu, layer), dense=(wd, layer), down=(wn, layer),
        starts=(start_col, None),
    )
    outs = dict(
        normed=shape_of(ROWS, WIDTH), inverse=shape_of(ROWS, 128), first=low_shape(ROWS, WIDTH),
        second=low_shape(ROWS, WIDTH), query=low_shape(ROWS, INNER), own=low_shape(2, ROWS, INNER),
        other=low_shape(2, ROWS, INNER), active=low_shape(ROWS, WIDTH), slope=low_shape(ROWS, WIDTH),
        mixed=low_shape(ROWS, INNER), log=shape_of(128, ROWS),
    )
    scratch = dict(
        wt=low_shape(2 * INNER, WIDTH), keys=low_shape(SEQ, INNER), values=low_shape(SEQ, INNER),
        logs=shape_of(ROWS, 128), bias=shape_of(BLOCK, SEQ),
    )
    if later:
        outs.update(middle=shape_of(ROWS, WIDTH), part=low_shape(2, BLOCK, WIDTH))
    else:
        outs.update(total=low_shape(2, BLOCK, WIDTH))
        scratch.update(part=low_shape(2, BLOCK, WIDTH), bufs=low_shape(2, 6, 64, 384))
    return fused(
        functools.partial(forward_body, later), "forward", ins, outs, scratch, 1 if later else 21, 5 if later else 4
    )


def backward_layer(layer, xg, add, stacks, tables, kept, kept_one):
    wq, wd, wu, wn, small = stacks
    cosine, sine, _, start_row = tables
    later = add is None
    if later:
        ins = dict(part=(kept.part, None), g=(xg, 1))
    else:
        ins = dict(
            g=(xg, 1), add=(add, None), n_one=(kept_one.normed, None), inv_one=(kept_one.inverse, None)
        )
    ins.update(
        own=(kept.own, None), other=(kept.other, None), query=(kept.query, None), mixed=(kept.mixed, None),
        log=(kept.log, None),
    )
    ins.update(dense=(wd, layer), starts=(start_row, None), down=(wn, layer), up=(wu, layer), small=(small, layer))
    ins.update(slope=(kept.slope, None), normed=(kept.normed, None))
    ins.update(cos=(cosine, None), sin=(sine, None), wq=(wq, layer))
    ins.update(first=(kept.first, None), second=(kept.second, None), active=(kept.active, None))
    outs = dict(
        grads_one=low_shape(3 * INNER, WIDTH), grads_two=low_shape(INNER + 2 * WIDTH, WIDTH),
        sums_one=shape_of(8, WIDTH), sums_two=shape_of(8, WIDTH),
    )
    scratch = dict(
        keys=low_shape(SEQ, INNER), values=low_shape(SEQ, INNER), bias=shape_of(SEQ, BLOCK),
        inner=shape_of(BLOCK, 128), dkeys=shape_of(SEQ, INNER), dvalues=shape_of(SEQ, INNER),
        d_query=shape_of(ROWS, INNER), d_other=low_shape(2, ROWS, INNER), got=low_shape(2, ROWS, INNER),
        hid=low_shape(ROWS, WIDTH), e_two=shape_of(ROWS, WIDTH), packed=low_shape(3, ROWS, INNER),
        e=low_shape(2, BLOCK, WIDTH), bufs=low_shape(2, 6, 64, 384),
    )
    if later:
        outs.update(total=low_shape(2, BLOCK, WIDTH), part_sum=shape_of(2, 64, WIDTH))
        scratch.update(part_bufs=low_shape(2, 6, 64, 384))
    else:
        outs.update(total=shape_of(2, 64, WIDTH), grad=shape_of(ROWS, WIDTH))
        scratch.update(low=low_shape(2, BLOCK, WIDTH))
    return fused(
        functools.partial(backward_body, later), "backward", ins, outs, scratch, 33 if later else 13, 6 if later else 7
    )


def prepare_kernel(
    boundary, segment_ids, gain_one, shift_one, gain_two, shift_two, wq, qkv_bias, dense_bias, up_bias, down_bias,
    block_out, wq_out, small_out, cos_out, sin_out, col_out, row_out,
):
    at = Place()
    for m in range(4):
        block_out[m] = boundary[0, m].astype(bf16)
    for kind in range(3):
        for h in range(HEADS):
            to, source = INNER * kind + HEAD_DIM * h, INNER * h + HEAD_DIM * kind
            wq_out[to : to + HEAD_DIM] = wq[source : source + HEAD_DIM]
    small_out[...] = jnp.zeros_like(small_out)
    for n, ref in enumerate((gain_one, shift_one, gain_two, shift_two)):
        small_out[n : n + 1] = ref[...]
    half = ROT // 2
    for kind in range(3):
        for h in range(HEADS):
            lanes = pl.ds(HEAD_DIM * h, HEAD_DIM)
            source = INNER * h + HEAD_DIM * kind
            piece = qkv_bias[:, source : source + HEAD_DIM]
            small_out[4 + kind : 5 + kind, lanes] = piece
            if kind < 2:
                small_out[9 + kind : 10 + kind, pl.ds(HEAD_DIM * h, half)] = -piece[:, half:ROT]
                small_out[9 + kind : 10 + kind, pl.ds(HEAD_DIM * h + half, half)] = piece[:, :half]
    small_out[7:8] = up_bias[...]
    small_out[8:9] = dense_bias[...] + down_bias[...]
    labels = segment_ids[at.y, pl.ds(at.z, 1)]
    start = jnp.zeros((1, SEQ), f32)
    for v in range(1, 5):
        count = jnp.sum((labels == v - 1).astype(f32), axis=1, keepdims=True)
        start = start + jnp.where(labels >= v, count, 0.0)
    cosine_lane = lax.broadcasted_iota(jnp.int32, (1, INNER), 1) % HEAD_DIM
    rotary = cosine_lane < ROT
    freqs = jnp.ones((1, INNER), f32)
    for n in range(1, half):
        freqs = jnp.where(cosine_lane % half == n, 10000.0 ** (-2.0 * n / ROT), freqs)
    for i in range(2):
        pieces = [start[:, BLOCK * (2 * i + k) : BLOCK * (2 * i + k + 1)] for k in range(2)]
        mine = jnp.where(at.c == 0, pieces[0], pieces[1])
        row_out[:, BLOCK * i : BLOCK * (i + 1)] = mine.astype(jnp.int32)
        column = jnp.broadcast_to(mine, (128, BLOCK)).T[:, 0:1]
        here = pl.ds(BLOCK * i, BLOCK)
        col_out[here] = column.astype(jnp.int32)
        spot = lax.broadcasted_iota(jnp.int32, (BLOCK, 1), 0) + (2 * i + at.c) * BLOCK
        angles = (spot.astype(f32) - column) * freqs
        cos_out[here] = jnp.where(rotary, jnp.cos(angles), 1.0)
        sin_out[here] = jnp.where(rotary, jnp.sin(angles), 0.0)


def finish_kernel(
    total, small, back, x_out, g1, s1, g2, s2, qkv_out, qkv_bias, dense_out, dense_bias, up_out, up_bias,
    down_out, down_bias, total_in, back_in, x_hold, qkv_hold, dense_hold, up_hold, down_hold, load_sems, store_sems,
):
    p = lax.axis_index("pipe")
    loads = [pltpu.make_async_copy(back.at[m], back_in.at[m], load_sems.at[m]) for m in range(4)]
    loads += [
        pltpu.make_async_copy(total.at[span], total_in.at[span], load_sems.at[4 + n])
        for n, span in enumerate((pl.ds(1536, 768), pl.ds(480, 672), pl.ds(1152, 384), pl.ds(0, 480)))
    ]
    for copy in loads:
        copy.start()
    stores = []

    def store(source, target):
        copy = pltpu.make_async_copy(source, target, store_sems.at[len(stores)])
        copy.start()
        stores.append(copy)

    for m in range(4):
        loads[m].wait()
        x_hold[m] = back_in[m].astype(f32)
        store(x_hold.at[m], x_out.at[0, m])
    loads[4].wait()
    down_hold[...] = total_in[1536:].astype(f32)
    store(down_hold, down_out.at[0])
    loads[5].wait()
    loads[6].wait()
    up_hold[:672] = total_in[480:1152].astype(f32)
    up_hold[672:] = total_in[1440:1536].astype(f32)
    store(up_hold, up_out.at[0])
    loads[7].wait()
    for h in range(HEADS):
        for kind in range(3):
            to, source = INNER * h + HEAD_DIM * kind, INNER * kind + HEAD_DIM * h
            qkv_bias[:, to : to + HEAD_DIM] = small[p, 2 + kind : 3 + kind, HEAD_DIM * h : HEAD_DIM * (h + 1)]
            for start in (source, source + HEAD_DIM // 2):
                place = start if start < 288 else start - 288 + 1152
                qkv_hold[to + start - source : to + start - source + HEAD_DIM // 2] = total_in[
                    place : place + HEAD_DIM // 2
                ].astype(f32)
    store(qkv_hold, qkv_out.at[0])
    dense_hold[...] = total_in[288:480].astype(f32)
    store(dense_hold, dense_out.at[0])
    for row, ref in ((0, g1), (1, s1), (8, g2), (9, s2), (10, dense_bias), (11, up_bias), (10, down_bias)):
        ref[...] = small[p, row : row + 1]
    for copy in stores:
        copy.wait()


def local(
    boundary,
    segment_ids,
    attn_gain,
    attn_shift,
    mlp_gain,
    mlp_shift,
    qkv_weight,
    qkv_bias,
    dense_weight,
    dense_bias,
    up_weight,
    up_bias,
    down_weight,
    down_bias,
):
    block, wq, small, cosine, sine, start_col, start_row = on_device(
        prepare_kernel, "prepare",
        [boundary, segment_ids, attn_gain, attn_shift, mlp_gain, mlp_shift, qkv_weight[0].T, qkv_bias, dense_bias, up_bias,
         down_bias],
        [None] * 11,
        [
            shape_of(4, BLOCK, WIDTH, dtype=bf16), shape_of(3 * INNER, WIDTH, dtype=bf16), shape_of(16, WIDTH),
            shape_of(ROWS, INNER), shape_of(ROWS, INNER), shape_of(ROWS, 1, dtype=jnp.int32),
            shape_of(1, ROWS, dtype=jnp.int32),
        ],
        [],
    )
    tables = (cosine, sine, start_col, start_row)
    xg, *stacks = spread(block, wq, dense_weight[0], up_weight[0], down_weight[0], small)
    zero = forward_layer(0, xg, None, stacks, tables)
    one = forward_layer(1, xg, zero.total, stacks, tables)
    back_one = backward_layer(1, xg, None, stacks, tables, one, one)
    back_zero = backward_layer(0, xg, back_one.total, stacks, tables, zero, one)
    total, small_total, back = final(
        [back_zero.grads_one, back_zero.grads_two, back_one.grads_one, back_one.grads_two],
        [back_zero.sums_one, back_zero.sums_two, back_one.sums_one, back_one.sums_two],
        [
            back_zero.total, back_one.part_sum, back_zero.grad, zero.normed, zero.inverse,
            one.middle, stacks[4],
        ],
    )
    vector = shape_of(1, WIDTH)
    vmem, any_space = pl.BlockSpec(memory_space=pltpu.VMEM), pl.BlockSpec(memory_space=pl.ANY)
    outs = list(
        pl.pallas_call(
            finish_kernel,
            out_shape=[shape_of(1, 4, BLOCK, WIDTH)] + [vector] * 4
            + [shape_of(1, 3 * INNER, WIDTH), shape_of(1, 3 * INNER), shape_of(1, INNER, WIDTH), vector]
            + [shape_of(1, WIDTH, WIDTH), vector] * 2,
            in_specs=[any_space, vmem, any_space],
            out_specs=[any_space] + [vmem] * 4 + [any_space, vmem] * 4,
            scratch_shapes=[
                pltpu.VMEM((GRAD_ROWS, WIDTH), bf16),
                pltpu.VMEM((4, BLOCK, WIDTH), bf16),
                pltpu.VMEM((4, BLOCK, WIDTH), f32),
                pltpu.VMEM((3 * INNER, WIDTH), f32),
                pltpu.VMEM((INNER, WIDTH), f32),
                pltpu.VMEM((WIDTH, WIDTH), f32),
                pltpu.VMEM((WIDTH, WIDTH), f32),
                pltpu.SemaphoreType.DMA((8,)),
                pltpu.SemaphoreType.DMA((8,)),
            ],
            compiler_params=pltpu.CompilerParams(vmem_limit_bytes=VMEM_LIMIT),
            name="finish",
        )(total, small_total, back)
    )
    outs[5] = outs[5].transpose(0, 2, 1)
    return tuple(outs)


def solution(mesh):
    in_specs = (
        P("pipe", None, "dp", None),
        P(),
        P("pipe", None),
        P("pipe", None),
        P("pipe", None),
        P("pipe", None),
        P("pipe", None, "tensor"),
        P("pipe", "tensor"),
        P("pipe", "tensor", None),
        P("pipe", None),
        P("pipe", None, "tensor"),
        P("pipe", "tensor"),
        P("pipe", "tensor", None),
        P("pipe", None),
    )
    out_specs = (
        P("pipe", None, "dp", None),
        P("pipe", None),
        P("pipe", None),
        P("pipe", None),
        P("pipe", None),
        P("pipe", None, "tensor"),
        P("pipe", "tensor"),
        P("pipe", "tensor", None),
        P("pipe", None),
        P("pipe", None, "tensor"),
        P("pipe", "tensor"),
        P("pipe", "tensor", None),
        P("pipe", None),
    )
    return jax.shard_map(local, mesh=mesh, in_specs=in_specs, out_specs=out_specs, check_vma=False)
```

```python
import functools
import types

import jax
import jax.numpy as jnp
from jax import lax
from jax.experimental import pallas as pl
from jax.experimental.pallas import tpu as pltpu
from jax.sharding import PartitionSpec as P

MESH = pl.DeviceIdType.MESH
HEAD_DIM = 64
ROT = 16
EPS = 1e-05
MASKED = -1e30
WIDTH = 768
SEQ = 1024
BLOCK = 256
HEADS = 3
INNER = HEADS * HEAD_DIM
GRAD_ROWS = 2304
bf16 = jnp.bfloat16
f32 = jnp.float32
VMEM_LIMIT = 56 * 1024 * 1024


class Place:
    def __init__(self):
        self.p = lax.axis_index("pipe")
        self.d = lax.axis_index("dp")
        self.x = lax.axis_index("tensor")
        self.z = self.d // 4
        self.low = (self.d // 2) % 2
        self.c = self.d % 2
        self.y = 2 * self.p + self.low

    def at_x(self, steps):
        return (self.p, self.d, (self.x + steps) % 4)

    def at_y(self, steps):
        y = (self.y + steps) % 4
        return (y // 2, self.z * 4 + (y % 2) * 2 + self.c, self.x)

    def at_z(self, steps):
        return (self.p, ((self.z + steps) % 4) * 4 + self.d % 4, self.x)

    def sibling(self):
        return (self.p, self.d + 1 - 2 * self.c, self.x)

    def partner(self):
        return (1 - self.p, self.z * 4 + (1 - self.low) * 2 + self.c, self.x)

    def beside(self):
        return (self.p, self.z * 4 + (1 - self.low) * 2 + self.c, self.x)


def greet(devices):
    barrier = pltpu.get_barrier_semaphore()
    for device in devices:
        pl.semaphore_signal(barrier, inc=1, device_id=device, device_id_type=MESH)
    pl.semaphore_wait(barrier, len(devices))


class Copies:
    def __init__(self, send_sems, recv_sems, somebody):
        self.send_sems, self.recv_sems = send_sems, recv_sems
        self.somebody = somebody
        self.count = 0
        self.started = []

    def send(self, src, dst, device):
        k = self.count
        self.count += 1
        copy = pltpu.make_async_remote_copy(
            src_ref=src,
            dst_ref=dst,
            send_sem=self.send_sems.at[k],
            recv_sem=self.recv_sems.at[k],
            device_id=device,
            device_id_type=MESH,
        )
        copy.start()
        self.started.append(copy)
        return k

    def landed(self, k, dst):
        pltpu.make_async_remote_copy(
            src_ref=dst,
            dst_ref=dst,
            send_sem=self.send_sems.at[k],
            recv_sem=self.recv_sems.at[k],
            device_id=self.somebody,
            device_id_type=MESH,
        ).wait_recv()

    def drain(self):
        for copy in self.started:
            copy.wait_send()


class RingSum:
    def __init__(self, copies, me, right, left, chunk, relay, direct, final):
        self.copies, self.me, self.right, self.left = copies, me, right, left
        self.chunk, self.relay_in, self.direct, self.final = chunk, relay, direct, final

    def start(self):
        me, send = self.me, self.copies.send
        far, after, before = (me + 2) % 4, (me + 1) % 4, (me + 3) % 4
        self.k = [
            send(self.chunk(far, 0), self.relay_in[0], self.right),
            send(self.chunk(far, 1), self.relay_in[1], self.left),
            send(self.chunk(after, 1), self.direct[1], self.right),
            send(self.chunk(before, 0), self.direct[0], self.left),
        ]

    def relay(self):
        me, copies = self.me, self.copies
        after, before = (me + 1) % 4, (me + 3) % 4
        copies.landed(self.k[0], self.relay_in[0])
        add_into(self.relay_in[0], self.chunk(after, 0))
        k0 = copies.send(self.relay_in[0], self.final[0], self.right)
        copies.landed(self.k[1], self.relay_in[1])
        add_into(self.relay_in[1], self.chunk(before, 1))
        k1 = copies.send(self.relay_in[1], self.final[1], self.left)
        self.k += [k0, k1]

    def finish(self, out):
        copies = self.copies
        copies.landed(self.k[3], self.direct[0])
        copies.landed(self.k[4], self.final[0])
        store_sum(out(0), self.chunk(self.me, 0), self.direct[0], self.final[0])
        copies.landed(self.k[2], self.direct[1])
        copies.landed(self.k[5], self.final[1])
        store_sum(out(1), self.chunk(self.me, 1), self.direct[1], self.final[1])


class RingGather:
    def __init__(self, copies, me, right, left, piece, halves):
        self.copies, self.me, self.right, self.left = copies, me, right, left
        self.piece, self.halves = piece, halves

    def start(self):
        mine = self.piece(self.me)
        self.k = [
            self.copies.send(mine, mine, self.right),
            self.copies.send(mine, mine, self.left),
        ]

    def relay(self):
        before, after = (self.me + 3) % 4, (self.me + 1) % 4
        self.copies.landed(self.k[0], self.piece(before))
        view = self.halves(before, 0)
        k0 = self.copies.send(view, view, self.right)
        self.copies.landed(self.k[1], self.piece(after))
        view = self.halves(after, 1)
        k1 = self.copies.send(view, view, self.left)
        self.k += [k0, k1]

    def finish(self):
        far = (self.me + 2) % 4
        self.copies.landed(self.k[2], self.halves(far, 0))
        self.copies.landed(self.k[3], self.halves(far, 1))


class DirectSum:
    def __init__(self, copies, me, to, chunk, bufs):
        self.copies, self.me, self.to, self.chunk, self.bufs = copies, me, to, chunk, bufs

    def start(self):
        self.k = [
            self.copies.send(self.chunk((self.me + k) % 4), self.bufs[k - 1], self.to(k)) for k in (1, 3, 2)
        ]

    def finish(self, out):
        for index, k in zip(self.k, (1, 3, 2)):
            self.copies.landed(index, self.bufs[k - 1])
        store_sum(out, self.chunk(self.me), *self.bufs)


class DirectGather:
    def __init__(self, copies, me, to, piece):
        self.copies, self.me, self.to, self.piece = copies, me, to, piece

    def start(self):
        mine = self.piece(self.me)
        self.k = [self.copies.send(mine, mine, self.to(k)) for k in (1, 3, 2)]

    def finish(self):
        for index, k in zip(self.k, (1, 3, 2)):
            self.copies.landed(index, self.piece((self.me + 4 - k) % 4))


def add_into(ref, other):
    ref[...] = (ref[...].astype(f32) + other[...].astype(f32)).astype(ref.dtype)


def store_sum(out, *parts):
    total = parts[0][...].astype(f32)
    for part in parts[1:]:
        total = total + part[...].astype(f32)
    out[...] = total.astype(out.dtype)


def rows(start, size, step=16):
    return pl.ds(pl.multiple_of(start, step), size)


PAIRS = 3
LANES = 128


class Flow:
    def __init__(self, at, copies, chip, own_half, out, cols):
        self.at, self.copies, self.cols = at, copies, cols
        self.chip, self.own_half, self.out = chip.at[:, :, cols], own_half.at[:, :, cols], out.at[:, cols]
        self.base, self.other_base = 1152 * at.c, 1152 * (1 - at.c)

    def send_core(self, layers):
        self.core = []
        for layer in range(2):
            for which, size, place in PARTS:
                src = layers[layer][which].at[rows(size * (1 - self.at.c), size), self.cols]
                dst = self.chip.at[layer, pl.ds(place, size)]
                self.core.append((self.copies.send(src, dst, self.at.sibling()), dst))

    def add_core(self):
        for index, dst in self.core:
            self.copies.landed(index, dst)
        chip, own_half = self.chip, self.own_half

        def body(i, carry):
            here = rows(i * 192, 192)
            for layer in range(2):
                chip[layer, here] = (chip[layer, here].astype(f32) + own_half[layer, here].astype(f32)).astype(bf16)
            return carry

        lax.fori_loop(0, 6, body, 0)

    def to_sibling(self, start, size):
        view = self.out.at[rows(self.base + start, size)]
        index = self.copies.send(view, view, self.at.sibling())
        return index, start, size

    def from_sibling(self, sent):
        index, start, size = sent
        self.copies.landed(index, self.out.at[rows(self.other_base + start, size)])


class FlowYZ(Flow):
    def begin(self, bufs, one, tail):
        at, chip = self.at, self.chip
        self.add_core()
        self.one, self.tail = one, tail
        self.ring = RingSum(
            self.copies, at.y, at.at_y(1), at.at_y(3),
            lambda j, h: chip.at[j // 2, rows(576 * (j % 2) + 288 * h, 288)],
            [bufs.at[0], bufs.at[1]], [bufs.at[2], bufs.at[3]], [bufs.at[4], bufs.at[5]],
        )
        self.ring.start()

    def relay(self):
        self.ring.relay()

    def second(self):
        at, one, tail = self.at, self.one, self.tail
        self.ring.finish(lambda h: one.at[pl.ds(288 * h, 288)])
        self.sum = DirectSum(
            self.copies, at.z, at.at_z, lambda j: one.at[rows(144 * j, 144)], [tail.at[n] for n in range(3)]
        )
        self.sum.start()

    def back(self):
        at, out = self.at, self.out
        start = self.base + 576 * at.low
        self.sum.finish(out.at[rows(start + 144 * at.z, 144)])
        self.gather = DirectGather(self.copies, at.z, at.at_z, lambda j: out.at[rows(start + 144 * j, 144)])
        self.gather.start()

    def beside(self):
        at, out = self.at, self.out
        self.gather.finish()
        view = out.at[rows(self.base + 576 * at.low, 576)]
        self.next = self.copies.send(view, view, at.beside())
        self.half = self.to_sibling(576 * at.low, 576)

    def share(self):
        at, out = self.at, self.out
        self.copies.landed(self.next, out.at[rows(self.base + 576 * (1 - at.low), 576)])
        self.rest = self.to_sibling(576 * (1 - at.low), 576)

    def share_rest(self):
        pass

    def end(self):
        self.from_sibling(self.half)
        self.from_sibling(self.rest)


class FlowZY(Flow):
    def begin(self, bufs, one, tail):
        at, chip = self.at, self.chip
        self.add_core()
        self.one, self.tail = one, tail
        self.ring = RingSum(
            self.copies, at.z, at.at_z(1), at.at_z(3),
            lambda j, h: chip.at[h, rows(288 * j, 288)],
            [bufs.at[0], bufs.at[1]], [bufs.at[2], bufs.at[3]], [bufs.at[4], bufs.at[5]],
        )
        self.ring.start()

    def relay(self):
        self.ring.relay()

    def second(self):
        at, one, tail = self.at, self.one, self.tail
        self.ring.finish(lambda h: one.at[pl.ds(288 * h, 288)])
        self.sum = DirectSum(
            self.copies, at.y, at.at_y, lambda j: one.at[rows(144 * j, 144)], [tail.at[n] for n in range(3)]
        )
        self.sum.start()

    def back(self):
        at, out = self.at, self.out
        view = out.at[rows(self.base + 288 * at.z + 144 * at.low, 144)]
        self.sum.finish(view)
        self.next = self.copies.send(view, view, at.beside())

    def beside(self):
        at, out = self.at, self.out
        self.copies.landed(self.next, out.at[rows(self.base + 288 * at.z + 144 * (1 - at.low), 144)])
        self.gather = RingGather(
            self.copies, at.z, at.at_z(1), at.at_z(3),
            lambda j: out.at[rows(self.base + 288 * j, 288)],
            lambda j, h: out.at[rows(self.base + 288 * j + 144 * h, 144)],
        )
        self.gather.start()

    def share(self):
        self.gather.relay()

    def share_rest(self):
        self.gather.finish()
        self.all = self.to_sibling(0, 1152)

    def end(self):
        self.from_sibling(self.all)


PARTS = ((0, 288, 0), (1, 864, 288))


def final_kernel(
    f_zero, e_zero, f_one, e_one, sf_zero, se_zero, sf_one, se_one,
    scaled, branch, grad, normed, inverse, middle, params, out, small_out, back,
    chip, own_half, ones, bufs, tails, got, first_small, grad_rows, normed_rows, inverse_rows, middle_rows,
    slices, send_sems, recv_sems, local_sem, half_sems, tail_sems,
):
    at = Place()
    x, y, c = at.x, at.y, at.c
    tail_loads = []
    for source, target in ((grad, grad_rows), (normed, normed_rows), (inverse, inverse_rows), (middle, middle_rows)):
        for h in range(2):
            copy = pltpu.make_async_copy(
                source.at[rows(256 * h + 64 * x, 64)], target.at[pl.ds(64 * h, 64)], tail_sems.at[len(tail_loads)]
            )
            copy.start()
            tail_loads.append(copy)
    greet(
        [at.at_x(k) for k in (1, 2, 3)]
        + [at.at_y(k) for k in (1, 2, 3)]
        + [at.at_z(k) for k in (1, 2, 3)]
        + [at.sibling()]
    )
    copies = Copies(send_sems, recv_sems, at.at_x(1))
    send, landed = copies.send, copies.landed
    quarter = rows(64 * x, 64)
    layers = ((f_zero, e_zero), (f_one, e_one))
    flows = []
    for n in range(PAIRS):
        for kind, start in ((FlowYZ, 0), (FlowZY, PAIRS * LANES)):
            flows.append(kind(at, copies, chip, own_half, out, pl.ds(start + n * LANES, LANES)))
    flows[0].send_core(layers)
    flows[1].send_core(layers)
    halves = []
    for layer in range(2):
        for which, size, place in PARTS:
            copy = pltpu.make_async_copy(
                layers[layer][which].at[rows(size * c, size)],
                own_half.at[layer, pl.ds(place, size)],
                half_sems.at[2 * layer + which],
            )
            copy.start()
            halves.append(copy)
    for copy in tail_loads:
        copy.wait()
    for h in range(2):
        here = pl.ds(64 * h, 64)
        value = grad_rows[here] + norm_back(scaled[h], normed_rows[here], inverse_rows[here, 0:1])
        slices[0, h] = value.astype(bf16)
        slices[1, h] = (middle_rows[here] + (branch[h] + params[1, 8:9])).astype(bf16)
    home = []
    for k in (1, 3, 2):
        j = (y + k) % 4
        home.append((k, send(slices.at[j // 2, j % 2], back.at[y, quarter], at.at_y(k))))
    own = pltpu.make_async_copy(slices.at[y // 2, y % 2], back.at[y, quarter], local_sem)
    own.start()
    for flow in flows[2:]:
        flow.send_core(layers)
    for layer, refs in enumerate(((sf_zero, se_zero), (sf_one, se_one))):
        for which, ref in enumerate(refs):
            first_small[layer, pl.ds(8 * which, 8)] = ref[...]
    small_x = [(k, send(first_small, got.at[k - 1], at.at_x(k))) for k in (1, 3, 2)]
    for copy in halves:
        copy.wait()

    def slot(t):
        for n in range(PAIRS):
            for m in (2 * n, 2 * n + 1):
                flow, stage = flows[m], t - n
                if stage == 0:
                    flow.begin(bufs.at[m], ones.at[m], tails.at[m])
                elif 0 < stage < 7:
                    (flow.relay, flow.second, flow.back, flow.beside, flow.share, flow.share_rest)[stage - 1]()

    slot(0)
    own.wait()
    for k, index in home:
        landed(index, back.at[(y + 4 - k) % 4, quarter])
    outer = RingGather(
        copies, x, at.at_x(1), at.at_x(3),
        lambda j: back.at[:, rows(64 * j, 64)],
        lambda j, h: back.at[pl.ds(2 * h, 2), rows(64 * j, 64)],
    )
    outer.start()
    slot(1)
    slot(2)
    outer.relay()
    for k, index in small_x:
        landed(index, got.at[k - 1])
    of_norms = lax.broadcasted_iota(jnp.int32, first_small.shape, 1) % 8 < 2
    others = got[0] + got[1] + got[2]
    small_out[...] = first_small[...] + jnp.where(of_norms, others, 0.0)
    small_z = [(k, send(small_out, got.at[2 + k], at.at_z(k))) for k in (1, 3, 2)]
    slot(3)
    for k, index in small_z:
        landed(index, got.at[2 + k])
    for k, index in small_z:
        copies.started[index].wait_send()
    small_out[...] = small_out[...] + (got[3] + got[4] + got[5])
    small_y = [(k, send(small_out, got.at[5 + k], at.at_y(k))) for k in (1, 3, 2)]
    slot(4)
    slot(5)
    for k, index in small_y:
        landed(index, got.at[5 + k])
    for k, index in small_y:
        copies.started[index].wait_send()
    small_out[...] = small_out[...] + (got[6] + got[7] + got[8])
    small_c = send(small_out, got.at[9], at.sibling())
    slot(6)
    landed(small_c, got.at[9])
    copies.started[small_c].wait_send()
    small_out[...] = small_out[...] + got[9]
    slot(7)
    slot(8)
    outer.finish()
    for flow in flows:
        flow.end()
    waited = {index for _, index in small_z} | {index for _, index in small_y} | {small_c}
    for index, copy in enumerate(copies.started):
        if index not in waited:
            copy.wait_send()


FINAL_COPIES = 160


def final(grads, small, last):
    vmem = pl.BlockSpec(memory_space=pltpu.VMEM)
    return pl.pallas_call(
        final_kernel,
        out_shape=[
            jax.ShapeDtypeStruct((GRAD_ROWS, WIDTH), bf16),
            jax.ShapeDtypeStruct((2, 16, WIDTH), f32),
            jax.ShapeDtypeStruct((4, BLOCK, WIDTH), bf16),
        ],
        in_specs=[pl.BlockSpec(memory_space=pl.ANY)] * 4 + [vmem] * 6 + [pl.BlockSpec(memory_space=pl.ANY)] * 4 + [vmem],
        out_specs=[vmem] * 3,
        scratch_shapes=[
            pltpu.VMEM((2, 1152, WIDTH), bf16),
            pltpu.VMEM((2, 1152, WIDTH), bf16),
            pltpu.VMEM((2 * PAIRS, 576, LANES), bf16),
            pltpu.VMEM((2 * PAIRS, 6, 288, LANES), bf16),
            pltpu.VMEM((2 * PAIRS, 3, 144, LANES), bf16),
            pltpu.VMEM((10, 2, 16, WIDTH), f32),
            pltpu.VMEM((2, 16, WIDTH), f32),
            pltpu.VMEM((128, WIDTH), f32),
            pltpu.VMEM((128, WIDTH), f32),
            pltpu.VMEM((128, 128), f32),
            pltpu.VMEM((128, WIDTH), f32),
            pltpu.VMEM((2, 2, 64, WIDTH), bf16),
            pltpu.SemaphoreType.DMA((FINAL_COPIES,)),
            pltpu.SemaphoreType.DMA((FINAL_COPIES,)),
            pltpu.SemaphoreType.DMA,
            pltpu.SemaphoreType.DMA((4,)),
            pltpu.SemaphoreType.DMA((8,)),
        ],
        compiler_params=pltpu.CompilerParams(
            collective_id=3, has_side_effects=True, vmem_limit_bytes=VMEM_LIMIT
        ),
        name="final",
    )(*grads, *small, *last)


def nn(a, b):
    return lax.dot_general(a, b, (((1,), (0,)), ((), ())), preferred_element_type=f32)


def nt(a, b):
    return lax.dot_general(a, b, (((1,), (1,)), ((), ())), preferred_element_type=f32)


def tn(a, b):
    return lax.dot_general(a, b, (((0,), (0,)), ((), ())), preferred_element_type=f32)


def turner():
    c = lax.broadcasted_iota(jnp.int32, (INNER, INNER), 0)
    r = lax.broadcasted_iota(jnp.int32, (INNER, INNER), 1)
    lane = c % HEAD_DIM
    half = ROT // 2
    minus = (lane < half) & (r == c + half)
    plus = (lane >= half) & (lane < ROT) & (r == c - half)
    return jnp.where(plus, 1.0, jnp.where(minus, -1.0, 0.0)).astype(bf16)


def head_lanes(shape, h):
    lane = lax.broadcasted_iota(jnp.int32, shape, len(shape) - 1)
    return (lane >= h * HEAD_DIM) & (lane < (h + 1) * HEAD_DIM)


def pick(value, h):
    return jnp.where(head_lanes(value.shape, h), value, jnp.zeros_like(value))


def chunk_rows(i):
    return pl.ds(pl.multiple_of(i * BLOCK, BLOCK), BLOCK)


def gather_keys(own, other, keys, values):
    for n, ref in enumerate((keys, values)):
        ref[0:BLOCK] = own[n, 0:BLOCK]
        ref[BLOCK : 2 * BLOCK] = other[n, 0:BLOCK]
        ref[2 * BLOCK : 3 * BLOCK] = own[n, BLOCK : 2 * BLOCK]
        ref[3 * BLOCK : 4 * BLOCK] = other[n, BLOCK : 2 * BLOCK]


def key_places(c, shape, dim, blocks):
    i = lax.broadcasted_iota(jnp.int32, shape, dim)
    place = jnp.where(i < BLOCK, i + BLOCK * c, i - BLOCK * c)
    if blocks == 4:
        late = jnp.where(i < 3 * BLOCK, i + BLOCK * c, i - BLOCK * c)
        place = jnp.where(i < 2 * BLOCK, place, late)
    return place


SPANS = ((0, 2), (1, 4))


ROWS = 2 * BLOCK


def shape_of(*dims, dtype=f32):
    return jax.ShapeDtypeStruct(dims, dtype)


def norm_back(scaled, normed, inverse):
    inner = scaled - jnp.mean(scaled, axis=-1, keepdims=True)
    inner = inner - normed * jnp.mean(scaled * normed, axis=-1, keepdims=True)
    return inner * inverse


class Env:
    def __init__(self, refs, ins, outs, scratch, raw):
        refs = list(refs)
        sources = {name: refs.pop(0) for name in ins}
        self.raw = types.SimpleNamespace(**{name: refs.pop(0) for name in raw})
        self.targets = {name: refs.pop(0) for name in outs}
        self.v = types.SimpleNamespace(**{name: refs.pop(0) for name in list(ins) + list(outs) + list(scratch)})
        self.send_sems, self.recv_sems, load_sems, self.store_sems, self.local_sems = refs
        self.held = [getattr(self.v, name) for name in ins]
        self.kept = [getattr(self.v, name) for name in outs]
        self.targets = list(self.targets.values())
        self.loads, self.stores = [], []
        for n, name in enumerate(ins):
            source, index = sources[name], ins[name][1]
            source = source if index is None else source.at[index]
            copy = pltpu.make_async_copy(source, self.held[n], load_sems.at[n])
            copy.start()
            self.loads.append(copy)

    def need(self, *refs):
        for ref in refs:
            n = [held is ref for held in self.held].index(True)
            if self.loads[n] is not None:
                self.loads[n].wait()
                self.loads[n] = None

    def done(self, *refs):
        for ref in refs:
            n = [kept is ref for kept in self.kept].index(True)
            copy = pltpu.make_async_copy(ref, self.targets[n], self.store_sems.at[n])
            copy.start()
            self.stores.append(copy)

    def close(self):
        assert not any(self.loads) and len(self.stores) == len(self.kept)
        for copy in self.stores:
            copy.wait()


def fused(body, name, ins, outs, scratch, copies, collective_id, raw={}, local_copies=1):
    def kernel(*refs):
        env = Env(refs, ins, outs, scratch, raw)
        body(env)
        env.close()

    any_space = pl.BlockSpec(memory_space=pl.ANY)
    arrays = [array for array, _ in ins.values()] + list(raw.values())
    held = [pltpu.VMEM(array.shape if index is None else array.shape[1:], array.dtype) for array, index in ins.values()]
    kept = [pltpu.VMEM(s.shape, s.dtype) for s in list(outs.values()) + list(scratch.values())]
    got = pl.pallas_call(
        kernel,
        out_shape=list(outs.values()),
        in_specs=[any_space] * len(arrays),
        out_specs=[any_space] * len(outs),
        scratch_shapes=held
        + kept
        + [
            pltpu.SemaphoreType.DMA((copies,)),
            pltpu.SemaphoreType.DMA((copies,)),
            pltpu.SemaphoreType.DMA((len(ins),)),
            pltpu.SemaphoreType.DMA((len(outs),)),
            pltpu.SemaphoreType.DMA((local_copies,)),
        ],
        compiler_params=pltpu.CompilerParams(
            collective_id=collective_id, has_side_effects=True, vmem_limit_bytes=VMEM_LIMIT
        ),
        name=name,
    )(*arrays)
    return types.SimpleNamespace(**dict(zip(outs, got)))


def block_sum(at, copies, part, bufs, block):
    return RingSum(
        copies, at.x, at.at_x(1), at.at_x(3),
        lambda j, h: part.at[block, rows(64 * j, 64), pl.ds(384 * h, 384)],
        [bufs.at[block, 0], bufs.at[block, 1]], [bufs.at[block, 2], bufs.at[block, 3]],
        [bufs.at[block, 4], bufs.at[block, 5]],
    )


def block_gather(at, copies, out, block):
    return RingGather(
        copies, at.x, at.at_x(1), at.at_x(3),
        lambda j: out.at[block, rows(64 * j, 64)],
        lambda j, h: out.at[block, rows(64 * j, 64), pl.ds(384 * h, 384)],
    )


def sum_out(at, out, block):
    return lambda h: out.at[block, rows(64 * at.x, 64), pl.ds(384 * h, 384)]


def piece_out(out, block):
    return lambda h: out.at[block, :, pl.ds(384 * h, 384)]


def forward_body(later, env):
    at, v = Place(), env.v
    greet([at.sibling()] if later else [at.sibling(), at.at_x(1), at.at_x(3)])
    copies = Copies(env.send_sems, env.recv_sems, at.sibling())
    forward_steps(
        later, at, copies, v, env.done,
        lambda: env.need(v.wq, v.small, v.x, v.cos, v.sin, v.add, v.before),
        lambda: env.need(v.up),
        lambda: env.need(v.dense, v.down, v.starts),
    )
    copies.drain()


def forward_steps(later, at, copies, v, done, for_front, for_feed, for_mix):
    for_front()
    wq, wt, small = v.wq, v.wt, v.small
    turn = turner()
    for i in range(2):
        wt[INNER * i : INNER * (i + 1)] = nn(turn, wq[INNER * i : INNER * (i + 1)]).astype(bf16)

    def row(i, wide=WIDTH):
        return small[i : i + 1, :wide]

    def front(i, carry):
        here = chunk_rows(i)
        x = v.x[i].astype(f32)
        if later:
            x = x + (v.add[i].astype(f32) + v.before[8:9])
            v.middle[here] = x
        centred = x - jnp.mean(x, axis=-1, keepdims=True)
        inverse = lax.rsqrt(jnp.mean(centred * centred, axis=-1, keepdims=True) + EPS)
        normed = centred * inverse
        v.normed[here] = normed
        v.inverse[here] = jnp.broadcast_to(inverse, (BLOCK, 128))
        first = (normed * row(0) + row(1)).astype(bf16)
        v.first[here] = first
        v.second[here] = (normed * row(2) + row(3)).astype(bf16)
        cosine, sine = v.cos[here], v.sin[here]
        query = (nt(first, wq[:INNER]) + row(4, INNER)) * cosine
        query = query + (nt(first, wt[:INNER]) + row(9, INNER)) * sine
        v.query[here] = (query * HEAD_DIM ** (-0.5)).astype(bf16)
        key = (nt(first, wq[INNER : 2 * INNER]) + row(5, INNER)) * cosine
        key = key + (nt(first, wt[INNER:]) + row(10, INNER)) * sine
        v.own[0, here] = key.astype(bf16)
        v.own[1, here] = (nt(first, wq[2 * INNER :]) + row(6, INNER)).astype(bf16)
        return carry

    lax.fori_loop(0, 2, front, 0)
    swap = copies.send(v.own, v.other, at.sibling())
    done(v.normed, v.inverse, v.first, v.second, v.query, v.own)
    if later:
        done(v.middle)
    for_feed()

    def feed(i, carry):
        here = pl.ds(pl.multiple_of(i * 128, 128), 128)
        hidden = nn(v.second[here], v.up[...]) + row(7)
        below = 0.5 + 0.5 * lax.erf(hidden * (0.5**0.5))
        v.active[here] = (hidden * below).astype(bf16)
        density = jnp.exp(-0.5 * hidden * hidden) * 0.3989422804014327
        v.slope[here] = (below + hidden * density).astype(bf16)
        return carry

    lax.fori_loop(0, 4, feed, 0)
    done(v.active, v.slope)
    copies.landed(swap, v.other)
    done(v.other)
    keys, values, bias, logs = v.keys, v.values, v.bias, v.logs
    gather_keys(v.own, v.other, keys, values)
    logs[...] = jnp.zeros_like(logs)
    for_mix()
    sums = {}
    for block, span in reversed(SPANS):
        here, n = pl.ds(block * BLOCK, BLOCK), span * BLOCK
        place = key_places(at.c, (BLOCK, n), 1, span)
        mine = lax.broadcasted_iota(jnp.int32, (BLOCK, n), 0) + (2 * block + at.c) * BLOCK
        allowed = (place <= mine) & (place >= v.starts[here])
        bias[:, :n] = jnp.where(allowed, 0.0, MASKED)
        query = v.query[here]
        mixed = jnp.zeros((BLOCK, INNER), f32)
        for h in range(HEADS):
            score = nt(pick(query, h), keys[:n]) + bias[:, :n]
            top = jnp.max(score, axis=-1, keepdims=True)
            expo = jnp.exp(score - top)
            total = jnp.sum(expo, axis=-1, keepdims=True)
            logs[here, h : h + 1] = top + jnp.log(total)
            mixed = mixed + pick(nn(expo.astype(bf16), values[:n]) * (1.0 / total), h)
        mixed = mixed.astype(bf16)
        v.mixed[here] = mixed
        v.part[block] = (nn(mixed, v.dense[...]) + nn(v.active[here], v.down[...])).astype(bf16)
        if not later:
            sums[block] = block_sum(at, copies, v.part, v.bufs, block)
            sums[block].start()
    v.log[...] = logs[...].T
    done(v.mixed, v.log)
    if later:
        done(v.part)
    else:
        reduce_and_gather(at, copies, sums, v.total, ())
        done(v.total)


def reduce_and_gather(at, copies, sums, out, between):
    between = list(between)

    def work():
        if between:
            between.pop(0)()

    work()
    sums[1].relay()
    work()
    sums[0].relay()
    work()
    gathers = {}
    for block in (1, 0):
        sums[block].finish(sum_out(at, out, block))
        gathers[block] = block_gather(at, copies, out, block)
        gathers[block].start()
        work()
    for block in (1, 0):
        gathers[block].relay()
        work()
    for block in (1, 0):
        gathers[block].finish()


def backward_body(later, env):
    at, v = Place(), env.v
    greet([at.sibling(), at.at_x(1), at.at_x(3)])
    copies = Copies(env.send_sems, env.recv_sems, at.sibling())
    extra = []
    if later:
        env.need(v.part)
        extra = [block_sum(at, copies, v.part, v.part_bufs, block) for block in (1, 0)]
        for ring in extra:
            ring.start()
        env.need(v.g)
        low = v.g
    else:
        env.need(v.g, v.add, v.n_one, v.inv_one)
        low = v.low

        def incoming(i, carry):
            here = chunk_rows(i)
            grad = v.g[i].astype(f32) + norm_back(
                v.add[i].astype(f32), v.n_one[here], v.inv_one[here, 0:1]
            )
            v.grad[here] = grad
            low[i] = grad.astype(bf16)
            return carry

        lax.fori_loop(0, 2, incoming, 0)
        env.done(v.grad)
    keys, values, bias, inner = v.keys, v.values, v.bias, v.inner
    env.need(v.own, v.other, v.query, v.mixed, v.log, v.dense, v.starts)
    gather_keys(v.own, v.other, keys, values)
    inner[...] = jnp.zeros_like(inner)
    dkeys, dvalues, log = v.dkeys, v.dvalues, v.log
    for block, span in reversed(SPANS):
        here, n = pl.ds(block * BLOCK, BLOCK), span * BLOCK
        place = key_places(at.c, (n, BLOCK), 0, span)
        mine = lax.broadcasted_iota(jnp.int32, (n, BLOCK), 1) + (2 * block + at.c) * BLOCK
        allowed = (place <= mine) & (place >= v.starts[0:1, here])
        bias[:n] = jnp.where(allowed, 0.0, MASKED)
        d_mixed = nt(low[block], v.dense[...]).astype(bf16)
        product = d_mixed.astype(f32) * v.mixed[here].astype(f32)
        for h in range(HEADS):
            inner[:, h : h + 1] = jnp.sum(pick(product, h), axis=-1, keepdims=True)
        inner_rows = inner[...].T
        query = v.query[here]
        d_query = jnp.zeros((BLOCK, INNER), f32)
        for h in range(HEADS):
            mine_q, mine_d = pick(query, h), pick(d_mixed, h)
            prob = jnp.exp(nt(keys[:n], mine_q) + bias[:n] - log[h : h + 1, here])
            d_prob = nt(values[:n], mine_d)
            d_score = (prob * (d_prob - inner_rows[h : h + 1])).astype(bf16)
            d_value = nn(prob.astype(bf16), mine_d)
            d_key = nn(d_score, mine_q)
            if span == 4 and h == 0:
                dvalues[...] = d_value
                dkeys[...] = d_key
            else:
                dvalues[:n] += d_value
                dkeys[:n] += d_key
            d_query = d_query + pick(tn(d_score, keys[:n]), h)
        v.d_query[here] = d_query * HEAD_DIM ** (-0.5)
    for n, ref in enumerate((dkeys, dvalues)):
        v.d_other[n, 0:BLOCK] = ref[BLOCK : 2 * BLOCK].astype(bf16)
        v.d_other[n, BLOCK : 2 * BLOCK] = ref[3 * BLOCK : 4 * BLOCK].astype(bf16)
    swap = copies.send(v.d_other, v.got, at.sibling())
    for ring in extra:
        ring.relay()

    small, hid, normed = v.small, v.hid, v.normed
    sums_one, sums_two = v.sums_one, v.sums_two
    sums_one[...] = jnp.zeros_like(sums_one)
    sums_two[...] = jnp.zeros_like(sums_two)
    env.need(v.down, v.up, v.small, v.slope, v.normed)

    def feed(i, carry):
        here = chunk_rows(i)
        g = low[i]
        d_hidden = (nt(g, v.down[...]) * v.slope[here].astype(f32)).astype(bf16)
        hid[here] = d_hidden
        d_second = nt(d_hidden, v.up[...])
        v.e_two[here] = d_second * small[2:3]
        sums_two[0:1] += jnp.sum(d_second * normed[here], axis=0, keepdims=True)
        sums_two[1:2] += jnp.sum(d_second, axis=0, keepdims=True)
        sums_two[2:3] += jnp.sum(g.astype(f32), axis=0, keepdims=True)
        sums_two[3:4] += jnp.sum(d_hidden.astype(f32), axis=0, keepdims=True)
        return carry

    lax.fori_loop(0, 2, feed, 0)
    env.done(v.sums_two)
    for ring, block in zip(extra, (1, 0)):
        ring.finish(piece_out(v.part_sum, block))
    if later:
        env.done(v.part_sum)

    env.need(v.cos, v.sin, v.wq, v.first, v.second, v.active)
    turn = turner()
    wq, packed, got = v.wq, v.packed, v.got

    def unrotate(value, cosine, sine):
        moved = value * sine
        high = moved.astype(bf16)
        lower = (moved - high.astype(f32)).astype(bf16)
        return value * cosine + (nn(high, turn) + nn(lower, turn))

    copies.landed(swap, got)
    sums = {}
    for i in (1, 0):
        here = pl.ds(i * BLOCK, BLOCK)
        there = pl.ds(2 * i * BLOCK, BLOCK)
        cosine, sine = v.cos[here], v.sin[here]
        parts = [
            unrotate(v.d_query[here], cosine, sine),
            unrotate(dkeys[there] + got[0, here].astype(f32), cosine, sine),
            dvalues[there] + got[1, here].astype(f32),
        ]
        d_first = jnp.zeros((BLOCK, WIDTH), f32)
        for n, part in enumerate(parts):
            part = part.astype(bf16)
            packed[n, here] = part
            d_first = d_first + nn(part, wq[INNER * n : INNER * (n + 1)])
            sums_one[2 + n : 3 + n, :INNER] += jnp.sum(part.astype(f32), axis=0, keepdims=True)
        v.e[i] = (d_first * small[0:1] + v.e_two[here]).astype(bf16)
        sums[i] = block_sum(at, copies, v.e, v.bufs, i)
        sums[i].start()
        sums_one[0:1] += jnp.sum(d_first * normed[here], axis=0, keepdims=True)
        sums_one[1:2] += jnp.sum(d_first, axis=0, keepdims=True)
    env.done(v.sums_one)

    grads_one, grads_two = v.grads_one, v.grads_two

    def grad_dense():
        grads_two[:INNER] = tn(v.mixed[...], low[...].reshape(ROWS, WIDTH)).astype(bf16)

    def grad_up():
        grads_two[INNER : INNER + WIDTH] = tn(v.second[...], hid[...]).astype(bf16)

    def grad_down():
        grads_two[INNER + WIDTH :] = tn(v.active[...], low[...].reshape(ROWS, WIDTH)).astype(bf16)

    def grad_packed():
        for n in range(3):
            grads_one[INNER * n : INNER * (n + 1)] = tn(packed[n], v.first[...]).astype(bf16)

    if later:
        reduce_and_gather(at, copies, sums, v.total, (grad_dense, grad_packed, grad_up, grad_down))
        env.done(v.total)
    else:
        grad_dense()
        sums[1].relay()
        grad_packed()
        sums[0].relay()
        grad_up()
        grad_down()
        for block in (1, 0):
            sums[block].finish(piece_out(v.total, block))
        env.done(v.total)
    env.done(v.grads_one, v.grads_two)
    copies.drain()


def low_shape(*dims):
    return shape_of(*dims, dtype=bf16)


def forward_outs():
    return dict(
        normed=shape_of(ROWS, WIDTH), inverse=shape_of(ROWS, 128), first=low_shape(ROWS, WIDTH),
        second=low_shape(ROWS, WIDTH), query=low_shape(ROWS, INNER), own=low_shape(2, ROWS, INNER),
        other=low_shape(2, ROWS, INNER), active=low_shape(ROWS, WIDTH), slope=low_shape(ROWS, WIDTH),
        mixed=low_shape(ROWS, INNER), log=shape_of(128, ROWS),
    )


def forward_scratch():
    return dict(
        wt=low_shape(2 * INNER, WIDTH), keys=low_shape(SEQ, INNER), values=low_shape(SEQ, INNER),
        logs=shape_of(ROWS, 128), bias=shape_of(BLOCK, SEQ),
    )


def start_layer(boundary, segment_ids, vectors, wq, wd, wu, wn):
    ins = dict(raw_q=(wq, None))
    ins.update({name: (array, None) for name, array in vectors.items()})
    ins.update(segment_ids=(segment_ids, None))
    outs = dict(
        wq=low_shape(2, 3 * INNER, WIDTH), wu=low_shape(2, WIDTH, WIDTH), wd=low_shape(2, INNER, WIDTH),
        wn=low_shape(2, WIDTH, WIDTH), smalls=shape_of(2, 16, WIDTH), xg=low_shape(2, 2, BLOCK, WIDTH),
        cos=shape_of(ROWS, INNER), sin=shape_of(ROWS, INNER), start_col=shape_of(ROWS, 1, dtype=jnp.int32),
        start_row=shape_of(1, ROWS, dtype=jnp.int32), total=low_shape(2, BLOCK, WIDTH), **forward_outs(),
    )
    scratch = dict(
        quarters=shape_of(4, 64, WIDTH), quarters_low=low_shape(4, 64, WIDTH), block=shape_of(BLOCK, WIDTH),
        vectors=shape_of(16, WIDTH), part=low_shape(2, BLOCK, WIDTH), bufs=low_shape(2, 6, 64, 384),
        **forward_scratch(),
    )
    raw = dict(boundary=boundary, up=wu, dense=wd, down=wn)
    return fused(start_body, "start", ins, outs, scratch, 52 + 21, 0, raw, 5)


def forward_layer(layer, xg, add, stacks, tables):
    wq, wd, wu, wn, small = stacks
    cosine, sine, start_col, _ = tables
    ins = dict(
        wq=(wq, layer), small=(small, layer), x=(xg, 0), add=(add, None), before=(small, 0), cos=(cosine, None),
        sin=(sine, None), up=(wu, layer), dense=(wd, layer), down=(wn, layer), starts=(start_col, None),
    )
    outs = dict(middle=shape_of(ROWS, WIDTH), part=low_shape(2, BLOCK, WIDTH), **forward_outs())
    return fused(functools.partial(forward_body, True), "forward", ins, outs, forward_scratch(), 1, 5)


def backward_layer(layer, xg, add, stacks, tables, kept, kept_one):
    wq, wd, wu, wn, small = stacks
    cosine, sine, _, start_row = tables
    later = add is None
    if later:
        ins = dict(part=(kept.part, None), g=(xg, 1))
    else:
        ins = dict(
            g=(xg, 1), add=(add, None), n_one=(kept_one.normed, None), inv_one=(kept_one.inverse, None)
        )
    ins.update(
        own=(kept.own, None), other=(kept.other, None), query=(kept.query, None), mixed=(kept.mixed, None),
        log=(kept.log, None),
    )
    ins.update(dense=(wd, layer), starts=(start_row, None), down=(wn, layer), up=(wu, layer), small=(small, layer))
    ins.update(slope=(kept.slope, None), normed=(kept.normed, None))
    ins.update(cos=(cosine, None), sin=(sine, None), wq=(wq, layer))
    ins.update(first=(kept.first, None), second=(kept.second, None), active=(kept.active, None))
    outs = dict(
        grads_one=low_shape(3 * INNER, WIDTH), grads_two=low_shape(INNER + 2 * WIDTH, WIDTH),
        sums_one=shape_of(8, WIDTH), sums_two=shape_of(8, WIDTH),
    )
    scratch = dict(
        keys=low_shape(SEQ, INNER), values=low_shape(SEQ, INNER), bias=shape_of(SEQ, BLOCK),
        inner=shape_of(BLOCK, 128), dkeys=shape_of(SEQ, INNER), dvalues=shape_of(SEQ, INNER),
        d_query=shape_of(ROWS, INNER), d_other=low_shape(2, ROWS, INNER), got=low_shape(2, ROWS, INNER),
        hid=low_shape(ROWS, WIDTH), e_two=shape_of(ROWS, WIDTH), packed=low_shape(3, ROWS, INNER),
        e=low_shape(2, BLOCK, WIDTH), bufs=low_shape(2, 6, 64, 384),
    )
    if later:
        outs.update(total=low_shape(2, BLOCK, WIDTH), part_sum=shape_of(2, 64, WIDTH))
        scratch.update(part_bufs=low_shape(2, 6, 64, 384))
    else:
        outs.update(total=shape_of(2, 64, WIDTH), grad=shape_of(ROWS, WIDTH))
        scratch.update(low=low_shape(2, BLOCK, WIDTH))
    return fused(
        functools.partial(backward_body, later), "backward", ins, outs, scratch, 33 if later else 13, 6 if later else 7
    )


def start_body(env):
    at, v, raw = Place(), env.v, env.raw
    p, x, y, z, c = at.p, at.x, at.y, at.z, at.c
    quarter = rows(64 * x, 64)
    local = []

    def bring(source, target):
        copy = pltpu.make_async_copy(source, target, env.local_sems.at[len(local)])
        copy.start()
        local.append(copy)
        return copy

    quarters_in = bring(raw.boundary.at[0, :, quarter], v.quarters)
    up_in = bring(raw.up, v.wu.at[p])
    dense_in = bring(raw.dense, v.wd.at[p])
    down_in = bring(raw.down, v.wn.at[p])
    block_in = bring(raw.boundary.at[0, y], v.block)
    greet(
        [at.at_x(1), at.at_x(3), at.at_y(1), at.at_y(2), at.at_y(3), at.at_z(1), at.at_z(3), at.sibling()]
    )
    copies = Copies(env.send_sems, env.recv_sems, at.at_x(1))

    def piece(ref, zz, cc):
        if ref.shape[-2] == WIDTH:
            return ref.at[rows(192 * zz + 96 * cc, 96)]
        each = ref.shape[-2] // 4
        return ref.at[rows(each * zz, each), pl.ds(pl.multiple_of(384 * cc, 128), 384)]

    def half(ref, zz, cc, h):
        if ref.shape[-2] == WIDTH:
            return ref.at[rows(192 * zz + 96 * cc + 48 * h, 48)]
        each = ref.shape[-2] // 4
        more = (each // 2 + 15) // 16 * 16
        size = each - more if h else more
        return ref.at[rows(each * zz + more * h, size), pl.ds(pl.multiple_of(384 * cc, 128), 384)]

    quarters_in.wait()
    v.quarters_low[...] = v.quarters[...].astype(bf16)
    first = [
        copies.send(v.quarters_low.at[(y + k) % 4], v.xg.at[p, at.low, quarter], at.at_y(k)) for k in (1, 3, 2)
    ]
    env.need(v.raw_q)
    for kind in range(3):
        for h in range(HEADS):
            to, source = INNER * kind + HEAD_DIM * h, INNER * h + HEAD_DIM * kind
            v.wq[p, to : to + HEAD_DIM] = v.raw_q[source : source + HEAD_DIM]
    stacks = [v.wq, v.wu, v.wd, v.wn]
    sent = []
    for stack, copy in zip(stacks, (None, up_in, dense_in, down_in)):
        if copy is not None:
            copy.wait()
        sent.append(copies.send(piece(stack.at[p], z, c), piece(stack.at[p], z, c), at.partner()))
    env.need(v.gain_one, v.shift_one, v.gain_two, v.shift_two, v.qkv_bias, v.dense_bias, v.up_bias, v.down_bias)
    vectors = v.vectors
    vectors[...] = jnp.zeros_like(vectors)
    for n, ref in enumerate((v.gain_one, v.shift_one, v.gain_two, v.shift_two)):
        vectors[n : n + 1] = ref[...]
    turned = ROT // 2
    for kind in range(3):
        for h in range(HEADS):
            source = INNER * h + HEAD_DIM * kind
            part = v.qkv_bias[:, source : source + HEAD_DIM]
            vectors[4 + kind : 5 + kind, pl.ds(HEAD_DIM * h, HEAD_DIM)] = part
            if kind < 2:
                vectors[9 + kind : 10 + kind, pl.ds(HEAD_DIM * h, turned)] = -part[:, turned:ROT]
                vectors[9 + kind : 10 + kind, pl.ds(HEAD_DIM * h + turned, turned)] = part[:, :turned]
    vectors[7:8] = v.up_bias[...]
    vectors[8:9] = v.dense_bias[...] + v.down_bias[...]
    v.smalls[p] = vectors[...]
    sent_small = copies.send(vectors, v.smalls.at[p], at.partner())
    block_in.wait()
    v.xg[p, at.low] = v.block[...].astype(bf16)
    env.need(v.segment_ids)
    labels = v.segment_ids[at.y, pl.ds(at.z, 1)]
    start = jnp.zeros((1, SEQ), f32)
    for label in range(1, 5):
        count = jnp.sum((labels == label - 1).astype(f32), axis=1, keepdims=True)
        start = start + jnp.where(labels >= label, count, 0.0)
    lane = lax.broadcasted_iota(jnp.int32, (1, INNER), 1) % HEAD_DIM
    freqs = jnp.ones((1, INNER), f32)
    for n in range(1, turned):
        freqs = jnp.where(lane % turned == n, 10000.0 ** (-2.0 * n / ROT), freqs)
    angles = []
    for i in range(2):
        pieces = [start[:, BLOCK * (2 * i + k) : BLOCK * (2 * i + k + 1)] for k in range(2)]
        mine = jnp.where(c == 0, pieces[0], pieces[1])
        v.start_row[:, BLOCK * i : BLOCK * (i + 1)] = mine.astype(jnp.int32)
        column = jnp.broadcast_to(mine, (128, BLOCK)).T[:, 0:1]
        v.start_col[BLOCK * i : BLOCK * (i + 1)] = column.astype(jnp.int32)
        spot = lax.broadcasted_iota(jnp.int32, (BLOCK, 1), 0) + (2 * i + c) * BLOCK
        angles.append((spot.astype(f32) - column) * freqs)

    def table(ref, function, rest):
        for i in range(2):
            ref[BLOCK * i : BLOCK * (i + 1)] = jnp.where(lane < ROT, function(angles[i]), rest)

    gathers = []
    for k, index in zip((1, 3, 2), first):
        source = (y + 4 - k) % 4
        slot = v.xg.at[source // 2, source % 2]
        copies.landed(index, slot.at[quarter])
        gather = RingGather(
            copies, x, at.at_x(1), at.at_x(3),
            lambda j, slot=slot: slot.at[rows(64 * j, 64)],
            lambda j, h, slot=slot: slot.at[rows(64 * j + 32 * h, 32)],
        )
        gather.start()
        gathers.append(gather)
    others = [stack.at[1 - p] for stack in stacks]
    rings, shared = [], []

    def share(n, j):
        mine = piece(others[n], j, c)
        shared[n].append((copies.send(mine, mine, at.sibling()), piece(others[n], j, 1 - c)))

    def begin(n):
        other = others[n]
        copies.landed(sent[n], piece(other, z, c))
        ring = RingGather(
            copies, z, at.at_z(1), at.at_z(3),
            lambda j: piece(other, j, c), lambda j, h: half(other, j, c, h),
        )
        ring.start()
        rings.append(ring)
        shared.append([])
        share(n, z)

    def relay(n):
        rings[n].relay()
        share(n, (z + 3) % 4)
        share(n, (z + 1) % 4)

    def finish(n):
        rings[n].finish()
        share(n, (z + 2) % 4)

    def arrived(n):
        for index, view in shared[n]:
            copies.landed(index, view)
        env.done(stacks[n])

    begin(0)
    begin(1)
    table(v.cos, jnp.cos, 1.0)
    begin(2)
    begin(3)
    table(v.sin, jnp.sin, 0.0)
    env.done(v.cos, v.sin, v.start_col, v.start_row)
    for gather in gathers:
        gather.relay()
    relay(0)
    relay(1)

    def for_front():
        finish(0)
        for gather in gathers:
            gather.finish()
        copies.landed(sent_small, v.smalls.at[1 - p])
        relay(2)
        relay(3)
        arrived(0)
        env.done(v.xg, v.smalls)

    def for_feed():
        finish(1)
        finish(2)
        finish(3)
        arrived(1)

    def for_mix():
        arrived(2)
        arrived(3)

    views = types.SimpleNamespace(**vars(v))
    views.wq, views.up, views.dense, views.down = [stack.at[0] for stack in stacks]
    views.small, views.x, views.starts = v.smalls.at[0], v.xg.at[0], v.start_col
    forward_steps(False, at, copies, views, env.done, for_front, for_feed, for_mix)
    copies.drain()


def finish_kernel(
    total, small, back, x_out, g1, s1, g2, s2, qkv_out, qkv_bias, dense_out, dense_bias, up_out, up_bias,
    down_out, down_bias, total_in, back_in, x_hold, qkv_hold, dense_hold, up_hold, down_hold, load_sems, store_sems,
):
    p = lax.axis_index("pipe")
    loads = [pltpu.make_async_copy(back.at[m], back_in.at[m], load_sems.at[m]) for m in range(4)]
    loads += [
        pltpu.make_async_copy(total.at[span], total_in.at[span], load_sems.at[4 + n])
        for n, span in enumerate((pl.ds(1536, 768), pl.ds(480, 672), pl.ds(1152, 384), pl.ds(0, 480)))
    ]
    for copy in loads:
        copy.start()
    stores = []

    def store(source, target):
        copy = pltpu.make_async_copy(source, target, store_sems.at[len(stores)])
        copy.start()
        stores.append(copy)

    for m in range(4):
        loads[m].wait()
        x_hold[m] = back_in[m].astype(f32)
        store(x_hold.at[m], x_out.at[0, m])
    loads[4].wait()
    down_hold[...] = total_in[1536:].astype(f32)
    store(down_hold, down_out.at[0])
    loads[5].wait()
    loads[6].wait()
    up_hold[:672] = total_in[480:1152].astype(f32)
    up_hold[672:] = total_in[1440:1536].astype(f32)
    store(up_hold, up_out.at[0])
    loads[7].wait()
    for h in range(HEADS):
        for kind in range(3):
            to, source = INNER * h + HEAD_DIM * kind, INNER * kind + HEAD_DIM * h
            qkv_bias[:, to : to + HEAD_DIM] = small[p, 2 + kind : 3 + kind, HEAD_DIM * h : HEAD_DIM * (h + 1)]
            for start in (source, source + HEAD_DIM // 2):
                place = start if start < 288 else start - 288 + 1152
                qkv_hold[to + start - source : to + start - source + HEAD_DIM // 2] = total_in[
                    place : place + HEAD_DIM // 2
                ].astype(f32)
    store(qkv_hold, qkv_out.at[0])
    dense_hold[...] = total_in[288:480].astype(f32)
    store(dense_hold, dense_out.at[0])
    for row, ref in ((0, g1), (1, s1), (8, g2), (9, s2), (10, dense_bias), (11, up_bias), (10, down_bias)):
        ref[...] = small[p, row : row + 1]
    for copy in stores:
        copy.wait()


def local(
    boundary,
    segment_ids,
    attn_gain,
    attn_shift,
    mlp_gain,
    mlp_shift,
    qkv_weight,
    qkv_bias,
    dense_weight,
    dense_bias,
    up_weight,
    up_bias,
    down_weight,
    down_bias,
):
    vectors = dict(
        gain_one=attn_gain, shift_one=attn_shift, gain_two=mlp_gain, shift_two=mlp_shift, qkv_bias=qkv_bias,
        dense_bias=dense_bias, up_bias=up_bias, down_bias=down_bias,
    )
    zero = start_layer(
        boundary, segment_ids, vectors, qkv_weight[0].T, dense_weight[0], up_weight[0], down_weight[0]
    )
    xg, stacks = zero.xg, [zero.wq, zero.wd, zero.wu, zero.wn, zero.smalls]
    tables = (zero.cos, zero.sin, zero.start_col, zero.start_row)
    one = forward_layer(1, xg, zero.total, stacks, tables)
    back_one = backward_layer(1, xg, None, stacks, tables, one, one)
    back_zero = backward_layer(0, xg, back_one.total, stacks, tables, zero, one)
    total, small_total, back = final(
        [back_zero.grads_one, back_zero.grads_two, back_one.grads_one, back_one.grads_two],
        [back_zero.sums_one, back_zero.sums_two, back_one.sums_one, back_one.sums_two],
        [
            back_zero.total, back_one.part_sum, back_zero.grad, zero.normed, zero.inverse,
            one.middle, stacks[4],
        ],
    )
    vector = shape_of(1, WIDTH)
    vmem, any_space = pl.BlockSpec(memory_space=pltpu.VMEM), pl.BlockSpec(memory_space=pl.ANY)
    outs = list(
        pl.pallas_call(
            finish_kernel,
            out_shape=[shape_of(1, 4, BLOCK, WIDTH)] + [vector] * 4
            + [shape_of(1, 3 * INNER, WIDTH), shape_of(1, 3 * INNER), shape_of(1, INNER, WIDTH), vector]
            + [shape_of(1, WIDTH, WIDTH), vector] * 2,
            in_specs=[any_space, vmem, any_space],
            out_specs=[any_space] + [vmem] * 4 + [any_space, vmem] * 4,
            scratch_shapes=[
                pltpu.VMEM((GRAD_ROWS, WIDTH), bf16),
                pltpu.VMEM((4, BLOCK, WIDTH), bf16),
                pltpu.VMEM((4, BLOCK, WIDTH), f32),
                pltpu.VMEM((3 * INNER, WIDTH), f32),
                pltpu.VMEM((INNER, WIDTH), f32),
                pltpu.VMEM((WIDTH, WIDTH), f32),
                pltpu.VMEM((WIDTH, WIDTH), f32),
                pltpu.SemaphoreType.DMA((8,)),
                pltpu.SemaphoreType.DMA((8,)),
            ],
            compiler_params=pltpu.CompilerParams(vmem_limit_bytes=VMEM_LIMIT),
            name="finish",
        )(total, small_total, back)
    )
    outs[5] = outs[5].transpose(0, 2, 1)
    return tuple(outs)


def solution(mesh):
    in_specs = (
        P("pipe", None, "dp", None),
        P(),
        P("pipe", None),
        P("pipe", None),
        P("pipe", None),
        P("pipe", None),
        P("pipe", None, "tensor"),
        P("pipe", "tensor"),
        P("pipe", "tensor", None),
        P("pipe", None),
        P("pipe", None, "tensor"),
        P("pipe", "tensor"),
        P("pipe", "tensor", None),
        P("pipe", None),
    )
    out_specs = (
        P("pipe", None, "dp", None),
        P("pipe", None),
        P("pipe", None),
        P("pipe", None),
        P("pipe", None),
        P("pipe", None, "tensor"),
        P("pipe", "tensor"),
        P("pipe", "tensor", None),
        P("pipe", None),
        P("pipe", None, "tensor"),
        P("pipe", "tensor"),
        P("pipe", "tensor", None),
        P("pipe", None),
    )
    return jax.shard_map(local, mesh=mesh, in_specs=in_specs, out_specs=out_specs, check_vma=False)
```

```python
import functools
import types

import jax
import jax.numpy as jnp
from jax import lax
from jax.experimental import pallas as pl
from jax.experimental.pallas import tpu as pltpu
from jax.sharding import PartitionSpec as P

MESH = pl.DeviceIdType.MESH
HEAD_DIM = 64
ROT = 16
EPS = 1e-05
MASKED = -1e30
WIDTH = 768
SEQ = 1024
BLOCK = 256
HEADS = 3
INNER = HEADS * HEAD_DIM
GRAD_ROWS = 2304
bf16 = jnp.bfloat16
f32 = jnp.float32
VMEM_LIMIT = 56 * 1024 * 1024


class Place:
    def __init__(self):
        self.p = lax.axis_index("pipe")
        self.d = lax.axis_index("dp")
        self.x = lax.axis_index("tensor")
        self.z = self.d // 4
        self.low = (self.d // 2) % 2
        self.c = self.d % 2
        self.y = 2 * self.p + self.low

    def at_x(self, steps):
        return (self.p, self.d, (self.x + steps) % 4)

    def at_y(self, steps):
        y = (self.y + steps) % 4
        return (y // 2, self.z * 4 + (y % 2) * 2 + self.c, self.x)

    def at_z(self, steps):
        return (self.p, ((self.z + steps) % 4) * 4 + self.d % 4, self.x)

    def sibling(self):
        return (self.p, self.d + 1 - 2 * self.c, self.x)

    def partner(self):
        return (1 - self.p, self.z * 4 + (1 - self.low) * 2 + self.c, self.x)

    def beside(self):
        return (self.p, self.z * 4 + (1 - self.low) * 2 + self.c, self.x)


def greet(devices):
    barrier = pltpu.get_barrier_semaphore()
    for device in devices:
        pl.semaphore_signal(barrier, inc=1, device_id=device, device_id_type=MESH)
    pl.semaphore_wait(barrier, len(devices))


class Copies:
    def __init__(self, send_sems, recv_sems, somebody):
        self.send_sems, self.recv_sems = send_sems, recv_sems
        self.somebody = somebody
        self.count = 0
        self.started = []

    def send(self, src, dst, device):
        k = self.count
        self.count += 1
        copy = pltpu.make_async_remote_copy(
            src_ref=src,
            dst_ref=dst,
            send_sem=self.send_sems.at[k],
            recv_sem=self.recv_sems.at[k],
            device_id=device,
            device_id_type=MESH,
        )
        copy.start()
        self.started.append(copy)
        return k

    def landed(self, k, dst):
        pltpu.make_async_remote_copy(
            src_ref=dst,
            dst_ref=dst,
            send_sem=self.send_sems.at[k],
            recv_sem=self.recv_sems.at[k],
            device_id=self.somebody,
            device_id_type=MESH,
        ).wait_recv()

    def sent(self, which):
        for k in which:
            self.started[k].wait_send()
            self.started[k] = None

    def drain(self):
        for copy in self.started:
            if copy is not None:
                copy.wait_send()


class RingSum:
    def __init__(self, copies, me, right, left, chunk, relay, direct, final):
        self.copies, self.me, self.right, self.left = copies, me, right, left
        self.chunk, self.relay_in, self.direct, self.final = chunk, relay, direct, final

    def start(self):
        me, send = self.me, self.copies.send
        far, after, before = (me + 2) % 4, (me + 1) % 4, (me + 3) % 4
        self.k = [
            send(self.chunk(far, 0), self.relay_in[0], self.right),
            send(self.chunk(far, 1), self.relay_in[1], self.left),
            send(self.chunk(after, 1), self.direct[1], self.right),
            send(self.chunk(before, 0), self.direct[0], self.left),
        ]

    def relay(self):
        me, copies = self.me, self.copies
        after, before = (me + 1) % 4, (me + 3) % 4
        copies.landed(self.k[0], self.relay_in[0])
        add_into(self.relay_in[0], self.chunk(after, 0))
        k0 = copies.send(self.relay_in[0], self.final[0], self.right)
        copies.landed(self.k[1], self.relay_in[1])
        add_into(self.relay_in[1], self.chunk(before, 1))
        k1 = copies.send(self.relay_in[1], self.final[1], self.left)
        self.k += [k0, k1]

    def finish(self, out):
        copies = self.copies
        copies.landed(self.k[3], self.direct[0])
        copies.landed(self.k[4], self.final[0])
        store_sum(out(0), self.chunk(self.me, 0), self.direct[0], self.final[0])
        copies.landed(self.k[2], self.direct[1])
        copies.landed(self.k[5], self.final[1])
        store_sum(out(1), self.chunk(self.me, 1), self.direct[1], self.final[1])


class RingGather:
    def __init__(self, copies, me, right, left, piece, halves):
        self.copies, self.me, self.right, self.left = copies, me, right, left
        self.piece, self.halves = piece, halves

    def start(self):
        mine = self.piece(self.me)
        self.k = [
            self.copies.send(mine, mine, self.right),
            self.copies.send(mine, mine, self.left),
        ]

    def relay(self):
        before, after = (self.me + 3) % 4, (self.me + 1) % 4
        self.copies.landed(self.k[0], self.piece(before))
        view = self.halves(before, 0)
        k0 = self.copies.send(view, view, self.right)
        self.copies.landed(self.k[1], self.piece(after))
        view = self.halves(after, 1)
        k1 = self.copies.send(view, view, self.left)
        self.k += [k0, k1]

    def finish(self):
        far = (self.me + 2) % 4
        self.copies.landed(self.k[2], self.halves(far, 0))
        self.copies.landed(self.k[3], self.halves(far, 1))


class DirectSum:
    def __init__(self, copies, me, to, chunk, bufs):
        self.copies, self.me, self.to, self.chunk, self.bufs = copies, me, to, chunk, bufs

    def start(self):
        self.k = [
            self.copies.send(self.chunk((self.me + k) % 4), self.bufs[k - 1], self.to(k)) for k in (1, 3, 2)
        ]

    def finish(self, out):
        for index, k in zip(self.k, (1, 3, 2)):
            self.copies.landed(index, self.bufs[k - 1])
        store_sum(out, self.chunk(self.me), *self.bufs)


class DirectGather:
    def __init__(self, copies, me, to, piece):
        self.copies, self.me, self.to, self.piece = copies, me, to, piece

    def start(self):
        mine = self.piece(self.me)
        self.k = [self.copies.send(mine, mine, self.to(k)) for k in (1, 3, 2)]

    def finish(self):
        for index, k in zip(self.k, (1, 3, 2)):
            self.copies.landed(index, self.piece((self.me + 4 - k) % 4))


def add_into(ref, other):
    ref[...] = (ref[...].astype(f32) + other[...].astype(f32)).astype(ref.dtype)


def store_sum(out, *parts):
    total = parts[0][...].astype(f32)
    for part in parts[1:]:
        total = total + part[...].astype(f32)
    out[...] = total.astype(out.dtype)


def rows(start, size, step=16):
    return pl.ds(pl.multiple_of(start, step), size)


GROUPS = ((0, 384, True), (640, 256, False), (384, 256, True), (896, 256, False))
HALF_ROWS = GRAD_ROWS // 2
F_ROWS, E_ROWS = 288, 864
FLOW_COPIES = 80
SLOTS = 9


class GradFlow:
    def __init__(self, at, copies, sources, chip, own, out, group, bufs, one, tail):
        self.at, self.copies, self.sources = at, copies, sources
        self.chip, self.own, self.out = chip, own, out
        self.start, self.count, y_first = group
        self.chunk, self.part = self.count // 4, self.count // 8
        self.bufs, self.one, self.tail = bufs, one, tail
        over_y, over_z = (at.y, at.at_y), (at.z, at.at_z)
        (self.a, self.to_a), (self.b, self.to_b) = (over_y, over_z) if y_first else (over_z, over_y)
        self.base, self.other_base = HALF_ROWS * at.c + self.start, HALF_ROWS * (1 - at.c) + self.start

    def pieces(self, core):
        first, end = self.start, self.start + self.count
        f, e = self.sources
        found = []
        if first < F_ROWS:
            found.append((f.at[rows(F_ROWS * core + first, F_ROWS - first)], pl.ds(first, F_ROWS - first)))
            first = F_ROWS
        found.append((e.at[rows(E_ROWS * core + first - F_ROWS, end - first)], pl.ds(first, end - first)))
        return found

    def send_core(self):
        self.core = []
        for src, place in self.pieces(1 - self.at.c):
            dst = self.chip.at[place]
            self.core.append((self.copies.send(src, dst, self.at.sibling()), dst))

    def quarter(self, ref, start, j):
        return ref.at[rows(start + self.part * (j // 2), self.part), pl.ds(pl.multiple_of(384 * (j % 2), 128), 384)]

    def begin(self):
        chip, own, bufs = self.chip, self.own, self.bufs
        for index, dst in self.core:
            self.copies.landed(index, dst)

        def body(i, carry):
            here = rows(self.start + i * 128, 128)
            chip[here] = (chip[here].astype(f32) + own[here].astype(f32)).astype(bf16)
            return carry

        lax.fori_loop(0, self.count // 128, body, 0)
        self.ring = RingSum(
            self.copies, self.a, self.to_a(1), self.to_a(3),
            lambda j, h: chip.at[rows(self.start + self.chunk * j + self.part * h, self.part)],
            [bufs.at[0], bufs.at[1]], [bufs.at[2], bufs.at[3]], [bufs.at[4], bufs.at[5]],
        )
        self.ring.start()

    def relay(self):
        self.ring.relay()

    def second(self):
        one, tail = self.one, self.tail
        self.ring.finish(lambda h: one.at[pl.ds(self.part * h, self.part)])
        self.sum = DirectSum(
            self.copies, self.b, self.to_b, lambda j: self.quarter(one, 0, j), [tail.at[n] for n in range(3)]
        )
        self.sum.start()

    def back(self):
        start = self.base + self.chunk * self.a
        self.sum.finish(self.quarter(self.out, start, self.b))
        self.gather = DirectGather(self.copies, self.b, self.to_b, lambda j: self.quarter(self.out, start, j))
        self.gather.start()

    def whole(self):
        self.gather.finish()
        out = self.out
        self.ring = RingGather(
            self.copies, self.a, self.to_a(1), self.to_a(3),
            lambda j: out.at[rows(self.base + self.chunk * j, self.chunk)],
            lambda j, h: out.at[rows(self.base + self.chunk * j + self.part * h, self.part)],
        )
        self.ring.start()

    def share(self):
        self.ring.finish()
        view = self.out.at[rows(self.base, self.count)]
        self.shared = self.copies.send(view, view, self.at.sibling())

    def end(self):
        self.copies.landed(self.shared, self.out.at[rows(self.other_base, self.count)])


class GradSum:
    def __init__(self, at, copies, sources, v, out, sems):
        bufs = ((v.bufs_a, v.one_a, v.tail_a), (v.bufs_b, v.one_b, v.tail_b), (v.bufs_c, v.one_c, v.tail_c),
                (v.bufs_d, v.one_d, v.tail_d))
        self.flows = [
            GradFlow(at, copies, sources, v.chip, v.own_half, out, group, *some) for group, some in zip(GROUPS, bufs)
        ]
        self.halves = []
        for flow in self.flows:
            flow.send_core()
            for src, place in flow.pieces(at.c):
                copy = pltpu.make_async_copy(src, v.own_half.at[place], sems.at[len(self.halves)])
                copy.start()
                self.halves.append(copy)

    def slot(self, t):
        if t == 0:
            for copy in self.halves:
                copy.wait()
        for n, flow in enumerate(self.flows):
            stage = t - n // 2
            if 0 <= stage < 8:
                steps = (flow.begin, flow.relay, flow.second, flow.back, flow.whole, flow.relay, flow.share, flow.end)
                steps[stage]()


def flow_scratch():
    shapes = dict(chip=low_shape(HALF_ROWS, WIDTH), own_half=low_shape(HALF_ROWS, WIDTH))
    for name, (_, count, _) in zip("abcd", GROUPS):
        shapes["bufs_" + name] = low_shape(6, count // 8, WIDTH)
        shapes["one_" + name] = low_shape(count // 4, WIDTH)
        shapes["tail_" + name] = low_shape(3, count // 8, 384)
    return shapes


def low_shape(*dims):
    return shape_of(*dims, dtype=bf16)


def shape_of(*dims, dtype=f32):
    return jax.ShapeDtypeStruct(dims, dtype)


def nn(a, b):
    return lax.dot_general(a, b, (((1,), (0,)), ((), ())), preferred_element_type=f32)


def nt(a, b):
    return lax.dot_general(a, b, (((1,), (1,)), ((), ())), preferred_element_type=f32)


def tn(a, b):
    return lax.dot_general(a, b, (((0,), (0,)), ((), ())), preferred_element_type=f32)


def turner():
    c = lax.broadcasted_iota(jnp.int32, (INNER, INNER), 0)
    r = lax.broadcasted_iota(jnp.int32, (INNER, INNER), 1)
    lane = c % HEAD_DIM
    half = ROT // 2
    minus = (lane < half) & (r == c + half)
    plus = (lane >= half) & (lane < ROT) & (r == c - half)
    return jnp.where(plus, 1.0, jnp.where(minus, -1.0, 0.0)).astype(bf16)


def head_lanes(shape, h):
    lane = lax.broadcasted_iota(jnp.int32, shape, len(shape) - 1)
    return (lane >= h * HEAD_DIM) & (lane < (h + 1) * HEAD_DIM)


def pick(value, h):
    return jnp.where(head_lanes(value.shape, h), value, jnp.zeros_like(value))


def chunk_rows(i):
    return pl.ds(pl.multiple_of(i * BLOCK, BLOCK), BLOCK)


def gather_keys(own, other, keys, values):
    for n, ref in enumerate((keys, values)):
        ref[0:BLOCK] = own[n, 0:BLOCK]
        ref[BLOCK : 2 * BLOCK] = other[n, 0:BLOCK]
        ref[2 * BLOCK : 3 * BLOCK] = own[n, BLOCK : 2 * BLOCK]
        ref[3 * BLOCK : 4 * BLOCK] = other[n, BLOCK : 2 * BLOCK]


def key_places(c, shape, dim, blocks):
    i = lax.broadcasted_iota(jnp.int32, shape, dim)
    place = jnp.where(i < BLOCK, i + BLOCK * c, i - BLOCK * c)
    if blocks == 4:
        late = jnp.where(i < 3 * BLOCK, i + BLOCK * c, i - BLOCK * c)
        place = jnp.where(i < 2 * BLOCK, place, late)
    return place


SPANS = ((0, 2), (1, 4))


ROWS = 2 * BLOCK


def norm_back(scaled, normed, inverse):
    inner = scaled - jnp.mean(scaled, axis=-1, keepdims=True)
    inner = inner - normed * jnp.mean(scaled * normed, axis=-1, keepdims=True)
    return inner * inverse


class Env:
    def __init__(self, refs, ins, outs, scratch, raw):
        refs = list(refs)
        sources = {name: refs.pop(0) for name in ins}
        self.raw = types.SimpleNamespace(**{name: refs.pop(0) for name in raw})
        self.targets = {name: refs.pop(0) for name in outs}
        self.v = types.SimpleNamespace(**{name: refs.pop(0) for name in list(ins) + list(outs) + list(scratch)})
        self.send_sems, self.recv_sems, load_sems, self.store_sems, self.local_sems = refs
        self.held = [getattr(self.v, name) for name in ins]
        self.kept = [getattr(self.v, name) for name in outs]
        self.targets = list(self.targets.values())
        self.loads, self.stores = [], []
        for n, name in enumerate(ins):
            source, index = sources[name], ins[name][1]
            source = source if index is None else source.at[index]
            copy = pltpu.make_async_copy(source, self.held[n], load_sems.at[n])
            copy.start()
            self.loads.append(copy)

    def need(self, *refs):
        for n, held in enumerate(self.held):
            if self.loads[n] is not None and any(held is ref for ref in refs):
                self.loads[n].wait()
                self.loads[n] = None

    def done(self, *refs):
        for n, ref in enumerate(self.kept):
            if not any(ref is other for other in refs):
                continue
            copy = pltpu.make_async_copy(ref, self.targets[n], self.store_sems.at[n])
            copy.start()
            self.stores.append(copy)

    def close(self):
        assert not any(self.loads) and len(self.stores) == len(self.kept)
        for copy in self.stores:
            copy.wait()


def fused(body, name, ins, outs, scratch, copies, collective_id, raw={}, local_copies=1):
    def kernel(*refs):
        env = Env(refs, ins, outs, scratch, raw)
        body(env)
        env.close()

    any_space = pl.BlockSpec(memory_space=pl.ANY)
    arrays = [array for array, _ in ins.values()] + list(raw.values())
    held = [pltpu.VMEM(array.shape if index is None else array.shape[1:], array.dtype) for array, index in ins.values()]
    kept = [pltpu.VMEM(s.shape, s.dtype) for s in list(outs.values()) + list(scratch.values())]
    got = pl.pallas_call(
        kernel,
        out_shape=list(outs.values()),
        in_specs=[any_space] * len(arrays),
        out_specs=[any_space] * len(outs),
        scratch_shapes=held
        + kept
        + [
            pltpu.SemaphoreType.DMA((copies,)),
            pltpu.SemaphoreType.DMA((copies,)),
            pltpu.SemaphoreType.DMA((len(ins),)),
            pltpu.SemaphoreType.DMA((len(outs),)),
            pltpu.SemaphoreType.DMA((local_copies,)),
        ],
        compiler_params=pltpu.CompilerParams(
            collective_id=collective_id, has_side_effects=True, vmem_limit_bytes=VMEM_LIMIT
        ),
        name=name,
    )(*arrays)
    return types.SimpleNamespace(**dict(zip(outs, got)))


def block_sum(at, copies, part, bufs, block):
    return RingSum(
        copies, at.x, at.at_x(1), at.at_x(3),
        lambda j, h: part.at[block, rows(64 * j, 64), pl.ds(384 * h, 384)],
        [bufs.at[block, 0], bufs.at[block, 1]], [bufs.at[block, 2], bufs.at[block, 3]],
        [bufs.at[block, 4], bufs.at[block, 5]],
    )


def block_gather(at, copies, out, block):
    return RingGather(
        copies, at.x, at.at_x(1), at.at_x(3),
        lambda j: out.at[block, rows(64 * j, 64)],
        lambda j, h: out.at[block, rows(64 * j, 64), pl.ds(384 * h, 384)],
    )


def sum_out(at, out, block):
    return lambda h: out.at[block, rows(64 * at.x, 64), pl.ds(384 * h, 384)]


def piece_out(out, block):
    return lambda h: out.at[block, :, pl.ds(384 * h, 384)]


def layer_one_body(env):
    at, v = Place(), env.v
    greet([at.sibling(), at.at_x(1), at.at_x(3)])
    copies = Copies(env.send_sems, env.recv_sems, at.sibling())
    forward_steps(
        True, at, copies, v, env.done,
        lambda: env.need(v.wq, v.small, v.x, v.cos, v.sin, v.add, v.before),
        lambda: env.need(v.up),
        lambda: env.need(v.dense, v.down, v.starts),
    )
    backward_steps(True, env, at, copies)
    copies.drain()


def layer_zero_back_body(env):
    at = Place()
    greet(
        [at.sibling()]
        + [at.at_x(k) for k in (1, 2, 3)]
        + [at.at_y(k) for k in (1, 2, 3)]
        + [at.at_z(k) for k in (1, 2, 3)]
    )
    copies = Copies(env.send_sems, env.recv_sems, at.sibling())
    backward_steps(False, env, at, copies)
    copies.drain()


def forward_steps(later, at, copies, v, done, for_front, for_feed, for_mix):
    for_front()
    wq, wt, small = v.wq, v.wt, v.small
    turn = turner()
    for i in range(2):
        wt[INNER * i : INNER * (i + 1)] = nn(turn, wq[INNER * i : INNER * (i + 1)]).astype(bf16)

    def row(i, wide=WIDTH):
        return small[i : i + 1, :wide]

    def front(i, carry):
        here = chunk_rows(i)
        x = v.x[i].astype(f32)
        if later:
            x = x + (v.add[i].astype(f32) + v.before[8:9])
            v.middle[here] = x
        centred = x - jnp.mean(x, axis=-1, keepdims=True)
        inverse = lax.rsqrt(jnp.mean(centred * centred, axis=-1, keepdims=True) + EPS)
        normed = centred * inverse
        v.normed[here] = normed
        v.inverse[here] = jnp.broadcast_to(inverse, (BLOCK, 128))
        first = (normed * row(0) + row(1)).astype(bf16)
        v.first[here] = first
        v.second[here] = (normed * row(2) + row(3)).astype(bf16)
        cosine, sine = v.cos[here], v.sin[here]
        query = (nt(first, wq[:INNER]) + row(4, INNER)) * cosine
        query = query + (nt(first, wt[:INNER]) + row(9, INNER)) * sine
        v.query[here] = (query * HEAD_DIM ** (-0.5)).astype(bf16)
        key = (nt(first, wq[INNER : 2 * INNER]) + row(5, INNER)) * cosine
        key = key + (nt(first, wt[INNER:]) + row(10, INNER)) * sine
        v.own[0, here] = key.astype(bf16)
        v.own[1, here] = (nt(first, wq[2 * INNER :]) + row(6, INNER)).astype(bf16)
        return carry

    lax.fori_loop(0, 2, front, 0)
    swap = copies.send(v.own, v.other, at.sibling())
    done(v.normed, v.inverse, v.first, v.second, v.query, v.own)
    if later:
        done(v.middle)
    for_feed()

    def feed(i, carry):
        here = pl.ds(pl.multiple_of(i * 128, 128), 128)
        hidden = nn(v.second[here], v.up[...]) + row(7)
        below = 0.5 + 0.5 * lax.erf(hidden * (0.5**0.5))
        v.active[here] = (hidden * below).astype(bf16)
        density = jnp.exp(-0.5 * hidden * hidden) * 0.3989422804014327
        v.slope[here] = (below + hidden * density).astype(bf16)
        return carry

    lax.fori_loop(0, 4, feed, 0)
    done(v.active, v.slope)
    copies.landed(swap, v.other)
    done(v.other)
    keys, values, bias, logs = v.keys, v.values, v.bias, v.logs
    gather_keys(v.own, v.other, keys, values)
    logs[...] = jnp.zeros_like(logs)
    for_mix()
    sums = {}
    for block, span in reversed(SPANS):
        here, n = pl.ds(block * BLOCK, BLOCK), span * BLOCK
        place = key_places(at.c, (BLOCK, n), 1, span)
        mine = lax.broadcasted_iota(jnp.int32, (BLOCK, n), 0) + (2 * block + at.c) * BLOCK
        allowed = (place <= mine) & (place >= v.starts[here])
        bias[:, :n] = jnp.where(allowed, 0.0, MASKED)
        query = v.query[here]
        mixed = jnp.zeros((BLOCK, INNER), f32)
        for h in range(HEADS):
            score = nt(pick(query, h), keys[:n]) + bias[:, :n]
            top = jnp.max(score, axis=-1, keepdims=True)
            expo = jnp.exp(score - top)
            total = jnp.sum(expo, axis=-1, keepdims=True)
            logs[here, h : h + 1] = top + jnp.log(total)
            mixed = mixed + pick(nn(expo.astype(bf16), values[:n]) * (1.0 / total), h)
        mixed = mixed.astype(bf16)
        v.mixed[here] = mixed
        v.part[block] = (nn(mixed, v.dense[...]) + nn(v.active[here], v.down[...])).astype(bf16)
        if not later:
            sums[block] = block_sum(at, copies, v.part, v.bufs, block)
            sums[block].start()
    v.log[...] = logs[...].T
    done(v.mixed, v.log)
    if later:
        done(v.part)
    else:
        reduce_and_gather(at, copies, sums, v.total, ())
        done(v.total)


def reduce_and_gather(at, copies, sums, out, between):
    between = list(between)

    def work():
        if between:
            between.pop(0)()

    work()
    sums[1].relay()
    work()
    sums[0].relay()
    work()
    gathers = {}
    for block in (1, 0):
        sums[block].finish(sum_out(at, out, block))
        gathers[block] = block_gather(at, copies, out, block)
        gathers[block].start()
        work()
    for block in (1, 0):
        gathers[block].relay()
        work()
    for block in (1, 0):
        gathers[block].finish()


def backward_steps(later, env, at, copies):
    v = env.v
    extra = []
    flows = None if later else GradSum(at, copies, (env.raw.f_one, env.raw.e_one), v, v.summed_one, env.local_sems)

    def slot(*which):
        for t in which if flows else ():
            flows.slot(t)

    if later:
        env.need(v.part)
        extra = [block_sum(at, copies, v.part, v.part_bufs, block) for block in (1, 0)]
        for ring in extra:
            ring.start()
        env.need(v.g)
        low = v.g
    else:
        env.need(v.g, v.add, v.n_one, v.inv_one)
        low = v.low

        def incoming(i, carry):
            here = chunk_rows(i)
            grad = v.g[i].astype(f32) + norm_back(
                v.add[i].astype(f32), v.n_one[here], v.inv_one[here, 0:1]
            )
            v.grad[here] = grad
            low[i] = grad.astype(bf16)
            return carry

        lax.fori_loop(0, 2, incoming, 0)
    keys, values, bias, inner = v.keys, v.values, v.bias_rows, v.inner
    env.need(v.own, v.other, v.query, v.mixed, v.log, v.dense, v.start_row)
    if not later:
        gather_keys(v.own, v.other, keys, values)
    inner[...] = jnp.zeros_like(inner)
    dkeys, dvalues, log = v.dkeys, v.dvalues, v.log
    for block, span in reversed(SPANS):
        here, n = pl.ds(block * BLOCK, BLOCK), span * BLOCK
        place = key_places(at.c, (n, BLOCK), 0, span)
        mine = lax.broadcasted_iota(jnp.int32, (n, BLOCK), 1) + (2 * block + at.c) * BLOCK
        allowed = (place <= mine) & (place >= v.start_row[0:1, here])
        bias[:n] = jnp.where(allowed, 0.0, MASKED)
        d_mixed = nt(low[block], v.dense[...]).astype(bf16)
        product = d_mixed.astype(f32) * v.mixed[here].astype(f32)
        for h in range(HEADS):
            inner[:, h : h + 1] = jnp.sum(pick(product, h), axis=-1, keepdims=True)
        inner_rows = inner[...].T
        query = v.query[here]
        d_query = jnp.zeros((BLOCK, INNER), f32)
        for h in range(HEADS):
            mine_q, mine_d = pick(query, h), pick(d_mixed, h)
            prob = jnp.exp(nt(keys[:n], mine_q) + bias[:n] - log[h : h + 1, here])
            d_prob = nt(values[:n], mine_d)
            d_score = (prob * (d_prob - inner_rows[h : h + 1])).astype(bf16)
            d_value = nn(prob.astype(bf16), mine_d)
            d_key = nn(d_score, mine_q)
            if span == 4 and h == 0:
                dvalues[...] = d_value
                dkeys[...] = d_key
            else:
                dvalues[:n] += d_value
                dkeys[:n] += d_key
            d_query = d_query + pick(tn(d_score, keys[:n]), h)
        v.d_query[here] = d_query * HEAD_DIM ** (-0.5)
        if block == 1:
            slot(0)
    for n, ref in enumerate((dkeys, dvalues)):
        v.d_other[n, 0:BLOCK] = ref[BLOCK : 2 * BLOCK].astype(bf16)
        v.d_other[n, BLOCK : 2 * BLOCK] = ref[3 * BLOCK : 4 * BLOCK].astype(bf16)
    swap = copies.send(v.d_other, v.got, at.sibling())
    for ring in extra:
        ring.relay()

    small, hid, normed = v.small, v.hid, v.normed
    sums_one, sums_two = v.sums_one, v.sums_two
    sums_one[...] = jnp.zeros_like(sums_one)
    sums_two[...] = jnp.zeros_like(sums_two)
    env.need(v.down, v.up, v.small, v.slope, v.normed)

    def feed(i, carry):
        here = chunk_rows(i)
        g = low[i]
        d_hidden = (nt(g, v.down[...]) * v.slope[here].astype(f32)).astype(bf16)
        hid[here] = d_hidden
        d_second = nt(d_hidden, v.up[...])
        v.e_two[here] = d_second * small[2:3]
        sums_two[0:1] += jnp.sum(d_second * normed[here], axis=0, keepdims=True)
        sums_two[1:2] += jnp.sum(d_second, axis=0, keepdims=True)
        sums_two[2:3] += jnp.sum(g.astype(f32), axis=0, keepdims=True)
        sums_two[3:4] += jnp.sum(d_hidden.astype(f32), axis=0, keepdims=True)
        return carry

    lax.fori_loop(0, 2, feed, 0)
    slot(1)
    if later:
        env.done(v.sums_two)
    for ring, block in zip(extra, (1, 0)):
        ring.finish(piece_out(v.part_sum, block))
    if later:
        env.done(v.part_sum)

    env.need(v.cos, v.sin, v.wq, v.first, v.second, v.active)
    turn = turner()
    wq, packed, got = v.wq, v.packed, v.got

    def unrotate(value, cosine, sine):
        moved = value * sine
        high = moved.astype(bf16)
        lower = (moved - high.astype(f32)).astype(bf16)
        return value * cosine + (nn(high, turn) + nn(lower, turn))

    copies.landed(swap, got)
    sums = {}
    for i in (1, 0):
        here = pl.ds(i * BLOCK, BLOCK)
        there = pl.ds(2 * i * BLOCK, BLOCK)
        cosine, sine = v.cos[here], v.sin[here]
        parts = [
            unrotate(v.d_query[here], cosine, sine),
            unrotate(dkeys[there] + got[0, here].astype(f32), cosine, sine),
            dvalues[there] + got[1, here].astype(f32),
        ]
        d_first = jnp.zeros((BLOCK, WIDTH), f32)
        for n, part in enumerate(parts):
            part = part.astype(bf16)
            packed[n, here] = part
            d_first = d_first + nn(part, wq[INNER * n : INNER * (n + 1)])
            sums_one[2 + n : 3 + n, :INNER] += jnp.sum(part.astype(f32), axis=0, keepdims=True)
        v.e[i] = (d_first * small[0:1] + v.e_two[here]).astype(bf16)
        sums[i] = block_sum(at, copies, v.e, v.bufs, i)
        sums[i].start()
        sums_one[0:1] += jnp.sum(d_first * normed[here], axis=0, keepdims=True)
        sums_one[1:2] += jnp.sum(d_first, axis=0, keepdims=True)
    if later:
        env.done(v.sums_one)

    grads_one, grads_two = v.grads_one, v.grads_two

    def grad_dense():
        grads_two[:INNER] = tn(v.mixed[...], low[...].reshape(ROWS, WIDTH)).astype(bf16)

    def grad_up():
        grads_two[INNER : INNER + WIDTH] = tn(v.second[...], hid[...]).astype(bf16)

    def grad_down():
        grads_two[INNER + WIDTH :] = tn(v.active[...], low[...].reshape(ROWS, WIDTH)).astype(bf16)

    def grad_packed():
        for n in range(3):
            grads_one[INNER * n : INNER * (n + 1)] = tn(packed[n], v.first[...]).astype(bf16)

    if later:
        reduce_and_gather(at, copies, sums, v.total, (grad_dense, grad_packed, grad_up, grad_down))
        env.done(v.total, v.grads_one, v.grads_two)
    else:
        slot(2)
        grad_dense()
        sums[1].relay()
        grad_packed()
        sums[0].relay()
        slot(3)
        grad_up()
        grad_down()
        last_steps(env, at, copies, flows, sums)


def last_steps(env, at, copies, flows_one, sums):
    v, x, y = env.v, at.x, at.y
    send, landed = copies.send, copies.landed
    quarter = rows(64 * x, 64)
    flows_zero = GradSum(at, copies, (v.grads_one, v.grads_two), *copied(v), env.local_sems.at[pl.ds(8, 8)])
    for block in (1, 0):
        sums[block].finish(piece_out(v.total, block))
    env.need(v.part_sum, v.inverse, v.middle, v.params)
    slices, back = v.slices, v.back
    for h in range(2):
        here = rows(256 * h + 64 * x, 64)
        value = v.grad[here] + norm_back(v.total[h], v.normed[here], v.inverse[here, 0:1])
        slices[0, h] = value.astype(bf16)
        slices[1, h] = (v.middle[here] + (v.part_sum[h] + v.params[8:9])).astype(bf16)
    home = []
    for k in (1, 3, 2):
        j = (y + k) % 4
        home.append((k, send(slices.at[j // 2, j % 2], back.at[y, quarter], at.at_y(k))))
    own = pltpu.make_async_copy(slices.at[y // 2, y % 2], back.at[y, quarter], env.local_sems.at[16])
    own.start()
    env.need(v.sf_one, v.se_one)
    first_small, small_out, got = v.first_small, v.small_out, v.small_got
    for layer, refs in enumerate(((v.sums_one, v.sums_two), (v.sf_one, v.se_one))):
        for which, ref in enumerate(refs):
            first_small[layer, pl.ds(8 * which, 8)] = ref[...]
    small_x = [(k, send(first_small, got.at[k - 1], at.at_x(k))) for k in (1, 3, 2)]
    flows_one.slot(4)
    flows_zero.slot(0)
    own.wait()
    for k, index in home:
        landed(index, back.at[(y + 4 - k) % 4, quarter])
    outer = RingGather(
        copies, x, at.at_x(1), at.at_x(3),
        lambda j: back.at[:, rows(64 * j, 64)],
        lambda j, h: back.at[pl.ds(2 * h, 2), rows(64 * j, 64)],
    )
    outer.start()
    flows_one.slot(5)
    flows_zero.slot(1)
    for k, index in small_x:
        landed(index, got.at[k - 1])
    of_norms = lax.broadcasted_iota(jnp.int32, first_small.shape, 1) % 8 < 2
    others = got[0] + got[1] + got[2]
    small_out[...] = first_small[...] + jnp.where(of_norms, others, 0.0)
    small_z = [(k, send(small_out, got.at[2 + k], at.at_z(k))) for k in (1, 3, 2)]
    flows_one.slot(6)
    flows_zero.slot(2)
    outer.relay()
    for k, index in small_z:
        landed(index, got.at[2 + k])
    copies.sent([index for _, index in small_z])
    small_out[...] = small_out[...] + (got[3] + got[4] + got[5])
    small_y = [(k, send(small_out, got.at[5 + k], at.at_y(k))) for k in (1, 3, 2)]
    flows_one.slot(7)
    flows_zero.slot(3)
    flows_one.slot(8)
    env.done(v.summed_one)
    for k, index in small_y:
        landed(index, got.at[5 + k])
    copies.sent([index for _, index in small_y])
    small_out[...] = small_out[...] + (got[6] + got[7] + got[8])
    small_c = send(small_out, got.at[9], at.sibling())
    flows_zero.slot(4)
    landed(small_c, got.at[9])
    copies.sent([small_c])
    small_out[...] = small_out[...] + got[9]
    env.done(v.small_out)
    flows_zero.slot(5)
    outer.finish()
    env.done(v.back)
    for t in (6, 7, 8):
        flows_zero.slot(t)
    env.done(v.summed_zero)


def copied(v):
    names = list(flow_scratch())
    second = types.SimpleNamespace(**{name: getattr(v, name + "_zero") for name in names})
    return second, v.summed_zero


def forward_outs():
    return dict(
        normed=shape_of(ROWS, WIDTH), inverse=shape_of(ROWS, 128), first=low_shape(ROWS, WIDTH),
        second=low_shape(ROWS, WIDTH), query=low_shape(ROWS, INNER), own=low_shape(2, ROWS, INNER),
        other=low_shape(2, ROWS, INNER), active=low_shape(ROWS, WIDTH), slope=low_shape(ROWS, WIDTH),
        mixed=low_shape(ROWS, INNER), log=shape_of(128, ROWS),
    )


def forward_scratch():
    return dict(
        wt=low_shape(2 * INNER, WIDTH), keys=low_shape(SEQ, INNER), values=low_shape(SEQ, INNER),
        logs=shape_of(ROWS, 128), bias=shape_of(BLOCK, SEQ),
    )


def start_layer(boundary, segment_ids, vectors, wq, wd, wu, wn):
    ins = dict(raw_q=(wq, None))
    ins.update({name: (array, None) for name, array in vectors.items()})
    ins.update(segment_ids=(segment_ids, None))
    outs = dict(
        wq=low_shape(2, 3 * INNER, WIDTH), wu=low_shape(2, WIDTH, WIDTH), wd=low_shape(2, INNER, WIDTH),
        wn=low_shape(2, WIDTH, WIDTH), smalls=shape_of(2, 16, WIDTH), xg=low_shape(2, 2, BLOCK, WIDTH),
        cos=shape_of(ROWS, INNER), sin=shape_of(ROWS, INNER), start_col=shape_of(ROWS, 1, dtype=jnp.int32),
        start_row=shape_of(1, ROWS, dtype=jnp.int32), total=low_shape(2, BLOCK, WIDTH), **forward_outs(),
    )
    scratch = dict(
        quarters=shape_of(4, 64, WIDTH), quarters_low=low_shape(4, 64, WIDTH), block=shape_of(BLOCK, WIDTH),
        vectors=shape_of(16, WIDTH), part=low_shape(2, BLOCK, WIDTH), bufs=low_shape(2, 6, 64, 384),
        **forward_scratch(),
    )
    raw = dict(boundary=boundary, up=wu, dense=wd, down=wn)
    return fused(start_body, "start", ins, outs, scratch, 52 + 21, 0, raw, 5)


def backward_results():
    return dict(
        grads_one=low_shape(3 * INNER, WIDTH), grads_two=low_shape(INNER + 2 * WIDTH, WIDTH),
        sums_one=shape_of(8, WIDTH), sums_two=shape_of(8, WIDTH),
    )


def backward_scratch():
    return dict(
        bias_rows=shape_of(SEQ, BLOCK), inner=shape_of(BLOCK, 128), dkeys=shape_of(SEQ, INNER),
        dvalues=shape_of(SEQ, INNER), d_query=shape_of(ROWS, INNER), d_other=low_shape(2, ROWS, INNER),
        got=low_shape(2, ROWS, INNER), hid=low_shape(ROWS, WIDTH), e_two=shape_of(ROWS, WIDTH),
        packed=low_shape(3, ROWS, INNER), e=low_shape(2, BLOCK, WIDTH), bufs=low_shape(2, 6, 64, 384),
    )


def layer_one(xg, add, stacks, tables):
    wq, wd, wu, wn, small = stacks
    cosine, sine, start_col, start_row = tables
    ins = dict(
        wq=(wq, 1), small=(small, 1), x=(xg, 0), add=(add, None), before=(small, 0), cos=(cosine, None),
        sin=(sine, None), up=(wu, 1), dense=(wd, 1), down=(wn, 1), starts=(start_col, None), g=(xg, 1),
        start_row=(start_row, None),
    )
    scratch = forward_outs()
    outs = dict(
        middle=shape_of(ROWS, WIDTH), normed=scratch.pop("normed"), inverse=scratch.pop("inverse"),
        total=low_shape(2, BLOCK, WIDTH), part_sum=shape_of(2, 64, WIDTH), **backward_results(),
    )
    scratch.update(
        part=low_shape(2, BLOCK, WIDTH), part_bufs=low_shape(2, 6, 64, 384), **forward_scratch(), **backward_scratch()
    )
    return fused(layer_one_body, "layer_one", ins, outs, scratch, 34, 5)


def layer_zero_back(xg, one, stacks, tables, kept):
    wq, wd, wu, wn, small = stacks
    cosine, sine, _, start_row = tables
    ins = dict(
        g=(xg, 1), add=(one.total, None), n_one=(one.normed, None), inv_one=(one.inverse, None),
        own=(kept.own, None), other=(kept.other, None), query=(kept.query, None), mixed=(kept.mixed, None),
        log=(kept.log, None), dense=(wd, 0), start_row=(start_row, None), down=(wn, 0), up=(wu, 0), small=(small, 0),
        slope=(kept.slope, None), normed=(kept.normed, None), cos=(cosine, None), sin=(sine, None), wq=(wq, 0),
        first=(kept.first, None), second=(kept.second, None), active=(kept.active, None),
        sf_one=(one.sums_one, None), se_one=(one.sums_two, None), part_sum=(one.part_sum, None),
        inverse=(kept.inverse, None), middle=(one.middle, None), params=(small, 1),
    )
    outs = dict(
        summed_zero=low_shape(GRAD_ROWS, WIDTH), summed_one=low_shape(GRAD_ROWS, WIDTH),
        small_out=shape_of(2, 16, WIDTH), back=low_shape(4, BLOCK, WIDTH),
    )
    scratch = dict(
        keys=low_shape(SEQ, INNER), values=low_shape(SEQ, INNER), low=low_shape(2, BLOCK, WIDTH),
        grad=shape_of(ROWS, WIDTH), total=shape_of(2, 64, WIDTH), slices=low_shape(2, 2, 64, WIDTH),
        first_small=shape_of(2, 16, WIDTH), small_got=shape_of(10, 2, 16, WIDTH),
        **backward_results(), **backward_scratch(), **flow_scratch(),
    )
    scratch.update({name + "_zero": shape for name, shape in flow_scratch().items()})
    raw = dict(f_one=one.grads_one, e_one=one.grads_two)
    return fused(layer_zero_back_body, "layer_zero_back", ins, outs, scratch, 2 * FLOW_COPIES + 40, 7, raw, 17)


def start_body(env):
    at, v, raw = Place(), env.v, env.raw
    p, x, y, z, c = at.p, at.x, at.y, at.z, at.c
    quarter = rows(64 * x, 64)
    local = []

    def bring(source, target):
        copy = pltpu.make_async_copy(source, target, env.local_sems.at[len(local)])
        copy.start()
        local.append(copy)
        return copy

    quarters_in = bring(raw.boundary.at[0, :, quarter], v.quarters)
    up_in = bring(raw.up, v.wu.at[p])
    dense_in = bring(raw.dense, v.wd.at[p])
    down_in = bring(raw.down, v.wn.at[p])
    block_in = bring(raw.boundary.at[0, y], v.block)
    greet(
        [at.at_x(1), at.at_x(3), at.at_y(1), at.at_y(2), at.at_y(3), at.at_z(1), at.at_z(3), at.sibling()]
    )
    copies = Copies(env.send_sems, env.recv_sems, at.at_x(1))

    def piece(ref, zz, cc):
        if ref.shape[-2] == WIDTH:
            return ref.at[rows(192 * zz + 96 * cc, 96)]
        each = ref.shape[-2] // 4
        return ref.at[rows(each * zz, each), pl.ds(pl.multiple_of(384 * cc, 128), 384)]

    def half(ref, zz, cc, h):
        if ref.shape[-2] == WIDTH:
            return ref.at[rows(192 * zz + 96 * cc + 48 * h, 48)]
        each = ref.shape[-2] // 4
        more = (each // 2 + 15) // 16 * 16
        size = each - more if h else more
        return ref.at[rows(each * zz + more * h, size), pl.ds(pl.multiple_of(384 * cc, 128), 384)]

    quarters_in.wait()
    v.quarters_low[...] = v.quarters[...].astype(bf16)
    first = [
        copies.send(v.quarters_low.at[(y + k) % 4], v.xg.at[p, at.low, quarter], at.at_y(k)) for k in (1, 3, 2)
    ]
    env.need(v.raw_q)
    for kind in range(3):
        for h in range(HEADS):
            to, source = INNER * kind + HEAD_DIM * h, INNER * h + HEAD_DIM * kind
            v.wq[p, to : to + HEAD_DIM] = v.raw_q[source : source + HEAD_DIM]
    stacks = [v.wq, v.wu, v.wd, v.wn]
    sent = []
    for stack, copy in zip(stacks, (None, up_in, dense_in, down_in)):
        if copy is not None:
            copy.wait()
        sent.append(copies.send(piece(stack.at[p], z, c), piece(stack.at[p], z, c), at.partner()))
    env.need(v.gain_one, v.shift_one, v.gain_two, v.shift_two, v.qkv_bias, v.dense_bias, v.up_bias, v.down_bias)
    vectors = v.vectors
    vectors[...] = jnp.zeros_like(vectors)
    for n, ref in enumerate((v.gain_one, v.shift_one, v.gain_two, v.shift_two)):
        vectors[n : n + 1] = ref[...]
    turned = ROT // 2
    for kind in range(3):
        for h in range(HEADS):
            source = INNER * h + HEAD_DIM * kind
            part = v.qkv_bias[:, source : source + HEAD_DIM]
            vectors[4 + kind : 5 + kind, pl.ds(HEAD_DIM * h, HEAD_DIM)] = part
            if kind < 2:
                vectors[9 + kind : 10 + kind, pl.ds(HEAD_DIM * h, turned)] = -part[:, turned:ROT]
                vectors[9 + kind : 10 + kind, pl.ds(HEAD_DIM * h + turned, turned)] = part[:, :turned]
    vectors[7:8] = v.up_bias[...]
    vectors[8:9] = v.dense_bias[...] + v.down_bias[...]
    v.smalls[p] = vectors[...]
    sent_small = copies.send(vectors, v.smalls.at[p], at.partner())
    block_in.wait()
    v.xg[p, at.low] = v.block[...].astype(bf16)
    env.need(v.segment_ids)
    labels = v.segment_ids[at.y, pl.ds(at.z, 1)]
    start = jnp.zeros((1, SEQ), f32)
    for label in range(1, 5):
        count = jnp.sum((labels == label - 1).astype(f32), axis=1, keepdims=True)
        start = start + jnp.where(labels >= label, count, 0.0)
    lane = lax.broadcasted_iota(jnp.int32, (1, INNER), 1) % HEAD_DIM
    freqs = jnp.ones((1, INNER), f32)
    for n in range(1, turned):
        freqs = jnp.where(lane % turned == n, 10000.0 ** (-2.0 * n / ROT), freqs)
    angles = []
    for i in range(2):
        pieces = [start[:, BLOCK * (2 * i + k) : BLOCK * (2 * i + k + 1)] for k in range(2)]
        mine = jnp.where(c == 0, pieces[0], pieces[1])
        v.start_row[:, BLOCK * i : BLOCK * (i + 1)] = mine.astype(jnp.int32)
        column = jnp.broadcast_to(mine, (128, BLOCK)).T[:, 0:1]
        v.start_col[BLOCK * i : BLOCK * (i + 1)] = column.astype(jnp.int32)
        spot = lax.broadcasted_iota(jnp.int32, (BLOCK, 1), 0) + (2 * i + c) * BLOCK
        angles.append((spot.astype(f32) - column) * freqs)

    def table(ref, function, rest):
        for i in range(2):
            ref[BLOCK * i : BLOCK * (i + 1)] = jnp.where(lane < ROT, function(angles[i]), rest)

    gathers = []
    for k, index in zip((1, 3, 2), first):
        source = (y + 4 - k) % 4
        slot = v.xg.at[source // 2, source % 2]
        copies.landed(index, slot.at[quarter])
        gather = RingGather(
            copies, x, at.at_x(1), at.at_x(3),
            lambda j, slot=slot: slot.at[rows(64 * j, 64)],
            lambda j, h, slot=slot: slot.at[rows(64 * j + 32 * h, 32)],
        )
        gather.start()
        gathers.append(gather)
    others = [stack.at[1 - p] for stack in stacks]
    rings, shared = [], []

    def share(n, j):
        mine = piece(others[n], j, c)
        shared[n].append((copies.send(mine, mine, at.sibling()), piece(others[n], j, 1 - c)))

    def begin(n):
        other = others[n]
        copies.landed(sent[n], piece(other, z, c))
        ring = RingGather(
            copies, z, at.at_z(1), at.at_z(3),
            lambda j: piece(other, j, c), lambda j, h: half(other, j, c, h),
        )
        ring.start()
        rings.append(ring)
        shared.append([])
        share(n, z)

    def relay(n):
        rings[n].relay()
        share(n, (z + 3) % 4)
        share(n, (z + 1) % 4)

    def finish(n):
        rings[n].finish()
        share(n, (z + 2) % 4)

    def arrived(n):
        for index, view in shared[n]:
            copies.landed(index, view)
        env.done(stacks[n])

    begin(0)
    begin(1)
    table(v.cos, jnp.cos, 1.0)
    begin(2)
    begin(3)
    table(v.sin, jnp.sin, 0.0)
    env.done(v.cos, v.sin, v.start_col, v.start_row)
    for gather in gathers:
        gather.relay()
    relay(0)
    relay(1)

    def for_front():
        finish(0)
        for gather in gathers:
            gather.finish()
        copies.landed(sent_small, v.smalls.at[1 - p])
        relay(2)
        relay(3)
        arrived(0)
        env.done(v.xg, v.smalls)

    def for_feed():
        finish(1)
        finish(2)
        finish(3)
        arrived(1)

    def for_mix():
        arrived(2)
        arrived(3)

    views = types.SimpleNamespace(**vars(v))
    views.wq, views.up, views.dense, views.down = [stack.at[0] for stack in stacks]
    views.small, views.x, views.starts = v.smalls.at[0], v.xg.at[0], v.start_col
    forward_steps(False, at, copies, views, env.done, for_front, for_feed, for_mix)
    copies.drain()


def finish_kernel(
    total, total_one, small, back, x_out, g1, s1, g2, s2, qkv_out, qkv_bias, dense_out, dense_bias, up_out, up_bias,
    down_out, down_bias, total_in, back_in, x_hold, qkv_hold, dense_hold, up_hold, down_hold, load_sems, store_sems,
):
    p = lax.axis_index("pipe")
    loads = [pltpu.make_async_copy(back.at[m], back_in.at[m], load_sems.at[m]) for m in range(4)]
    spans = (pl.ds(1536, 768), pl.ds(480, 672), pl.ds(1152, 384), pl.ds(0, 480))
    for copy in loads:
        copy.start()
    for layer, source in enumerate((total, total_one)):

        @pl.when(p == layer)
        def _(source=source):
            for n, span in enumerate(spans):
                pltpu.make_async_copy(source.at[span], total_in.at[span], load_sems.at[4 + n]).start()

    loads += [
        pltpu.make_async_copy(total.at[span], total_in.at[span], load_sems.at[4 + n]) for n, span in enumerate(spans)
    ]
    stores = []

    def store(source, target):
        copy = pltpu.make_async_copy(source, target, store_sems.at[len(stores)])
        copy.start()
        stores.append(copy)

    for m in range(4):
        loads[m].wait()
        x_hold[m] = back_in[m].astype(f32)
        store(x_hold.at[m], x_out.at[0, m])
    loads[4].wait()
    down_hold[...] = total_in[1536:].astype(f32)
    store(down_hold, down_out.at[0])
    loads[5].wait()
    loads[6].wait()
    up_hold[:672] = total_in[480:1152].astype(f32)
    up_hold[672:] = total_in[1440:1536].astype(f32)
    store(up_hold, up_out.at[0])
    loads[7].wait()
    for h in range(HEADS):
        for kind in range(3):
            to, source = INNER * h + HEAD_DIM * kind, INNER * kind + HEAD_DIM * h
            qkv_bias[:, to : to + HEAD_DIM] = small[p, 2 + kind : 3 + kind, HEAD_DIM * h : HEAD_DIM * (h + 1)]
            for start in (source, source + HEAD_DIM // 2):
                place = start if start < 288 else start - 288 + 1152
                qkv_hold[to + start - source : to + start - source + HEAD_DIM // 2] = total_in[
                    place : place + HEAD_DIM // 2
                ].astype(f32)
    store(qkv_hold, qkv_out.at[0])
    dense_hold[...] = total_in[288:480].astype(f32)
    store(dense_hold, dense_out.at[0])
    for row, ref in ((0, g1), (1, s1), (8, g2), (9, s2), (10, dense_bias), (11, up_bias), (10, down_bias)):
        ref[...] = small[p, row : row + 1]
    for copy in stores:
        copy.wait()


def local(
    boundary,
    segment_ids,
    attn_gain,
    attn_shift,
    mlp_gain,
    mlp_shift,
    qkv_weight,
    qkv_bias,
    dense_weight,
    dense_bias,
    up_weight,
    up_bias,
    down_weight,
    down_bias,
):
    vectors = dict(
        gain_one=attn_gain, shift_one=attn_shift, gain_two=mlp_gain, shift_two=mlp_shift, qkv_bias=qkv_bias,
        dense_bias=dense_bias, up_bias=up_bias, down_bias=down_bias,
    )
    zero = start_layer(
        boundary, segment_ids, vectors, qkv_weight[0].T, dense_weight[0], up_weight[0], down_weight[0]
    )
    xg, stacks = zero.xg, [zero.wq, zero.wd, zero.wu, zero.wn, zero.smalls]
    tables = (zero.cos, zero.sin, zero.start_col, zero.start_row)
    one = layer_one(xg, zero.total, stacks, tables)
    last = layer_zero_back(xg, one, stacks, tables, zero)
    vector = shape_of(1, WIDTH)
    vmem, any_space = pl.BlockSpec(memory_space=pltpu.VMEM), pl.BlockSpec(memory_space=pl.ANY)
    outs = list(
        pl.pallas_call(
            finish_kernel,
            out_shape=[shape_of(1, 4, BLOCK, WIDTH)] + [vector] * 4
            + [shape_of(1, 3 * INNER, WIDTH), shape_of(1, 3 * INNER), shape_of(1, INNER, WIDTH), vector]
            + [shape_of(1, WIDTH, WIDTH), vector] * 2,
            in_specs=[any_space, any_space, vmem, any_space],
            out_specs=[any_space] + [vmem] * 4 + [any_space, vmem] * 4,
            scratch_shapes=[
                pltpu.VMEM((GRAD_ROWS, WIDTH), bf16),
                pltpu.VMEM((4, BLOCK, WIDTH), bf16),
                pltpu.VMEM((4, BLOCK, WIDTH), f32),
                pltpu.VMEM((3 * INNER, WIDTH), f32),
                pltpu.VMEM((INNER, WIDTH), f32),
                pltpu.VMEM((WIDTH, WIDTH), f32),
                pltpu.VMEM((WIDTH, WIDTH), f32),
                pltpu.SemaphoreType.DMA((8,)),
                pltpu.SemaphoreType.DMA((8,)),
            ],
            compiler_params=pltpu.CompilerParams(vmem_limit_bytes=VMEM_LIMIT),
            name="finish",
        )(last.summed_zero, last.summed_one, last.small_out, last.back)
    )
    outs[5] = outs[5].transpose(0, 2, 1)
    return tuple(outs)


def solution(mesh):
    in_specs = (
        P("pipe", None, "dp", None),
        P(),
        P("pipe", None),
        P("pipe", None),
        P("pipe", None),
        P("pipe", None),
        P("pipe", None, "tensor"),
        P("pipe", "tensor"),
        P("pipe", "tensor", None),
        P("pipe", None),
        P("pipe", None, "tensor"),
        P("pipe", "tensor"),
        P("pipe", "tensor", None),
        P("pipe", None),
    )
    out_specs = (
        P("pipe", None, "dp", None),
        P("pipe", None),
        P("pipe", None),
        P("pipe", None),
        P("pipe", None),
        P("pipe", None, "tensor"),
        P("pipe", "tensor"),
        P("pipe", "tensor", None),
        P("pipe", None),
        P("pipe", None, "tensor"),
        P("pipe", "tensor"),
        P("pipe", "tensor", None),
        P("pipe", None),
    )
    return jax.shard_map(local, mesh=mesh, in_specs=in_specs, out_specs=out_specs, check_vma=False)
```
